32 devices in a mesh: section: 2 (over x), batch: 16 (over z, y, core).
Axes of the slice: x: 2, y: 2, z: 4, core: 2. Of those that a mesh axis runs over, the one named last changes fastest.
Arguments:
- patches: bfloat16 [8192, 768], P('batch'), may hold values from -6 to 6
- code_signs: int32 [8192, 18], P('batch'), may hold values from 0 to 1
- tile_ids: int32 [32, 256], P('batch'), may hold values from 0 to 2, never falling along the last dimension, each value on 1 to 128 neighbouring positions
- patch_valid: int32 [32, 256], P('batch'), may hold values 0 or 1
- cotangent: bfloat16 [8192, 768], P('batch'), may hold values from -6 to 6
- attend_weight: bfloat16 [2, 768, 2304], P('section'), may hold values from -0.21875 to 0.21875
- project_weight: bfloat16 [2, 768, 768], P('section'), may hold values from -1.75 to 1.75
- expand_weight: bfloat16 [2, 768, 3072], P('section'), may hold values from -0.21875 to 0.21875
- shrink_weight: bfloat16 [2, 3072, 768], P('section'), may hold values from -0.15625 to 0.15625
- norm_first: float32 [2, 768], P('section'), may hold values from 0.1 to 1.9
- norm_second: float32 [2, 768], P('section'), may hold values from 0.1 to 1.9
- bottleneck: bfloat16 [2, 768, 18], P('section'), may hold values from -6 to 6
Outputs:
- results: bfloat16 [2, 8192, 768], P('section', 'batch')
- grad_attend: float32 [2, 768, 2304], P('section', 'batch')
- grad_project: float32 [2, 768, 768], P('section', 'batch')
- grad_expand: float32 [2, 768, 3072], P('section', 'batch')
- grad_shrink: float32 [2, 3072, 768], P('section', 'batch')
- grad_first: float32 [2, 768], P('section', 'batch')
- grad_second: float32 [2, 768], P('section', 'batch')
- grad_bottleneck: float32 [2, 768, 18], P('section', 'batch')
The draws below stay inside these ranges and needn't reach their ends.
Inputs may be any that keep to these rules, and one draw needn't show every extreme that they name: `tile_ids`: within each image the tile numbers never fall; each tile covers 1 to 128 slots, and one tile of each image covers exactly 128.
All inputs are finite; a program needn't handle non-finite values. No bound on the sum of `patch_valid` on one device may be relied on, other than what follows from the above.
Results may differ from the reference program's by a relative error of at most 0.02.
Values may be sent and summed in bfloat16 or wider, within the bound.
A program may use at most 256 MiB of HBM per device.

```python
import math
import jax
import jax.numpy as jnp
import numpy as np
from jax import lax

D = 768
H = 12
HD = 64
FF = 3072
K = 18
SEQ = 256
IMAGES = 32
TOKENS = 8192


def plant(result, key, least, top_value):
    shape = result.shape
    place = [jax.random.randint(jax.random.fold_in(key, axis), (), 0, shape[axis]) for axis in range(len(shape))]
    result = result.at[tuple(place)].set(least)
    longest = shape.index(max(shape))
    place[longest] = (place[longest] + 1) % shape[longest]
    return result.at[tuple(place)].set(top_value)


def block_levels(own_key, dims, cuts, low, top_value):
    level, own = 1.0, jax.random.fold_in(own_key, 6)
    for position, shards_of in cuts:
        steps = jnp.exp(jax.random.uniform(jax.random.fold_in(own, position), (shards_of,), jnp.float32, low / len(cuts), top_value / len(cuts)))
        level = level * jnp.repeat(steps, dims[position] // shards_of).reshape([-1 if axis == position else 1 for axis in range(len(dims))])
    return level


def length_profile(number_of, total, most, slope):
    portions = [(1 << 20) // math.isqrt(standing ** slope) + 1 for standing in range(2, number_of + 1)]
    rest, holding = total - most - (number_of - 1), [1] * (number_of - 1)
    while rest > 0:
        candidates = [i for i in range(number_of - 1) if holding[i] < most]
        mass, remaining = sum([portions[i] for i in candidates]), rest
        for i in candidates:
            addition = min(most - holding[i], max(1, remaining * portions[i] // mass), rest)
            holding[i] = holding[i] + addition
            rest = rest - addition
    return np.array([most] + holding)


def ragged_sizes(key, amount, total, most, lean):
    if amount == 2:
        one = jax.random.randint(key, (), max(1, total - most), min(most, total - 1) + 1)
        return jnp.stack([one, total - one])
    lengths = jnp.asarray(length_profile(amount, total, most, lean), jnp.int32)
    twos = (amount - 1) // 2
    source_of, taker = lengths[1:1 + 2 * twos:2], lengths[2:2 + 2 * twos:2]
    margin = jnp.minimum(source_of - 1, most - taker)
    shifted = jax.random.randint(jax.random.fold_in(key, 1), (twos,), 0, 1 << 20) % (margin + 1)
    lengths = lengths.at[1:1 + 2 * twos:2].set(source_of - shifted).at[2:2 + 2 * twos:2].set(taker + shifted)
    return lengths[jax.random.permutation(jax.random.fold_in(key, 2), amount)]


def gaussian(own_key, dims, width, limit, split=(), held_as=jnp.bfloat16):
    values = width * jax.random.normal(own_key, dims, jnp.float32)
    if split:
        values = values * block_levels(own_key, dims, split, -0.22, 0.18)
    return jnp.clip(values, -limit, limit).astype(held_as)


def setup_inputs(seed: int = 0) -> dict:
    streams_of = jax.random.split(jax.random.key(seed), 13)
    return {
        "patches": gaussian(streams_of[0], (TOKENS, D), 1.0, 6.0, ((0, 16),)),
        "code_signs": plant(jax.random.randint(streams_of[1], (TOKENS, K), 0, 2), jax.random.fold_in(streams_of[1], 1), 0, 1).astype(jnp.int32),
        "tile_ids": jax.vmap(lambda own: jnp.searchsorted(jnp.cumsum(ragged_sizes(own, 3, SEQ, SEQ // 2, 0)), jnp.arange(SEQ), side="right"))(jax.random.split(streams_of[2], IMAGES)).reshape((IMAGES, SEQ)).astype(jnp.int32),
        "patch_valid": plant((jax.random.randint(streams_of[3], (IMAGES, SEQ), 0, 8) < 7).astype(jnp.int32), jax.random.fold_in(streams_of[3], 1), 0, 1),
        "cotangent": gaussian(streams_of[4], (TOKENS, D), 1.0, 6.0, ((0, 16),)),
        "attend_weight": gaussian(streams_of[5], (2, D, 3 * D), D ** -0.5, 0.21875, ((0, 2),)),
        "project_weight": gaussian(streams_of[6], (2, D, D), (D // 64) ** -0.5, 1.75, ((0, 2),)),
        "expand_weight": gaussian(streams_of[7], (2, D, FF), D ** -0.5, 0.21875, ((0, 2),)),
        "shrink_weight": gaussian(streams_of[8], (2, FF, D), (FF // 2) ** -0.5, 0.15625, ((0, 2),)),
        "norm_first": jnp.clip(1.0 + 0.18 * jax.random.normal(streams_of[9], (2, D), jnp.float32), 0.1, 1.9),
        "norm_second": jnp.clip(1.0 + 0.18 * jax.random.normal(streams_of[10], (2, D), jnp.float32), 0.1, 1.9),
        "bottleneck": gaussian(streams_of[11], (2, D, K), 1.0, 6.0, ((0, 2),)),
    }


HIGHEST = lax.Precision.HIGHEST

@jax.custom_vjp
def low(v):
    return lax.optimization_barrier(v.astype(jnp.bfloat16)).astype(jnp.float32)

@jax.custom_vjp
def low_back(v):
    return v

def low_keep(v):
    return (low(v), None)

def low_pass(kept, grad):
    return (grad,)

def back_keep(v):
    return (v, None)

def back_low(kept, grad):
    return (low(grad),)
low.defvjp(low_keep, low_pass)
low_back.defvjp(back_keep, back_low)

def layer_norm(values, gain):
    average = lax.optimization_barrier(jnp.mean(values, axis=-1, keepdims=True))
    center = values - average
    spread = lax.optimization_barrier(jnp.mean(center * center, axis=-1, keepdims=True))
    return center * lax.rsqrt(spread + 1e-06) * gain

def allowed(tile_row, keep_row):
    places = jnp.arange(tile_row.shape[0])
    same_tile = tile_row[:, None] == tile_row[None, :]
    live_keys = keep_row[None, :] == 1
    return same_tile & live_keys | (places[:, None] == places[None, :])

def block(residual, weights, allowed_keys):
    attend, project, expand, shrink, first, second = weights
    length = residual.shape[0]
    normed_one = low(layer_norm(residual, first))
    joint_proj = low_back(low(jnp.dot(normed_one, attend, precision=HIGHEST)))
    split_parts = joint_proj.reshape(length, 3, H, HD)
    queries = split_parts[:, 0]
    key_rows = split_parts[:, 1]
    value_rows = split_parts[:, 2]
    scores = low_back(jnp.einsum('qhd,khd->hqk', queries, key_rows, precision=HIGHEST) * HD ** (-0.5))
    scores = jnp.where(allowed_keys[None], scores, -1000000000.0)
    softmax_out = jax.nn.softmax(scores, axis=-1)
    mixed_heads = jnp.einsum('hqk,khd->qhd', low(softmax_out), value_rows, precision=HIGHEST).reshape(length, H * HD)
    mixed_heads = low_back(low(mixed_heads))
    middle = residual + low_back(jnp.dot(mixed_heads, project, precision=HIGHEST))
    normed_two = low(layer_norm(middle, second))
    hidden = low_back(jnp.dot(normed_two, expand, precision=HIGHEST))
    active = low(jax.nn.gelu(hidden, approximate=False))
    return middle + low_back(jnp.dot(active, shrink, precision=HIGHEST))

def forward(params, images, code_base, tile_ids, patch_valid, fixed_units):
    attend, project, expand, shrink, first, second, bottle = params
    encoder = tuple((member[0] for member in (attend, project, expand, shrink, first, second)))
    decoder = tuple((member[1] for member in (attend, project, expand, shrink, first, second)))

    def one_image(image_rows, base_rows, tile_row, keep_row, fixed_row):
        allowed_keys = allowed(tile_row, keep_row)
        encoded = block(image_rows, encoder, allowed_keys)
        latent = low_back(jnp.dot(low(encoded), bottle[0], precision=HIGHEST))
        unit_code = latent * lax.rsqrt(lax.optimization_barrier(jnp.sum(latent * latent, axis=-1, keepdims=True)) + 1e-06)
        code_value = low_back(low(base_rows + unit_code - fixed_row))
        decoder_in = low_back(jnp.dot(code_value, bottle[1].T, precision=HIGHEST))
        return (block(decoder_in, decoder, allowed_keys), unit_code)
    checked = jax.checkpoint(one_image)

    def scan_step(carried, members):
        return (carried, checked(*members))
    _, (decoded, units) = lax.scan(scan_step, jnp.zeros((), jnp.float32), (images, code_base, tile_ids, patch_valid, fixed_units))
    return (decoded, units)

def reference(patches, code_signs, tile_ids, patch_valid, cotangent, attend_weight, project_weight, expand_weight, shrink_weight, norm_first, norm_second, bottleneck):
    params = tuple((member.astype(jnp.float32) for member in (attend_weight, project_weight, expand_weight, shrink_weight, norm_first, norm_second, bottleneck)))
    images = patches.astype(jnp.float32).reshape(IMAGES, SEQ, D)
    code_base = ((2 * code_signs - 1).astype(jnp.float32) / math.sqrt(K)).reshape(IMAGES, SEQ, K)
    zero_units = jnp.zeros((IMAGES, SEQ, K), jnp.float32)
    _, fixed_units = forward(params, images, code_base, tile_ids, patch_valid, zero_units)

    def evaluate(param_set, image_set):
        return forward(param_set, image_set, code_base, tile_ids, patch_valid, fixed_units)
    decoded, pullback, _ = jax.vjp(evaluate, params, images, has_aux=True)
    param_grads, image_grad = pullback(cotangent.astype(jnp.float32).reshape(IMAGES, SEQ, D))
    results = jnp.stack([image_grad.reshape(TOKENS, D).astype(jnp.bfloat16), decoded.reshape(TOKENS, D).astype(jnp.bfloat16)])
    return (results, param_grads[0], param_grads[1], param_grads[2], param_grads[3], param_grads[4], param_grads[5], param_grads[6])
```

```python
import functools
import math

import jax
import jax.numpy as jnp
from jax import lax
from jax.experimental import pallas as pl
from jax.experimental.pallas import tpu as pltpu
from jax.sharding import PartitionSpec as P

H = 12
HD = 64
MESH = pl.DeviceIdType.MESH
ROWS = 48


def passed_along(block, axis, distance):
    devices = range(lax.axis_size(axis))
    route = [(i - distance, i) for i in devices if i - distance in devices]
    return lax.ppermute(block, axis, route)


def contract_rows(former, latter):
    return lax.dot_general(
        former, latter, (((0,), (0,)), ((), ())), preferred_element_type=jnp.float32
    )


def times_transpose(former, latter):
    return lax.dot_general(
        former, latter, (((1,), (1,)), ((), ())), preferred_element_type=jnp.float32
    )


def normalize(values):
    average = jnp.mean(values, axis=-1, keepdims=True)
    center = values - average
    spread = jnp.mean(center * center, axis=-1, keepdims=True)
    factor = lax.rsqrt(spread + 1e-06)
    return (center * factor, factor)


def norm_back(grad_normed, normed, factor):
    return factor * (
        grad_normed
        - jnp.mean(grad_normed, axis=-1, keepdims=True)
        - normed * jnp.mean(grad_normed * normed, axis=-1, keepdims=True)
    )


def allowed(tile_row, keep_row):
    places = jnp.arange(tile_row.shape[0])
    same_tile = tile_row[:, None] == tile_row[None, :]
    live_keys = keep_row[None, :] == 1
    return same_tile & live_keys | (places[:, None] == places[None, :])


def block_forward(residual, weights, allowed_keys):
    attend, project, expand, shrink, first, second = weights
    length, model_width = residual.shape
    normed_one, factor_one = normalize(residual)
    input_one = (normed_one * first).astype(jnp.bfloat16)
    joint_proj = jnp.dot(input_one, attend, preferred_element_type=jnp.float32).astype(jnp.bfloat16)
    split_parts = joint_proj.reshape(length, 3, H, HD)
    queries = split_parts[:, 0]
    key_rows = split_parts[:, 1]
    value_rows = split_parts[:, 2]
    scores = jnp.einsum(
        "qhd,khd->hqk", queries, key_rows, preferred_element_type=jnp.float32
    ) * HD ** (-0.5)
    scores = jnp.where(allowed_keys[None], scores, -1000000000.0)
    maximum = jnp.max(scores, axis=-1, keepdims=True)
    raised = jnp.exp(scores - maximum)
    softmax_out = raised / jnp.sum(raised, axis=-1, keepdims=True)
    softmax_low = softmax_out.astype(jnp.bfloat16)
    mixed_heads = jnp.einsum(
        "hqk,khd->qhd", softmax_low, value_rows, preferred_element_type=jnp.float32
    )
    mixed_heads = mixed_heads.reshape(length, model_width).astype(jnp.bfloat16)
    middle = residual + jnp.dot(mixed_heads, project, preferred_element_type=jnp.float32)
    normed_two, factor_two = normalize(middle)
    input_two = (normed_two * second).astype(jnp.bfloat16)
    hidden = jnp.dot(input_two, expand, preferred_element_type=jnp.float32)
    active = jax.nn.gelu(hidden, approximate=False).astype(jnp.bfloat16)
    output = middle + jnp.dot(active, shrink, preferred_element_type=jnp.float32)
    kept_parts = (
        normed_one,
        factor_one,
        input_one,
        queries,
        key_rows,
        value_rows,
        softmax_out,
        softmax_low,
        mixed_heads,
        normed_two,
        factor_two,
        input_two,
        hidden,
        active,
    )
    return (output, kept_parts)


def block_backward(kept_parts, grad_out, weights):
    attend, project, expand, shrink, first, second = weights
    (
        normed_one,
        factor_one,
        input_one,
        queries,
        key_rows,
        value_rows,
        softmax_out,
        softmax_low,
        mixed_heads,
        normed_two,
        factor_two,
        input_two,
        hidden,
        active,
    ) = kept_parts
    length, model_width = grad_out.shape
    grad_rounded = grad_out.astype(jnp.bfloat16)
    grad_shrink = contract_rows(active, grad_rounded)
    grad_active = times_transpose(grad_rounded, shrink)
    _, gelu_back = jax.vjp(lambda values: jax.nn.gelu(values, approximate=False), hidden)
    grad_hidden = gelu_back(grad_active)[0].astype(jnp.bfloat16)
    grad_expand = contract_rows(input_two, grad_hidden)
    grad_input_two = times_transpose(grad_hidden, expand)
    grad_second = jnp.sum(grad_input_two * normed_two, axis=0)
    grad_middle = grad_out + norm_back(grad_input_two * second, normed_two, factor_two)
    middle_low = grad_middle.astype(jnp.bfloat16)
    grad_project = contract_rows(mixed_heads, middle_low)
    grad_mixed = times_transpose(middle_low, project).astype(jnp.bfloat16).reshape(length, H, HD)
    grad_soft = jnp.einsum(
        "qhd,khd->hqk", grad_mixed, value_rows, preferred_element_type=jnp.float32
    )
    grad_values = jnp.einsum(
        "hqk,qhd->khd", softmax_low, grad_mixed, preferred_element_type=jnp.float32
    )
    inner_sum = jnp.sum(softmax_out * grad_soft, axis=-1, keepdims=True)
    grad_scores = (softmax_out * (grad_soft - inner_sum)).astype(jnp.bfloat16)
    score_scale = HD ** (-0.5)
    grad_queries = (
        jnp.einsum("hqk,khd->qhd", grad_scores, key_rows, preferred_element_type=jnp.float32)
        * score_scale
    )
    grad_keys = (
        jnp.einsum("hqk,qhd->khd", grad_scores, queries, preferred_element_type=jnp.float32)
        * score_scale
    )
    grad_joint = (
        jnp.stack([grad_queries, grad_keys, grad_values], axis=1)
        .reshape(length, 3 * model_width)
        .astype(jnp.bfloat16)
    )
    grad_attend = contract_rows(input_one, grad_joint)
    grad_input_one = times_transpose(grad_joint, attend)
    grad_first = jnp.sum(grad_input_one * normed_one, axis=0)
    grad_residual = grad_middle + norm_back(grad_input_one * first, normed_one, factor_one)
    return (
        grad_residual,
        (grad_attend, grad_project, grad_expand, grad_shrink, grad_first, grad_second),
    )


class Reduction:
    def __init__(self, depth, parts, from_core, from_y, from_low, from_high, total, sems):
        self.depth = depth
        self.parts, self.total = parts, total
        self.from_core, self.from_y = from_core, from_y
        self.from_low, self.from_high = from_low, from_high
        self.core_s, self.core_r, self.y_s, self.y_r, self.up_s, self.up_r, self.down_s, self.down_r = sems
        self.section = lax.axis_index("section")
        self.me = lax.axis_index("batch")
        self.z, self.y, self.core = self.me // 4, (self.me // 2) % 2, self.me % 2

    def device(self, z, y, core):
        return (self.section, z * 4 + y * 2 + core)

    def peers(self):
        return (
            self.device(self.z, self.y, 1 - self.core),
            self.device(self.z, 1 - self.y, self.core),
            self.device(jnp.minimum(self.z + 1, self.depth - 1), self.y, self.core),
            self.device(jnp.maximum(self.z - 1, 0), self.y, self.core),
        )

    def greet(self):
        barrier = pltpu.get_barrier_semaphore()
        core, other, high, low = self.peers()

        def signal(device):
            pl.semaphore_signal(barrier, inc=1, device_id=device, device_id_type=MESH)

        signal(core)
        signal(other)

        @pl.when(self.z < self.depth - 1)
        def _():
            signal(high)

        @pl.when(self.z > 0)
        def _():
            signal(low)

        ends = (self.z == 0) | (self.z == self.depth - 1)

        @pl.when(ends)
        def _():
            pl.semaphore_wait(barrier, 3)

        @pl.when(jnp.logical_not(ends))
        def _():
            pl.semaphore_wait(barrier, 4)

    def core_copy(self, k):
        return pltpu.make_async_remote_copy(
            self.parts.at[k, 1 - self.core], self.from_core.at[k], self.core_s.at[k], self.core_r.at[k],
            device_id=self.peers()[0], device_id_type=MESH,
        )

    def y_copy(self, k):
        return pltpu.make_async_remote_copy(
            self.parts.at[k, self.core, 1 - self.y], self.from_y.at[k], self.y_s.at[k], self.y_r.at[k],
            device_id=self.peers()[1], device_id_type=MESH,
        )

    def up_copy(self, k, to):
        return pltpu.make_async_remote_copy(
            self.parts.at[k, self.core, self.y, to], self.from_low.at[k, to], self.up_s.at[k, to], self.up_r.at[k, to],
            device_id=self.peers()[2], device_id_type=MESH,
        )

    def down_copy(self, k, to):
        return pltpu.make_async_remote_copy(
            self.parts.at[k, self.core, self.y, to], self.from_high.at[k, to], self.down_s.at[k, to], self.down_r.at[k, to],
            device_id=self.peers()[3], device_id_type=MESH,
        )

    def start(self, k):
        self.core_copy(k).start()

    def after_core(self, k):
        self.core_copy(k).wait_recv()
        for far in (1, 0):
            half = (self.y + far) % 2

            @pl.loop(0, self.depth)
            def _(to):
                here = self.parts.at[k, self.core, half, to]
                here[...] = (here[...].astype(jnp.float32) + self.from_core[k, half, to].astype(jnp.float32)).astype(jnp.bfloat16)

            if far:
                self.y_copy(k).start()

    def after_y(self, k):
        self.y_copy(k).wait_recv()

        @pl.loop(0, self.depth)
        def _(to):
            here = self.parts.at[k, self.core, self.y, to]
            here[...] = (here[...].astype(jnp.float32) + self.from_y[k, to].astype(jnp.float32)).astype(jnp.bfloat16)

    def go_up(self, k):
        for to in range(self.depth - 1, 0, -1):

            @pl.when(self.z < to)
            def _():
                copy = self.up_copy(k, to)

                @pl.when(self.z > 0)
                def _():
                    copy.wait_recv()
                    here = self.parts.at[k, self.core, self.y, to]
                    here[...] = (here[...].astype(jnp.float32) + self.from_low[k, to].astype(jnp.float32)).astype(jnp.bfloat16)

                copy.start()

    def go_down(self, k):
        for to in range(self.depth - 1):

            @pl.when(self.z > to)
            def _():
                copy = self.down_copy(k, to)

                @pl.when(self.z < self.depth - 1)
                def _():
                    copy.wait_recv()
                    here = self.parts.at[k, self.core, self.y, to]
                    here[...] = (here[...].astype(jnp.float32) + self.from_high[k, to].astype(jnp.float32)).astype(jnp.bfloat16)

                copy.start()

    def finish(self, k):
        here = self.parts.at[k, self.core, self.y, self.z]

        @pl.when(self.z == 0)
        def _():
            self.down_copy(k, self.z).wait_recv()
            self.total[k] = here[...].astype(jnp.float32) + self.from_high[k, self.z].astype(jnp.float32)

        @pl.when(self.z == self.depth - 1)
        def _():
            self.up_copy(k, self.z).wait_recv()
            self.total[k] = here[...].astype(jnp.float32) + self.from_low[k, self.z].astype(jnp.float32)

        @pl.when((self.z > 0) & (self.z < self.depth - 1))
        def _():
            self.down_copy(k, self.z).wait_recv()
            self.up_copy(k, self.z).wait_recv()
            self.total[k] = (
                here[...].astype(jnp.float32)
                + self.from_high[k, self.z].astype(jnp.float32)
                + self.from_low[k, self.z].astype(jnp.float32)
            )

    def drain(self, k):
        self.core_copy(k).wait_send()
        self.y_copy(k).wait_send()
        for to in range(self.depth):

            @pl.when(self.z < to)
            def _():
                self.up_copy(k, to).wait_send()

            @pl.when(self.z > to)
            def _():
                self.down_copy(k, to).wait_send()

    def step(self, t, count):
        last = self.depth - 1

        def at(offset, action):
            k = t - offset

            @pl.when((k >= 0) & (k < count))
            def _():
                action(k)

        at(1, self.after_core)
        at(2, self.after_y)
        at(2 + self.z, self.go_up)
        at(2 + last - self.z, self.go_down)
        at(3 + last, self.finish)

    def scratch(depth, count, wide):
        return [
            pltpu.VMEM((count, 2, depth, ROWS, wide), jnp.bfloat16),
            pltpu.VMEM((count, depth, ROWS, wide), jnp.bfloat16),
            pltpu.VMEM((count, depth, ROWS, wide), jnp.bfloat16),
            pltpu.VMEM((count, depth, ROWS, wide), jnp.bfloat16),
        ] + [pltpu.SemaphoreType.DMA((count,))] * 4 + [pltpu.SemaphoreType.DMA((count, depth))] * 4


def sum_kernel(depth, parts_in, extra_in, total, extra_total, parts, extra, loads, *scratch):
    count = parts.shape[0]
    main = Reduction(depth, parts, *scratch[:4], total, scratch[4:12])
    small = Reduction(depth, extra, *scratch[12:16], extra_total, scratch[16:24])

    def load(k):
        return pltpu.make_async_copy(parts_in.at[k], parts.at[k], loads.at[k])

    @pl.loop(0, count)
    def _(k):
        load(k).start()

    extra[...] = extra_in[...]
    main.greet()
    small.start(0)

    @pl.loop(0, count)
    def _(k):
        load(k).wait()
        main.start(k)

    @pl.loop(0, depth + 4)
    def _(t):
        small.step(t, 1)

    @pl.loop(0, count + depth + 3)
    def _(t):
        main.step(t, count)

    small.drain(0)

    @pl.loop(0, count)
    def _(k):
        main.drain(k)


def sum_over_batch(parts, extra):
    count, _, _, depth, _, wide = parts.shape
    narrow = extra.shape[-1]
    return pl.pallas_call(
        functools.partial(sum_kernel, depth),
        out_shape=(
            jax.ShapeDtypeStruct((count, ROWS, wide), jnp.float32),
            jax.ShapeDtypeStruct((1, ROWS, narrow), jnp.float32),
        ),
        in_specs=[pl.BlockSpec(memory_space=pl.ANY), pl.BlockSpec(memory_space=pltpu.VMEM)],
        out_specs=[pl.BlockSpec(memory_space=pltpu.VMEM)] * 2,
        scratch_shapes=[
            pltpu.VMEM(parts.shape, jnp.bfloat16),
            pltpu.VMEM(extra.shape, jnp.bfloat16),
            pltpu.SemaphoreType.DMA((count,)),
        ]
        + Reduction.scratch(depth, count, wide)
        + Reduction.scratch(depth, 1, narrow),
        compiler_params=pltpu.CompilerParams(collective_id=0, has_side_effects=True, vmem_limit_bytes=60 << 20),
        name="sum_over_batch",
    )(parts, extra)


def to_pieces(grad, batch, wide):
    rows, columns = grad.shape
    grad = grad.astype(jnp.bfloat16).reshape(batch // 4, 2, 2, rows // batch // ROWS, ROWS, columns // wide, wide)
    return grad.transpose(3, 5, 2, 1, 0, 4, 6).reshape(-1, 2, 2, batch // 4, ROWS, wide)


def sum_scatter(totals):
    batch = lax.axis_size("batch")
    attend, project, expand, shrink, first, second, bottle = totals
    width, code = bottle.shape
    if batch % 4 or width // batch != ROWS:
        return lax.psum_scatter(totals, "batch", scatter_dimension=0, tiled=True)
    parts = jnp.concatenate([to_pieces(member, batch, width) for member in (shrink, expand, project, attend)])
    extra = jnp.concatenate(
        [bottle, first[:, None], second[:, None], jnp.zeros((width, 128 - code - 2), jnp.float32)], axis=1
    )
    total, rest = sum_over_batch(parts, to_pieces(extra, batch, 128))
    deep, broad = shrink.shape[0] // width, expand.shape[1] // width
    beside = lambda low, high: total[low:high].transpose(1, 0, 2).reshape(ROWS, -1)
    return (
        beside(deep + broad + 1, total.shape[0]),
        total[deep + broad],
        beside(deep, deep + broad),
        total[:deep].reshape(-1, width),
        rest[0, :, code],
        rest[0, :, code + 1],
        rest[0, :, :code],
    )


def pick_index(stacked, chosen):
    return lax.dynamic_index_in_dim(stacked, chosen, 0, keepdims=False)


def body(
    patches,
    code_signs,
    tile_ids,
    patch_valid,
    cotangent,
    attend_weight,
    project_weight,
    expand_weight,
    shrink_weight,
    norm_first,
    norm_second,
    bottleneck,
):
    micro_count = tile_ids.shape[0]
    length = tile_ids.shape[1]
    code_width = code_signs.shape[1]
    encoding = lax.axis_index("section") == 0
    encoding_int = encoding.astype(jnp.int32)
    weights = (
        attend_weight[0],
        project_weight[0],
        expand_weight[0],
        shrink_weight[0],
        norm_first[0],
        norm_second[0],
    )
    bottle = bottleneck[0]
    code_values = ((2 * code_signs - 1).astype(jnp.float32) / math.sqrt(code_width)).astype(
        jnp.bfloat16
    )
    block_inputs = []
    outputs_low = []
    unit_codes = []
    unit_factors = []
    decoded_list = []
    kept_list = []
    for turn_index in range(micro_count):
        image_rows = patches[turn_index * length : (turn_index + 1) * length].astype(jnp.float32)
        decoder_in = times_transpose(
            code_values[turn_index * length : (turn_index + 1) * length], bottle
        )
        block_in = jnp.where(encoding, image_rows, decoder_in)
        allowed_keys = allowed(tile_ids[turn_index], patch_valid[turn_index])
        output, kept_parts = block_forward(block_in, weights, allowed_keys)
        output_low = output.astype(jnp.bfloat16)
        latent = jnp.dot(output_low, bottle, preferred_element_type=jnp.float32)
        factor = lax.rsqrt(jnp.sum(latent * latent, axis=-1, keepdims=True) + 1e-06)
        block_inputs.append(block_in)
        outputs_low.append(output_low)
        unit_codes.append(latent * factor)
        unit_factors.append(factor)
        decoded_list.append(output_low)
        kept_list.append(kept_parts)
    block_inputs = jnp.stack(block_inputs)
    outputs_low = jnp.stack(outputs_low)
    unit_codes = jnp.stack(unit_codes)
    unit_factors = jnp.stack(unit_factors)
    kept_stack = jax.tree.map(lambda *members: jnp.stack(members), *kept_list)
    totals = None
    sent_grad = jnp.zeros((length, code_width), jnp.bfloat16)
    input_grads = []
    for turn_index in range(micro_count + 1):
        if turn_index > 0:
            received = passed_along(sent_grad, "section", -1)
        else:
            received = jnp.zeros_like(sent_grad)
        chosen = jnp.clip(turn_index - encoding_int, 0, micro_count - 1)
        turn_flag = jnp.where(encoding, turn_index >= 1, turn_index < micro_count).astype(
            jnp.float32
        )
        kept_parts = jax.tree.map(lambda stacked: pick_index(stacked, chosen), kept_stack)
        unit_code = pick_index(unit_codes, chosen)
        factor = pick_index(unit_factors, chosen)
        output_low = pick_index(outputs_low, chosen)
        grad_unit = received.astype(jnp.float32)
        grad_latent = (
            factor
            * (grad_unit - unit_code * jnp.sum(unit_code * grad_unit, axis=-1, keepdims=True))
        ).astype(jnp.bfloat16)
        grad_encoded = times_transpose(grad_latent, bottle)
        bottle_encoder = contract_rows(output_low, grad_latent)
        given_grad = lax.dynamic_slice_in_dim(cotangent, chosen * length, length, 0).astype(
            jnp.float32
        )
        grad_out = jnp.where(encoding, grad_encoded, given_grad)
        grad_in, grads = block_backward(kept_parts, grad_out, weights)
        grad_in_low = grad_in.astype(jnp.bfloat16)
        code_rows = lax.dynamic_slice_in_dim(code_values, chosen * length, length, 0)
        bottle_decoder = contract_rows(grad_in_low, code_rows)
        sent_grad = jnp.dot(grad_in_low, bottle, preferred_element_type=jnp.float32).astype(
            jnp.bfloat16
        )
        grads = grads + (jnp.where(encoding, bottle_encoder, bottle_decoder),)
        grads = tuple((turn_flag * member for member in grads))
        if turn_index > 0:
            input_grads.append(grad_in_low)
        totals = (
            grads
            if totals is None
            else tuple((former + latter for former, latter in zip(totals, grads)))
        )
    totals = sum_scatter(totals)
    pieces = [
        jnp.where(encoding, input_grads[turn_index], decoded_list[turn_index])
        for turn_index in range(micro_count)
    ]
    results = jnp.concatenate(pieces, axis=0)[None]
    return (
        results,
        totals[0][None],
        totals[1][None],
        totals[2][None],
        totals[3][None],
        totals[4][None],
        totals[5][None],
        totals[6][None],
    )


def solution(mesh):
    return jax.shard_map(
        body,
        mesh=mesh,
        in_specs=(
            P("batch", None),
            P("batch", None),
            P("batch", None),
            P("batch", None),
            P("batch", None),
            P("section", None, None),
            P("section", None, None),
            P("section", None, None),
            P("section", None, None),
            P("section", None),
            P("section", None),
            P("section", None, None),
        ),
        out_specs=(
            P("section", "batch", None),
            P("section", "batch", None),
            P("section", "batch", None),
            P("section", "batch", None),
            P("section", "batch", None),
            P("section", "batch"),
            P("section", "batch"),
            P("section", "batch", None),
        ),
        check_vma=False,
    )
```

```python
import functools
import math

import jax
import jax.numpy as jnp
from jax import lax
from jax.experimental import pallas as pl
from jax.experimental.pallas import tpu as pltpu
from jax.sharding import PartitionSpec as P

H = 12
HD = 64
MESH = pl.DeviceIdType.MESH
ROWS = 48


def passed_along(block, axis, distance):
    devices = range(lax.axis_size(axis))
    route = [(i - distance, i) for i in devices if i - distance in devices]
    return lax.ppermute(block, axis, route)


def contract_rows(former, latter):
    return lax.dot_general(
        former, latter, (((0,), (0,)), ((), ())), preferred_element_type=jnp.float32
    )


def times_transpose(former, latter):
    return lax.dot_general(
        former, latter, (((1,), (1,)), ((), ())), preferred_element_type=jnp.float32
    )


def normalize(values):
    average = jnp.mean(values, axis=-1, keepdims=True)
    center = values - average
    spread = jnp.mean(center * center, axis=-1, keepdims=True)
    factor = lax.rsqrt(spread + 1e-06)
    return (center * factor, factor)


def norm_back(grad_normed, normed, factor):
    return factor * (
        grad_normed
        - jnp.mean(grad_normed, axis=-1, keepdims=True)
        - normed * jnp.mean(grad_normed * normed, axis=-1, keepdims=True)
    )


def allowed(tile_row, keep_row):
    places = jnp.arange(tile_row.shape[0])
    same_tile = tile_row[:, None] == tile_row[None, :]
    live_keys = keep_row[None, :] == 1
    return same_tile & live_keys | (places[:, None] == places[None, :])


def block_forward(residual, weights, allowed_keys):
    attend, project, expand, shrink, first, second = weights
    length, model_width = residual.shape
    normed_one, factor_one = normalize(residual)
    input_one = (normed_one * first).astype(jnp.bfloat16)
    joint_proj = jnp.dot(input_one, attend, preferred_element_type=jnp.float32).astype(jnp.bfloat16)
    split_parts = joint_proj.reshape(length, 3, H, HD)
    queries = split_parts[:, 0]
    key_rows = split_parts[:, 1]
    value_rows = split_parts[:, 2]
    scores = jnp.einsum(
        "qhd,khd->hqk", queries, key_rows, preferred_element_type=jnp.float32
    ) * HD ** (-0.5)
    scores = jnp.where(allowed_keys[None], scores, -1000000000.0)
    maximum = jnp.max(scores, axis=-1, keepdims=True)
    raised = jnp.exp(scores - maximum)
    softmax_out = raised / jnp.sum(raised, axis=-1, keepdims=True)
    softmax_low = softmax_out.astype(jnp.bfloat16)
    mixed_heads = jnp.einsum(
        "hqk,khd->qhd", softmax_low, value_rows, preferred_element_type=jnp.float32
    )
    mixed_heads = mixed_heads.reshape(length, model_width).astype(jnp.bfloat16)
    middle = residual + jnp.dot(mixed_heads, project, preferred_element_type=jnp.float32)
    normed_two, factor_two = normalize(middle)
    input_two = (normed_two * second).astype(jnp.bfloat16)
    hidden = jnp.dot(input_two, expand, preferred_element_type=jnp.float32)
    active = jax.nn.gelu(hidden, approximate=False).astype(jnp.bfloat16)
    output = middle + jnp.dot(active, shrink, preferred_element_type=jnp.float32)
    kept_parts = (
        normed_one,
        factor_one,
        input_one,
        queries,
        key_rows,
        value_rows,
        softmax_out,
        softmax_low,
        mixed_heads,
        normed_two,
        factor_two,
        input_two,
        hidden,
        active,
    )
    return (output, kept_parts)


def block_backward(kept_parts, grad_out, weights):
    attend, project, expand, shrink, first, second = weights
    (
        normed_one,
        factor_one,
        input_one,
        queries,
        key_rows,
        value_rows,
        softmax_out,
        softmax_low,
        mixed_heads,
        normed_two,
        factor_two,
        input_two,
        hidden,
        active,
    ) = kept_parts
    length, model_width = grad_out.shape
    grad_rounded = grad_out.astype(jnp.bfloat16)
    grad_shrink = contract_rows(active, grad_rounded)
    grad_active = times_transpose(grad_rounded, shrink)
    _, gelu_back = jax.vjp(lambda values: jax.nn.gelu(values, approximate=False), hidden)
    grad_hidden = gelu_back(grad_active)[0].astype(jnp.bfloat16)
    grad_expand = contract_rows(input_two, grad_hidden)
    grad_input_two = times_transpose(grad_hidden, expand)
    grad_second = jnp.sum(grad_input_two * normed_two, axis=0)
    grad_middle = grad_out + norm_back(grad_input_two * second, normed_two, factor_two)
    middle_low = grad_middle.astype(jnp.bfloat16)
    grad_project = contract_rows(mixed_heads, middle_low)
    grad_mixed = times_transpose(middle_low, project).astype(jnp.bfloat16).reshape(length, H, HD)
    grad_soft = jnp.einsum(
        "qhd,khd->hqk", grad_mixed, value_rows, preferred_element_type=jnp.float32
    )
    grad_values = jnp.einsum(
        "hqk,qhd->khd", softmax_low, grad_mixed, preferred_element_type=jnp.float32
    )
    inner_sum = jnp.sum(softmax_out * grad_soft, axis=-1, keepdims=True)
    grad_scores = (softmax_out * (grad_soft - inner_sum)).astype(jnp.bfloat16)
    score_scale = HD ** (-0.5)
    grad_queries = (
        jnp.einsum("hqk,khd->qhd", grad_scores, key_rows, preferred_element_type=jnp.float32)
        * score_scale
    )
    grad_keys = (
        jnp.einsum("hqk,qhd->khd", grad_scores, queries, preferred_element_type=jnp.float32)
        * score_scale
    )
    grad_joint = (
        jnp.stack([grad_queries, grad_keys, grad_values], axis=1)
        .reshape(length, 3 * model_width)
        .astype(jnp.bfloat16)
    )
    grad_attend = contract_rows(input_one, grad_joint)
    grad_input_one = times_transpose(grad_joint, attend)
    grad_first = jnp.sum(grad_input_one * normed_one, axis=0)
    grad_residual = grad_middle + norm_back(grad_input_one * first, normed_one, factor_one)
    return (
        grad_residual,
        (grad_attend, grad_project, grad_expand, grad_shrink, grad_first, grad_second),
    )


def rows_of(index):
    return pl.ds(pl.multiple_of(index * ROWS, ROWS), ROWS)


def place(z, y, core, depth):
    return (core * 2 + y) * depth + z


class Reduction:
    def __init__(self, depth, parts, total, scratch):
        self.depth = depth
        self.parts, self.total = parts, total
        self.from_core, self.from_y, self.from_low, self.from_high = scratch[:4]
        self.core_s, self.core_r, self.y_s, self.y_r = scratch[4:8]
        self.up_s, self.up_r, self.down_s, self.down_r = scratch[8:12]
        self.section = lax.axis_index("section")
        self.me = lax.axis_index("batch")
        self.z, self.y, self.core = self.me // 4, (self.me // 2) % 2, self.me % 2

    def scratch(depth, count, wide):
        return (
            [pltpu.VMEM((count, 2 * depth * ROWS, wide), jnp.bfloat16)]
            + [pltpu.VMEM((count, depth * ROWS, wide), jnp.bfloat16)]
            + [pltpu.VMEM((count, (depth - 1) * ROWS, wide), jnp.bfloat16)] * 2
            + [pltpu.SemaphoreType.DMA((count,))] * 4
            + [pltpu.SemaphoreType.DMA((count, depth))] * 4
        )

    def peers(self):
        def device(z, y, core):
            return (self.section, z * 4 + y * 2 + core)

        return (
            device(self.z, self.y, 1 - self.core),
            device(self.z, 1 - self.y, self.core),
            device(jnp.minimum(self.z + 1, self.depth - 1), self.y, self.core),
            device(jnp.maximum(self.z - 1, 0), self.y, self.core),
            (1 - self.section, self.me),
        )

    def greet(self):
        barrier = pltpu.get_barrier_semaphore()
        core, other, high, low, across = self.peers()

        def signal(device):
            pl.semaphore_signal(barrier, inc=1, device_id=device, device_id_type=MESH)

        signal(core)
        signal(other)
        signal(across)

        @pl.when(self.z < self.depth - 1)
        def _():
            signal(high)

        @pl.when(self.z > 0)
        def _():
            signal(low)

        ends = (self.z == 0) | (self.z == self.depth - 1)

        @pl.when(ends)
        def _():
            pl.semaphore_wait(barrier, 4)

        @pl.when(jnp.logical_not(ends))
        def _():
            pl.semaphore_wait(barrier, 5)

    def block(self, k, core, y, z):
        return self.parts.at[k, rows_of(place(z, y, core, self.depth))]

    def core_copy(self, k):
        half = 2 * self.depth * ROWS
        return pltpu.make_async_remote_copy(
            self.parts.at[k, pl.ds(pl.multiple_of((1 - self.core) * half, half), half)],
            self.from_core.at[k], self.core_s.at[k], self.core_r.at[k],
            device_id=self.peers()[0], device_id_type=MESH,
        )

    def y_copy(self, k):
        quarter = self.depth * ROWS
        start = (self.core * 2 + 1 - self.y) * quarter
        return pltpu.make_async_remote_copy(
            self.parts.at[k, pl.ds(pl.multiple_of(start, quarter), quarter)],
            self.from_y.at[k], self.y_s.at[k], self.y_r.at[k],
            device_id=self.peers()[1], device_id_type=MESH,
        )

    def up_copy(self, k, to):
        return pltpu.make_async_remote_copy(
            self.block(k, self.core, self.y, to), self.from_low.at[k, rows_of(to - 1)],
            self.up_s.at[k, to], self.up_r.at[k, to],
            device_id=self.peers()[2], device_id_type=MESH,
        )

    def down_copy(self, k, to):
        return pltpu.make_async_remote_copy(
            self.block(k, self.core, self.y, to), self.from_high.at[k, rows_of(to)],
            self.down_s.at[k, to], self.down_r.at[k, to],
            device_id=self.peers()[3], device_id_type=MESH,
        )

    def add(self, here, other):
        here[...] = (here[...].astype(jnp.float32) + other.astype(jnp.float32)).astype(jnp.bfloat16)

    def start(self, k):
        self.core_copy(k).start()

    def after_core(self, k):
        self.core_copy(k).wait_recv()
        for far in (1, 0):
            half = (self.y + far) % 2

            @pl.loop(0, self.depth)
            def _(to):
                self.add(self.block(k, self.core, half, to), self.from_core[k, rows_of(half * self.depth + to)])

            if far:
                self.y_copy(k).start()

    def after_y(self, k):
        self.y_copy(k).wait_recv()

        @pl.loop(0, self.depth)
        def _(to):
            self.add(self.block(k, self.core, self.y, to), self.from_y[k, rows_of(to)])

    def go_up(self, k):
        for to in range(self.depth - 1, 0, -1):

            @pl.when(self.z < to)
            def _():
                copy = self.up_copy(k, to)

                @pl.when(self.z > 0)
                def _():
                    copy.wait_recv()
                    self.add(self.block(k, self.core, self.y, to), self.from_low[k, rows_of(to - 1)])

                copy.start()

    def go_down(self, k):
        for to in range(self.depth - 1):

            @pl.when(self.z > to)
            def _():
                copy = self.down_copy(k, to)

                @pl.when(self.z < self.depth - 1)
                def _():
                    copy.wait_recv()
                    self.add(self.block(k, self.core, self.y, to), self.from_high[k, rows_of(to)])

                copy.start()

    def finish(self, k):
        own = self.block(k, self.core, self.y, self.z)
        low = self.from_low.at[k, rows_of(jnp.maximum(self.z - 1, 0))]
        high = self.from_high.at[k, rows_of(jnp.minimum(self.z, self.depth - 2))]

        @pl.when(self.z == 0)
        def _():
            self.down_copy(k, self.z).wait_recv()
            self.total[k] = own[...].astype(jnp.float32) + high[...].astype(jnp.float32)

        @pl.when(self.z == self.depth - 1)
        def _():
            self.up_copy(k, self.z).wait_recv()
            self.total[k] = own[...].astype(jnp.float32) + low[...].astype(jnp.float32)

        @pl.when((self.z > 0) & (self.z < self.depth - 1))
        def _():
            self.down_copy(k, self.z).wait_recv()
            self.up_copy(k, self.z).wait_recv()
            self.total[k] = (
                own[...].astype(jnp.float32) + high[...].astype(jnp.float32) + low[...].astype(jnp.float32)
            )

    def drain(self, k):
        self.core_copy(k).wait_send()
        self.y_copy(k).wait_send()
        for to in range(self.depth - 1):

            @pl.when(self.z < to + 1)
            def _():
                self.up_copy(k, to + 1).wait_send()

            @pl.when(self.z > to)
            def _():
                self.down_copy(k, to).wait_send()

    def along(self, t, count):
        last = self.depth - 1
        at(t, count, self.after_y)
        at(t - self.z, count, self.go_up)
        at(t - last + self.z, count, self.go_down)
        at(t - 1 - last, count, self.finish)


def at(k, count, action):
    @pl.when((k >= 0) & (k < count))
    def _():
        action(k)


def over(count, size):
    def run(action):
        @pl.loop(0, count // size)
        def _(i):
            action(pl.ds(pl.multiple_of(i * size, size), size))

    return run


def train_kernel(
    depth, images,
    patches, signs, tiles, valid, cotangent, attend_in, project_in, expand_in, shrink_in, first, second, bottle_in,
    results, total, rest,
    parts, attend, project, left, right, soft, temp, saved, normed_one, normed_two, residual, work, factor_one,
    factor_two, bias, codes, bottle, delta, code_grad, bottle_sum, gain_one, gain_two, extra,
    loads, code_sems, *scratch,
):
    rows, width = patches.shape
    length = rows // images
    count, slabs = parts.shape[0], shrink_in.shape[0] // width
    pairs = width // 128
    main = Reduction(depth, parts, total, scratch[:12])
    small = Reduction(depth, extra, rest, scratch[12:24])
    encoding = main.section == 0
    lane = lax.broadcasted_iota(jnp.int32, (length, 128), 1)
    low_half = lane < HD
    bf, f32 = jnp.bfloat16, jnp.float32

    def dot(a, b):
        return jnp.dot(a, b, preferred_element_type=f32)

    def load(source, target, i):
        return pltpu.make_async_copy(source, target, loads.at[i])

    fetch = [load(patches, right.at[5], 0)]
    fetch += [load(attend_in.at[:, pl.ds(j * width, width)], attend.at[j], 1 + j) for j in range(3)]
    fetch += [load(project_in, project, 4)]
    fetch += [load(expand_in.at[:, pl.ds(j * width, width)], parts.at[slabs + j], 5 + j) for j in range(slabs)]
    fetch += [load(shrink_in.at[pl.ds(j * width, width)], parts.at[2 * slabs + j], 5 + slabs + j) for j in range(slabs)]
    fetch += [load(cotangent, right.at[0], 5 + 2 * slabs)]
    for copy in fetch:
        copy.start()
    main.greet()

    for i in range(images):
        row = jnp.broadcast_to(tiles[i : i + 1, :].astype(f32), (length, length))
        live = jnp.broadcast_to(valid[i : i + 1, :], (length, length)) == 1
        spot = lax.broadcasted_iota(jnp.int32, (length, length), 0) == lax.broadcasted_iota(
            jnp.int32, (length, length), 1
        )
        bias[i] = jnp.where(((row == row.T) & live) | spot, 0.0, -1000000000.0)
    code_width = signs.shape[1]
    codes[...] = jnp.zeros_like(codes)
    codes[:, :code_width] = ((2 * signs[...] - 1).astype(f32) / math.sqrt(code_width)).astype(bf)
    bottle[...] = jnp.zeros_like(bottle)
    bottle[:, :code_width] = bottle_in[...]
    gain_one[...] = jnp.zeros_like(gain_one)
    gain_two[...] = jnp.zeros_like(gain_two)
    fetch[0].wait()

    @pl.when(encoding)
    def _():
        residual[...] = right[5].astype(f32)

    @pl.when(jnp.logical_not(encoding))
    def _():
        residual[...] = times_transpose(codes[...], bottle[...])

    def norm(gain, normed, factor):
        @over(rows, 64)
        def _(r):
            values = residual[r, :]
            center = values - jnp.mean(values, axis=-1, keepdims=True)
            scale = lax.rsqrt(jnp.mean(center * center, axis=-1, keepdims=True) + 1e-06)
            unscaled = center * scale
            normed[r, :] = unscaled
            factor[r, :] = scale
            temp[r, :] = (unscaled * gain[...]).astype(bf)

    def keep_transpose(source, target):
        half = 8 * ROWS
        for i in range(width // half):
            turned = source[:, i * half : (i + 1) * half].T
            for j in range(8):
                z, y, core = i * 2 + j // 4, (j // 2) % 2, j % 2
                target[place(z, y, core, depth) * ROWS : (place(z, y, core, depth) + 1) * ROWS, :] = turned[
                    j * ROWS : (j + 1) * ROWS
                ]

    norm(first, normed_one, factor_one)
    for j in range(3):
        fetch[1 + j].wait()

        @over(width, 256)
        def _(c):
            right[6 + j, :, c] = dot(temp[...], attend[j, :, c]).astype(bf)

    keep_transpose(temp, left.at[slabs + 2])

    def pair_of(turn):
        image, pair = turn // pairs, turn % pairs
        r = pl.ds(pl.multiple_of(image * length, length), length)
        c = pl.ds(pl.multiple_of(pair * 128, 128), 128)
        return image, r, c

    def masked(values, low, scale=1.0):
        return jnp.where(low_half if low else jnp.logical_not(low_half), values * scale, 0.0).astype(bf)

    @pl.loop(0, images * pairs)
    def _(turn):
        image, r, c = pair_of(turn)
        query, key, value = right[6, r, c], right[7, r, c], right[8, r, c]
        mixed = []
        for head in range(2):
            scores = times_transpose(masked(query, head == 0, HD**-0.5), key) + bias[image]
            raised = jnp.exp(scores - jnp.max(scores, axis=-1, keepdims=True))
            weights = (raised * (1.0 / jnp.sum(raised, axis=-1, keepdims=True))).astype(bf)
            soft[turn, head * length : (head + 1) * length, :] = weights
            mixed.append(dot(weights, value))
        temp[r, c] = jnp.where(low_half, mixed[0], mixed[1]).astype(bf)

    fetch[4].wait()

    @over(width, 256)
    def _(c):
        residual[:, c] += dot(temp[...], project[:, c])

    keep_transpose(temp, left.at[slabs + 1])
    norm(second, normed_two, factor_two)
    keep_transpose(temp, left.at[slabs])

    for j in range(slabs):
        fetch[5 + j].wait()

        @over(width, 256)
        def _(c):
            hidden = dot(temp[...], parts[slabs + j, :, c])
            share = 0.5 + 0.5 * lax.erf(hidden * math.sqrt(0.5))
            slope = share + hidden * jnp.exp(-0.5 * hidden * hidden) * (1.0 / math.sqrt(2.0 * math.pi))
            parts[j, :rows, c] = (hidden * share).astype(bf)
            right[1 + j, :, c] = slope.astype(bf)

    for j in range(slabs):
        fetch[5 + slabs + j].wait()

    @over(width, 256)
    def _(c):
        for j in range(slabs):
            residual[:, c] += dot(parts[j, :rows, :], parts[2 * slabs + j, :, c])

    for i in range(2 * slabs):
        z, y = i // 2, i % 2
        turned = parts[i // 2, :rows, (i % 2) * 8 * ROWS : (i % 2 + 1) * 8 * ROWS].T
        for core in range(2):
            for j in range(slabs):
                spot = place(z, y, core, depth)
                left[j, spot * ROWS : (spot + 1) * ROWS, :] = turned[(core * 4 + j) * ROWS : (core * 4 + j + 1) * ROWS]

    saved[...] = residual[...].astype(bf)
    out_copy = pltpu.make_async_copy(saved, results, loads.at[6 + 2 * slabs])
    across = pltpu.make_async_remote_copy(
        delta, code_grad, code_sems.at[0], code_sems.at[1], device_id=main.peers()[4], device_id_type=MESH
    )
    fetch[5 + 2 * slabs].wait()

    @pl.when(encoding)
    def _():
        latent = dot(saved[...], bottle[...])
        scale = lax.rsqrt(jnp.sum(latent * latent, axis=-1, keepdims=True) + 1e-06)
        unit_code = latent * scale
        across.wait_recv()
        grad_unit = code_grad[...].astype(f32)
        grad_latent = (
            scale * (grad_unit - unit_code * jnp.sum(unit_code * grad_unit, axis=-1, keepdims=True))
        ).astype(bf)
        grad_out = times_transpose(grad_latent, bottle[...])
        residual[...] = grad_out
        right[0] = grad_out.astype(bf)
        bottle_sum[...] = contract_rows(saved[...], grad_latent)

    @pl.when(jnp.logical_not(encoding))
    def _():
        out_copy.start()
        residual[...] = right[0].astype(f32)

    def piece(k):
        a = jnp.minimum(k, slabs) + (k >= 2 * slabs).astype(jnp.int32) + (k > 2 * slabs).astype(jnp.int32)
        b = jnp.maximum(k - slabs + 1, 0)

        @over(width, 256)
        def _(c):
            parts[k, :, c] = dot(left[a], right[b, :, c]).astype(bf)

        main.start(k)

    def norm_back(gain, normed, factor, gain_sum):
        @over(rows, 64)
        def _(r):
            given, unscaled = work[r, :], normed[r, :]
            gain_sum[...] += jnp.sum((given * unscaled).reshape(8, 8, width), axis=0)
            grad = given * gain[...]
            inner = jnp.mean(grad * unscaled, axis=-1, keepdims=True)
            grad = residual[r, :] + factor[r, :] * (grad - jnp.mean(grad, axis=-1, keepdims=True) - unscaled * inner)
            residual[r, :] = grad
            saved[r, :] = grad.astype(bf)

    def chain():
        for j in range(slabs):

            @over(width, 256)
            def _(c):
                grad = times_transpose(right[0], parts[2 * slabs + j, c, :])
                right[1 + j, :, c] = (grad * right[1 + j, :, c].astype(f32)).astype(bf)

        @over(width, 256)
        def _(c):
            grad = times_transpose(right[1], parts[slabs, c, :])
            for j in range(1, slabs):
                grad += times_transpose(right[1 + j], parts[slabs + j, c, :])
            work[:, c] = grad

        @pl.when(jnp.logical_not(encoding))
        def _():
            out_copy.wait()

        norm_back(second, normed_two, factor_two, gain_two)
        right[5] = saved[...]

        @over(width, 256)
        def _(c):
            temp[:, c] = times_transpose(right[5], project[c, :]).astype(bf)

        @pl.loop(0, images * pairs)
        def _(turn):
            image, r, c = pair_of(turn)
            query, key, value, grad = right[6, r, c], right[7, r, c], right[8, r, c], temp[r, c]
            to_query, to_key, to_value = [], [], []
            for head in range(2):
                weights = soft[turn, head * length : (head + 1) * length, :]
                grad_head = masked(grad, head == 0)
                grad_soft = times_transpose(grad_head, value)
                exact = weights.astype(f32)
                inner = jnp.sum(exact * grad_soft, axis=-1, keepdims=True)
                grad_scores = (exact * (grad_soft - inner)).astype(bf)
                to_query.append(dot(grad_scores, key))
                to_key.append(contract_rows(grad_scores, masked(query, head == 0, HD**-0.5)))
                to_value.append(contract_rows(weights, grad_head))
            right[6, r, c] = (jnp.where(low_half, to_query[0], to_query[1]) * HD**-0.5).astype(bf)
            right[7, r, c] = (to_key[0] + to_key[1]).astype(bf)
            right[8, r, c] = (to_value[0] + to_value[1]).astype(bf)

        @over(width, 256)
        def _(c):
            grad = times_transpose(right[6], attend[0, c, :])
            for j in range(1, 3):
                grad += times_transpose(right[6 + j], attend[j, c, :])
            work[:, c] = grad

        norm_back(first, normed_one, factor_one, gain_one)

        @pl.when(jnp.logical_not(encoding))
        def _():
            delta[...] = dot(saved[...], bottle[...]).astype(bf)
            across.start()
            bottle_sum[...] = contract_rows(saved[...], codes[...])

        @pl.when(encoding)
        def _():
            out_copy.start()

    def first_pieces():
        @pl.loop(0, slabs)
        def _(k):
            piece(k)
            at(k - 1, slabs, main.after_core)

    @pl.loop(0, 2)
    def _(phase):
        pl.when(phase == main.section)(first_pieces)
        pl.when(phase != main.section)(chain)

    spare = lax.broadcasted_iota(jnp.int32, (width, 128), 1)
    column_one = jnp.sum(gain_one[...].T, axis=1, keepdims=True)
    column_two = jnp.sum(gain_two[...].T, axis=1, keepdims=True)
    gathered = jnp.where(
        spare == code_width, column_one, jnp.where(spare == code_width + 1, column_two, bottle_sum[...])
    ).astype(bf)
    for i in range(4 * depth):
        spot = place(i // 4, (i // 2) % 2, i % 2, depth)
        extra[0, spot * ROWS : (spot + 1) * ROWS, :] = gathered[i * ROWS : (i + 1) * ROWS]
    small.start(0)

    @pl.loop(slabs, count + depth + slabs)
    def _(t):
        at(t, count, piece)
        at(t - 1, count, main.after_core)
        at(t - slabs - 1, 1, small.after_core)
        main.along(t - slabs, count)
        small.along(t - slabs - 2, 1)

    @pl.when(encoding)
    def _():
        out_copy.wait()

    @pl.when(jnp.logical_not(encoding))
    def _():
        across.wait_send()

    small.drain(0)

    @pl.loop(0, count)
    def _(k):
        main.drain(k)


def train(depth, images, arrays):
    patches, signs, _, _, _, attend, project, expand, shrink, _, _, bottle = arrays
    rows, width = patches.shape
    slabs = shrink.shape[0] // width
    count = 2 * slabs + 4
    pairs, length = width // 128, rows // images
    hbm, vmem = pl.BlockSpec(memory_space=pl.ANY), pl.BlockSpec(memory_space=pltpu.VMEM)
    low, full = lambda *shape: pltpu.VMEM(shape, jnp.bfloat16), lambda *shape: pltpu.VMEM(shape, jnp.float32)
    return pl.pallas_call(
        functools.partial(train_kernel, depth, images),
        out_shape=(
            jax.ShapeDtypeStruct((rows, width), jnp.bfloat16),
            jax.ShapeDtypeStruct((count, ROWS, width), jnp.float32),
            jax.ShapeDtypeStruct((1, ROWS, 128), jnp.float32),
        ),
        in_specs=[hbm, vmem, vmem, vmem, hbm, hbm, hbm, hbm, hbm, vmem, vmem, vmem],
        out_specs=[hbm, vmem, vmem],
        scratch_shapes=[
            low(count, width, width),
            low(3, width, width),
            low(width, width),
            low(slabs + 3, width, rows),
            low(slabs + 5, rows, width),
            low(images * pairs, 2 * length, length),
            low(rows, width),
            low(rows, width),
            full(rows, width),
            full(rows, width),
            full(rows, width),
            full(rows, width),
            full(rows, 1),
            full(rows, 1),
            full(images, length, length),
            low(rows, 128),
            low(width, 128),
            low(rows, 128),
            low(rows, 128),
            full(width, 128),
            full(8, width),
            full(8, width),
            low(1, width, 128),
            pltpu.SemaphoreType.DMA((7 + 2 * slabs,)),
            pltpu.SemaphoreType.DMA((2,)),
        ]
        + Reduction.scratch(depth, count, width)
        + Reduction.scratch(depth, 1, 128),
        compiler_params=pltpu.CompilerParams(collective_id=0, has_side_effects=True, vmem_limit_bytes=63 << 20),
        name="train",
    )(*arrays)


def small_slice(*arrays):
    images = arrays[2].shape[0]
    arrays = arrays[:5] + tuple(member[0] for member in arrays[5:9]) + arrays[9:11] + (arrays[11][0],)
    results, total, rest = train(lax.axis_size("batch") // 4, images, arrays)
    width, code = arrays[11].shape
    slabs = arrays[8].shape[0] // width
    beside = lambda low, high: total[low:high].transpose(1, 0, 2).reshape(ROWS, -1)
    outs = (
        results,
        beside(2 * slabs + 1, total.shape[0]),
        total[2 * slabs],
        beside(slabs, 2 * slabs),
        total[:slabs].reshape(-1, width),
        rest[0, :, code],
        rest[0, :, code + 1],
        rest[0, :, :code],
    )
    return tuple(member[None] for member in outs)


def pick_index(stacked, chosen):
    return lax.dynamic_index_in_dim(stacked, chosen, 0, keepdims=False)


def body(
    patches,
    code_signs,
    tile_ids,
    patch_valid,
    cotangent,
    attend_weight,
    project_weight,
    expand_weight,
    shrink_weight,
    norm_first,
    norm_second,
    bottleneck,
):
    micro_count = tile_ids.shape[0]
    length = tile_ids.shape[1]
    code_width = code_signs.shape[1]
    encoding = lax.axis_index("section") == 0
    encoding_int = encoding.astype(jnp.int32)
    weights = (
        attend_weight[0],
        project_weight[0],
        expand_weight[0],
        shrink_weight[0],
        norm_first[0],
        norm_second[0],
    )
    bottle = bottleneck[0]
    code_values = ((2 * code_signs - 1).astype(jnp.float32) / math.sqrt(code_width)).astype(
        jnp.bfloat16
    )
    block_inputs = []
    outputs_low = []
    unit_codes = []
    unit_factors = []
    decoded_list = []
    kept_list = []
    for turn_index in range(micro_count):
        image_rows = patches[turn_index * length : (turn_index + 1) * length].astype(jnp.float32)
        decoder_in = times_transpose(
            code_values[turn_index * length : (turn_index + 1) * length], bottle
        )
        block_in = jnp.where(encoding, image_rows, decoder_in)
        allowed_keys = allowed(tile_ids[turn_index], patch_valid[turn_index])
        output, kept_parts = block_forward(block_in, weights, allowed_keys)
        output_low = output.astype(jnp.bfloat16)
        latent = jnp.dot(output_low, bottle, preferred_element_type=jnp.float32)
        factor = lax.rsqrt(jnp.sum(latent * latent, axis=-1, keepdims=True) + 1e-06)
        block_inputs.append(block_in)
        outputs_low.append(output_low)
        unit_codes.append(latent * factor)
        unit_factors.append(factor)
        decoded_list.append(output_low)
        kept_list.append(kept_parts)
    block_inputs = jnp.stack(block_inputs)
    outputs_low = jnp.stack(outputs_low)
    unit_codes = jnp.stack(unit_codes)
    unit_factors = jnp.stack(unit_factors)
    kept_stack = jax.tree.map(lambda *members: jnp.stack(members), *kept_list)
    totals = None
    sent_grad = jnp.zeros((length, code_width), jnp.bfloat16)
    input_grads = []
    for turn_index in range(micro_count + 1):
        if turn_index > 0:
            received = passed_along(sent_grad, "section", -1)
        else:
            received = jnp.zeros_like(sent_grad)
        chosen = jnp.clip(turn_index - encoding_int, 0, micro_count - 1)
        turn_flag = jnp.where(encoding, turn_index >= 1, turn_index < micro_count).astype(
            jnp.float32
        )
        kept_parts = jax.tree.map(lambda stacked: pick_index(stacked, chosen), kept_stack)
        unit_code = pick_index(unit_codes, chosen)
        factor = pick_index(unit_factors, chosen)
        output_low = pick_index(outputs_low, chosen)
        grad_unit = received.astype(jnp.float32)
        grad_latent = (
            factor
            * (grad_unit - unit_code * jnp.sum(unit_code * grad_unit, axis=-1, keepdims=True))
        ).astype(jnp.bfloat16)
        grad_encoded = times_transpose(grad_latent, bottle)
        bottle_encoder = contract_rows(output_low, grad_latent)
        given_grad = lax.dynamic_slice_in_dim(cotangent, chosen * length, length, 0).astype(
            jnp.float32
        )
        grad_out = jnp.where(encoding, grad_encoded, given_grad)
        grad_in, grads = block_backward(kept_parts, grad_out, weights)
        grad_in_low = grad_in.astype(jnp.bfloat16)
        code_rows = lax.dynamic_slice_in_dim(code_values, chosen * length, length, 0)
        bottle_decoder = contract_rows(grad_in_low, code_rows)
        sent_grad = jnp.dot(grad_in_low, bottle, preferred_element_type=jnp.float32).astype(
            jnp.bfloat16
        )
        grads = grads + (jnp.where(encoding, bottle_encoder, bottle_decoder),)
        grads = tuple((turn_flag * member for member in grads))
        if turn_index > 0:
            input_grads.append(grad_in_low)
        totals = (
            grads
            if totals is None
            else tuple((former + latter for former, latter in zip(totals, grads)))
        )
    totals = lax.psum_scatter(totals, "batch", scatter_dimension=0, tiled=True)
    pieces = [
        jnp.where(encoding, input_grads[turn_index], decoded_list[turn_index])
        for turn_index in range(micro_count)
    ]
    results = jnp.concatenate(pieces, axis=0)[None]
    return (
        results,
        totals[0][None],
        totals[1][None],
        totals[2][None],
        totals[3][None],
        totals[4][None],
        totals[5][None],
        totals[6][None],
    )


def solution(mesh):
    batch = mesh.shape["batch"]
    return jax.shard_map(
        small_slice if batch == 16 else body,
        mesh=mesh,
        in_specs=(
            P("batch", None),
            P("batch", None),
            P("batch", None),
            P("batch", None),
            P("batch", None),
            P("section", None, None),
            P("section", None, None),
            P("section", None, None),
            P("section", None, None),
            P("section", None),
            P("section", None),
            P("section", None, None),
        ),
        out_specs=(
            P("section", "batch", None),
            P("section", "batch", None),
            P("section", "batch", None),
            P("section", "batch", None),
            P("section", "batch", None),
            P("section", "batch"),
            P("section", "batch"),
            P("section", "batch", None),
        ),
        check_vma=False,
    )
```

```python
import functools
import math

import jax
import jax.numpy as jnp
from jax import lax
from jax.experimental import pallas as pl
from jax.experimental.pallas import tpu as pltpu
from jax.sharding import PartitionSpec as P

H = 12
HD = 64
MESH = pl.DeviceIdType.MESH
ROWS = 48
SLOTS = 8


def passed_along(block, axis, distance):
    devices = range(lax.axis_size(axis))
    route = [(i - distance, i) for i in devices if i - distance in devices]
    return lax.ppermute(block, axis, route)


def contract_rows(former, latter):
    return lax.dot_general(
        former, latter, (((0,), (0,)), ((), ())), preferred_element_type=jnp.float32
    )


def times_transpose(former, latter):
    return lax.dot_general(
        former, latter, (((1,), (1,)), ((), ())), preferred_element_type=jnp.float32
    )


def normalize(values):
    average = jnp.mean(values, axis=-1, keepdims=True)
    center = values - average
    spread = jnp.mean(center * center, axis=-1, keepdims=True)
    factor = lax.rsqrt(spread + 1e-06)
    return (center * factor, factor)


def norm_back(grad_normed, normed, factor):
    return factor * (
        grad_normed
        - jnp.mean(grad_normed, axis=-1, keepdims=True)
        - normed * jnp.mean(grad_normed * normed, axis=-1, keepdims=True)
    )


def allowed(tile_row, keep_row):
    places = jnp.arange(tile_row.shape[0])
    same_tile = tile_row[:, None] == tile_row[None, :]
    live_keys = keep_row[None, :] == 1
    return same_tile & live_keys | (places[:, None] == places[None, :])


def block_forward(residual, weights, allowed_keys):
    attend, project, expand, shrink, first, second = weights
    length, model_width = residual.shape
    normed_one, factor_one = normalize(residual)
    input_one = (normed_one * first).astype(jnp.bfloat16)
    joint_proj = jnp.dot(input_one, attend, preferred_element_type=jnp.float32).astype(jnp.bfloat16)
    split_parts = joint_proj.reshape(length, 3, H, HD)
    queries = split_parts[:, 0]
    key_rows = split_parts[:, 1]
    value_rows = split_parts[:, 2]
    scores = jnp.einsum(
        "qhd,khd->hqk", queries, key_rows, preferred_element_type=jnp.float32
    ) * HD ** (-0.5)
    scores = jnp.where(allowed_keys[None], scores, -1000000000.0)
    maximum = jnp.max(scores, axis=-1, keepdims=True)
    raised = jnp.exp(scores - maximum)
    softmax_out = raised / jnp.sum(raised, axis=-1, keepdims=True)
    softmax_low = softmax_out.astype(jnp.bfloat16)
    mixed_heads = jnp.einsum(
        "hqk,khd->qhd", softmax_low, value_rows, preferred_element_type=jnp.float32
    )
    mixed_heads = mixed_heads.reshape(length, model_width).astype(jnp.bfloat16)
    middle = residual + jnp.dot(mixed_heads, project, preferred_element_type=jnp.float32)
    normed_two, factor_two = normalize(middle)
    input_two = (normed_two * second).astype(jnp.bfloat16)
    hidden = jnp.dot(input_two, expand, preferred_element_type=jnp.float32)
    active = jax.nn.gelu(hidden, approximate=False).astype(jnp.bfloat16)
    output = middle + jnp.dot(active, shrink, preferred_element_type=jnp.float32)
    kept_parts = (
        normed_one,
        factor_one,
        input_one,
        queries,
        key_rows,
        value_rows,
        softmax_out,
        softmax_low,
        mixed_heads,
        normed_two,
        factor_two,
        input_two,
        hidden,
        active,
    )
    return (output, kept_parts)


def block_backward(kept_parts, grad_out, weights):
    attend, project, expand, shrink, first, second = weights
    (
        normed_one,
        factor_one,
        input_one,
        queries,
        key_rows,
        value_rows,
        softmax_out,
        softmax_low,
        mixed_heads,
        normed_two,
        factor_two,
        input_two,
        hidden,
        active,
    ) = kept_parts
    length, model_width = grad_out.shape
    grad_rounded = grad_out.astype(jnp.bfloat16)
    grad_shrink = contract_rows(active, grad_rounded)
    grad_active = times_transpose(grad_rounded, shrink)
    _, gelu_back = jax.vjp(lambda values: jax.nn.gelu(values, approximate=False), hidden)
    grad_hidden = gelu_back(grad_active)[0].astype(jnp.bfloat16)
    grad_expand = contract_rows(input_two, grad_hidden)
    grad_input_two = times_transpose(grad_hidden, expand)
    grad_second = jnp.sum(grad_input_two * normed_two, axis=0)
    grad_middle = grad_out + norm_back(grad_input_two * second, normed_two, factor_two)
    middle_low = grad_middle.astype(jnp.bfloat16)
    grad_project = contract_rows(mixed_heads, middle_low)
    grad_mixed = times_transpose(middle_low, project).astype(jnp.bfloat16).reshape(length, H, HD)
    grad_soft = jnp.einsum(
        "qhd,khd->hqk", grad_mixed, value_rows, preferred_element_type=jnp.float32
    )
    grad_values = jnp.einsum(
        "hqk,qhd->khd", softmax_low, grad_mixed, preferred_element_type=jnp.float32
    )
    inner_sum = jnp.sum(softmax_out * grad_soft, axis=-1, keepdims=True)
    grad_scores = (softmax_out * (grad_soft - inner_sum)).astype(jnp.bfloat16)
    score_scale = HD ** (-0.5)
    grad_queries = (
        jnp.einsum("hqk,khd->qhd", grad_scores, key_rows, preferred_element_type=jnp.float32)
        * score_scale
    )
    grad_keys = (
        jnp.einsum("hqk,qhd->khd", grad_scores, queries, preferred_element_type=jnp.float32)
        * score_scale
    )
    grad_joint = (
        jnp.stack([grad_queries, grad_keys, grad_values], axis=1)
        .reshape(length, 3 * model_width)
        .astype(jnp.bfloat16)
    )
    grad_attend = contract_rows(input_one, grad_joint)
    grad_input_one = times_transpose(grad_joint, attend)
    grad_first = jnp.sum(grad_input_one * normed_one, axis=0)
    grad_residual = grad_middle + norm_back(grad_input_one * first, normed_one, factor_one)
    return (
        grad_residual,
        (grad_attend, grad_project, grad_expand, grad_shrink, grad_first, grad_second),
    )


def rows_of(index):
    return pl.ds(pl.multiple_of(index * ROWS, ROWS), ROWS)


def place(z, y, core, depth):
    return (core * 2 + y) * depth + z


class Reduction:
    def __init__(self, depth, parts, total, scratch):
        self.depth = depth
        self.parts, self.total = parts, total
        self.from_core, self.from_y, self.from_low, self.from_high = scratch[:4]
        self.core_s, self.core_r, self.y_s, self.y_r = scratch[4:8]
        self.up_s, self.up_r, self.down_s, self.down_r, self.free = scratch[8:13]
        self.section = lax.axis_index("section")
        self.me = lax.axis_index("batch")
        self.z, self.y, self.core = self.me // 4, (self.me // 2) % 2, self.me % 2

    def scratch(depth, count, wide):
        return (
            [pltpu.VMEM((min(count, SLOTS), 2 * depth * ROWS, wide), jnp.bfloat16)]
            + [pltpu.VMEM((count, depth * ROWS, wide), jnp.bfloat16)]
            + [pltpu.VMEM((count, (depth - 1) * ROWS, wide), jnp.bfloat16)] * 2
            + [pltpu.SemaphoreType.DMA((count,))] * 4
            + [pltpu.SemaphoreType.DMA((count, depth))] * 4
            + [pltpu.SemaphoreType.REGULAR]
        )

    def peers(self):
        def device(z, y, core):
            return (self.section, z * 4 + y * 2 + core)

        return (
            device(self.z, self.y, 1 - self.core),
            device(self.z, 1 - self.y, self.core),
            device(jnp.minimum(self.z + 1, self.depth - 1), self.y, self.core),
            device(jnp.maximum(self.z - 1, 0), self.y, self.core),
            (1 - self.section, self.me),
        )

    def greet(self):
        barrier = pltpu.get_barrier_semaphore()
        core, other, high, low, across = self.peers()

        def signal(device):
            pl.semaphore_signal(barrier, inc=1, device_id=device, device_id_type=MESH)

        signal(core)
        signal(other)
        signal(across)

        @pl.when(self.z < self.depth - 1)
        def _():
            signal(high)

        @pl.when(self.z > 0)
        def _():
            signal(low)

        ends = (self.z == 0) | (self.z == self.depth - 1)

        @pl.when(ends)
        def _():
            pl.semaphore_wait(barrier, 4)

        @pl.when(jnp.logical_not(ends))
        def _():
            pl.semaphore_wait(barrier, 5)

    def block(self, k, core, y, z):
        return self.parts.at[k, rows_of(place(z, y, core, self.depth))]

    def core_copy(self, k):
        half = 2 * self.depth * ROWS
        return pltpu.make_async_remote_copy(
            self.parts.at[k, pl.ds(pl.multiple_of((1 - self.core) * half, half), half)],
            self.from_core.at[k % SLOTS], self.core_s.at[k], self.core_r.at[k],
            device_id=self.peers()[0], device_id_type=MESH,
        )

    def y_copy(self, k):
        quarter = self.depth * ROWS
        start = (self.core * 2 + 1 - self.y) * quarter
        return pltpu.make_async_remote_copy(
            self.parts.at[k, pl.ds(pl.multiple_of(start, quarter), quarter)],
            self.from_y.at[k], self.y_s.at[k], self.y_r.at[k],
            device_id=self.peers()[1], device_id_type=MESH,
        )

    def up_copy(self, k, to):
        return pltpu.make_async_remote_copy(
            self.block(k, self.core, self.y, to), self.from_low.at[k, rows_of(to - 1)],
            self.up_s.at[k, to], self.up_r.at[k, to],
            device_id=self.peers()[2], device_id_type=MESH,
        )

    def down_copy(self, k, to):
        return pltpu.make_async_remote_copy(
            self.block(k, self.core, self.y, to), self.from_high.at[k, rows_of(to)],
            self.down_s.at[k, to], self.down_r.at[k, to],
            device_id=self.peers()[3], device_id_type=MESH,
        )

    def add(self, here, other):
        here[...] = (here[...].astype(jnp.float32) + other.astype(jnp.float32)).astype(jnp.bfloat16)

    def start(self, k):
        @pl.when(k >= SLOTS)
        def _():
            pl.semaphore_wait(self.free, 1)

        self.core_copy(k).start()

    def after_core(self, k):
        self.core_copy(k).wait_recv()
        for far in (1, 0):
            half = (self.y + far) % 2

            @pl.loop(0, self.depth)
            def _(to):
                self.add(self.block(k, self.core, half, to), self.from_core[k % SLOTS, rows_of(half * self.depth + to)])

            if far:
                self.y_copy(k).start()

        @pl.when(k + SLOTS < self.parts.shape[0])
        def _():
            pl.semaphore_signal(self.free, inc=1, device_id=self.peers()[0], device_id_type=MESH)

    def after_y(self, k):
        self.y_copy(k).wait_recv()

        @pl.loop(0, self.depth)
        def _(to):
            self.add(self.block(k, self.core, self.y, to), self.from_y[k, rows_of(to)])

    def go_up(self, k):
        for to in range(self.depth - 1, 0, -1):

            @pl.when(self.z < to)
            def _():
                copy = self.up_copy(k, to)

                @pl.when(self.z > 0)
                def _():
                    copy.wait_recv()
                    self.add(self.block(k, self.core, self.y, to), self.from_low[k, rows_of(to - 1)])

                copy.start()

    def go_down(self, k):
        for to in range(self.depth - 1):

            @pl.when(self.z > to)
            def _():
                copy = self.down_copy(k, to)

                @pl.when(self.z < self.depth - 1)
                def _():
                    copy.wait_recv()
                    self.add(self.block(k, self.core, self.y, to), self.from_high[k, rows_of(to)])

                copy.start()

    def finish(self, k):
        own = self.block(k, self.core, self.y, self.z)
        low = self.from_low.at[k, rows_of(jnp.maximum(self.z - 1, 0))]
        high = self.from_high.at[k, rows_of(jnp.minimum(self.z, self.depth - 2))]

        @pl.when(self.z == 0)
        def _():
            self.down_copy(k, self.z).wait_recv()
            self.total[rows_of(k), :] = own[...].astype(jnp.float32) + high[...].astype(jnp.float32)

        @pl.when(self.z == self.depth - 1)
        def _():
            self.up_copy(k, self.z).wait_recv()
            self.total[rows_of(k), :] = own[...].astype(jnp.float32) + low[...].astype(jnp.float32)

        @pl.when((self.z > 0) & (self.z < self.depth - 1))
        def _():
            self.down_copy(k, self.z).wait_recv()
            self.up_copy(k, self.z).wait_recv()
            self.total[rows_of(k), :] = (
                own[...].astype(jnp.float32) + high[...].astype(jnp.float32) + low[...].astype(jnp.float32)
            )

    def drain(self, k):
        self.core_copy(k).wait_send()
        self.y_copy(k).wait_send()
        for to in range(self.depth - 1):

            @pl.when(self.z < to + 1)
            def _():
                self.up_copy(k, to + 1).wait_send()

            @pl.when(self.z > to)
            def _():
                self.down_copy(k, to).wait_send()

    def along(self, t, count):
        last = self.depth - 1
        at(t, count, self.after_y)
        at(t - self.z, count, self.go_up)
        at(t - last + self.z, count, self.go_down)
        at(t - 1 - last, count, self.finish)


def at(k, count, action):
    @pl.when((k >= 0) & (k < count))
    def _():
        action(k)


def over(count, size):
    def run(action):
        @pl.loop(0, count // size)
        def _(i):
            action(pl.ds(pl.multiple_of(i * size, size), size))

    return run


def train_kernel(
    depth, images,
    patches, signs, tiles, valid, cotangent, attend_in, project_in, expand_in, shrink_in, first, second, bottle_in,
    results, total, rest,
    parts, attend, project, left, right, soft, temp, saved, normed_one, normed_two, residual, factor_one,
    factor_two, bias, codes, bottle, delta, code_grad, bottle_sum, gain_one, gain_two, extra,
    loads, code_sems, *scratch,
):
    rows, width = patches.shape
    length = rows // images
    work = total.at[:rows]
    count, slabs = parts.shape[0], shrink_in.shape[0] // width
    pairs = width // 128
    main = Reduction(depth, parts, total, scratch[:13])
    small = Reduction(depth, extra, rest, scratch[13:26])
    encoding = main.section == 0
    lane = lax.broadcasted_iota(jnp.int32, (length, 128), 1)
    low_half = lane < HD
    bf, f32 = jnp.bfloat16, jnp.float32

    def dot(a, b):
        return jnp.dot(a, b, preferred_element_type=f32)

    def load(source, target, i):
        return pltpu.make_async_copy(source, target, loads.at[i])

    fetch = [load(patches, right.at[5], 0)]
    fetch += [load(attend_in.at[:, pl.ds(j * width, width)], attend.at[j], 1 + j) for j in range(3)]
    fetch += [load(project_in, project, 4)]
    fetch += [load(expand_in.at[:, pl.ds(j * width, width)], parts.at[slabs + j], 5 + j) for j in range(slabs)]
    fetch += [load(shrink_in.at[pl.ds(j * width, width)], parts.at[2 * slabs + j], 5 + slabs + j) for j in range(slabs)]
    fetch += [load(cotangent, right.at[0], 5 + 2 * slabs)]
    for copy in fetch:
        copy.start()
    main.greet()

    for i in range(images):
        row = jnp.broadcast_to(tiles[i : i + 1, :].astype(f32), (length, length))
        live = jnp.broadcast_to(valid[i : i + 1, :], (length, length)) == 1
        spot = lax.broadcasted_iota(jnp.int32, (length, length), 0) == lax.broadcasted_iota(
            jnp.int32, (length, length), 1
        )
        bias[i] = jnp.where(((row == row.T) & live) | spot, 0.0, -1000000000.0)
    code_width = signs.shape[0]
    work[:256, :] = jnp.zeros((256, width), f32)
    work[:code_width, :rows] = (2 * signs[...] - 1).astype(f32) / math.sqrt(code_width)
    work[128 : 128 + code_width, :] = bottle_in[...].astype(f32)
    codes[...] = work[:128, :rows].T.astype(bf)
    bottle[...] = work[128:256, :].T.astype(bf)
    gain_one[...] = jnp.zeros_like(gain_one)
    gain_two[...] = jnp.zeros_like(gain_two)
    fetch[0].wait()

    @pl.when(encoding)
    def _():
        residual[...] = right[5].astype(f32)

    @pl.when(jnp.logical_not(encoding))
    def _():
        residual[...] = times_transpose(codes[...], bottle[...])

    def norm(gain, normed, factor):
        values = residual[...]
        center = values - jnp.mean(values, axis=-1, keepdims=True)
        scale = lax.rsqrt(jnp.mean(center * center, axis=-1, keepdims=True) + 1e-06)
        unscaled = center * scale
        normed[...] = unscaled
        factor[...] = scale
        temp[...] = (unscaled * gain[...]).astype(bf)

    def keep_transpose(source, target):
        half = 8 * ROWS
        for i in range(width // half):
            turned = source[:, i * half : (i + 1) * half].T
            for j in range(8):
                z, y, core = i * 2 + j // 4, (j // 2) % 2, j % 2
                target[place(z, y, core, depth) * ROWS : (place(z, y, core, depth) + 1) * ROWS, :] = turned[
                    j * ROWS : (j + 1) * ROWS
                ]

    norm(first, normed_one, factor_one)
    for j in range(3):
        fetch[1 + j].wait()
        right[6 + j] = dot(temp[...], attend[j]).astype(bf)

    keep_transpose(temp, left.at[slabs + 2])

    group = 3
    heads = [(pair, head) for pair in range(group) for head in range(2)]

    def group_of(turn):
        image = turn * group // pairs
        start = turn * group - image * pairs
        lanes = [pl.ds(pl.multiple_of((start + pair) * 128, 128), 128) for pair in range(group)]
        return pl.ds(pl.multiple_of(image * length, length), length), lanes, image

    def masked(values, low, scale=1.0):
        return jnp.where(low_half if low else jnp.logical_not(low_half), values * scale, 0.0).astype(bf)

    def merged(members, pair):
        return jnp.where(low_half, members[2 * pair], members[2 * pair + 1])

    @pl.loop(0, images * pairs // group)
    def _(turn):
        r, lanes, image = group_of(turn)
        query, key, value = ([right[6 + j, r, c] for c in lanes] for j in range(3))
        scores = [
            times_transpose(masked(query[pair], head == 0, HD**-0.5), key[pair]) + bias[image] for pair, head in heads
        ]
        raised = [jnp.exp(member - jnp.max(member, axis=-1, keepdims=True)) for member in scores]
        weights = [(member * (1.0 / jnp.sum(member, axis=-1, keepdims=True))).astype(bf) for member in raised]
        for (pair, head), member in zip(heads, weights):
            soft[turn * group + pair, head * length : (head + 1) * length, :] = member
        mixed = [dot(member, value[pair]) for (pair, head), member in zip(heads, weights)]
        for pair, c in enumerate(lanes):
            temp[r, c] = merged(mixed, pair).astype(bf)

    fetch[4].wait()

    residual[...] += dot(temp[...], project[...])

    keep_transpose(temp, left.at[slabs + 1])
    norm(second, normed_two, factor_two)
    keep_transpose(temp, left.at[slabs])

    for j in range(slabs):
        fetch[5 + j].wait()

        hidden = dot(temp[...], parts[slabs + j])
        share = 0.5 + 0.5 * lax.erf(hidden * math.sqrt(0.5))
        slope = share + hidden * jnp.exp(-0.5 * hidden * hidden) * (1.0 / math.sqrt(2.0 * math.pi))
        parts[j, :rows, :] = (hidden * share).astype(bf)
        right[1 + j] = slope.astype(bf)

    for j in range(slabs):
        fetch[5 + slabs + j].wait()
        residual[...] += dot(parts[j, :rows, :], parts[2 * slabs + j])

    for i in range(2 * slabs):
        z, y = i // 2, i % 2
        turned = parts[i // 2, :rows, (i % 2) * 8 * ROWS : (i % 2 + 1) * 8 * ROWS].T
        for core in range(2):
            for j in range(slabs):
                spot = place(z, y, core, depth)
                left[j, spot * ROWS : (spot + 1) * ROWS, :] = turned[(core * 4 + j) * ROWS : (core * 4 + j + 1) * ROWS]

    saved[...] = residual[...].astype(bf)
    out_copy = pltpu.make_async_copy(saved, results, loads.at[6 + 2 * slabs])
    across = pltpu.make_async_remote_copy(
        delta, code_grad, code_sems.at[0], code_sems.at[1], device_id=main.peers()[4], device_id_type=MESH
    )
    fetch[5 + 2 * slabs].wait()

    @pl.when(encoding)
    def _():
        latent = dot(saved[...], bottle[...])
        scale = lax.rsqrt(jnp.sum(latent * latent, axis=-1, keepdims=True) + 1e-06)
        unit_code = latent * scale
        across.wait_recv()
        grad_unit = code_grad[...].astype(f32)
        grad_latent = (
            scale * (grad_unit - unit_code * jnp.sum(unit_code * grad_unit, axis=-1, keepdims=True))
        ).astype(bf)
        grad_out = times_transpose(grad_latent, bottle[...])
        residual[...] = grad_out
        right[0] = grad_out.astype(bf)
        bottle_sum[...] = contract_rows(saved[...], grad_latent)

    @pl.when(jnp.logical_not(encoding))
    def _():
        out_copy.start()
        residual[...] = right[0].astype(f32)

    def piece(k):
        a = jnp.minimum(k, slabs) + (k >= 2 * slabs).astype(jnp.int32) + (k > 2 * slabs).astype(jnp.int32)
        b = jnp.maximum(k - slabs + 1, 0)

        parts[k] = dot(left[a], right[b]).astype(bf)
        main.start(k)

    def norm_back(gain, normed, factor, gain_sum, low):
        @over(rows, length)
        def _(r):
            given, unscaled = work[r, :], normed[r, :]
            gain_sum[...] += jnp.sum((given * unscaled).reshape(-1, 8, width), axis=0)
            grad = given * gain[...]
            inner = jnp.mean(grad * unscaled, axis=-1, keepdims=True)
            grad = residual[r, :] + factor[r, :] * (grad - jnp.mean(grad, axis=-1, keepdims=True) - unscaled * inner)
            residual[r, :] = grad
            low[r, :] = grad.astype(bf)

    def chain():
        for j in range(slabs):
            grad = times_transpose(right[0], parts[2 * slabs + j])
            right[1 + j] = (grad * right[1 + j].astype(f32)).astype(bf)
        grad = times_transpose(right[1], parts[slabs])
        for j in range(1, slabs):
            grad += times_transpose(right[1 + j], parts[slabs + j])
        work[...] = grad

        norm_back(second, normed_two, factor_two, gain_two, right.at[5])

        temp[...] = times_transpose(right[5], project[...]).astype(bf)

        @pl.loop(0, images * pairs // group)
        def _(turn):
            r, lanes, image = group_of(turn)
            query, key, value = ([right[6 + j, r, c] for c in lanes] for j in range(3))
            weights = [soft[turn * group + pair, head * length : (head + 1) * length, :] for pair, head in heads]
            grad_heads = [masked(temp[r, lanes[pair]], head == 0) for pair, head in heads]
            grad_soft = [times_transpose(member, value[pair]) for (pair, head), member in zip(heads, grad_heads)]
            grad_scores = []
            for low, member in zip(weights, grad_soft):
                exact = low.astype(f32)
                inner = jnp.sum(exact * member, axis=-1, keepdims=True)
                grad_scores.append((exact * (member - inner)).astype(bf))
            to_query = [dot(member, key[pair]) for (pair, head), member in zip(heads, grad_scores)]
            to_key = [
                contract_rows(member, masked(query[pair], head == 0, HD**-0.5))
                for (pair, head), member in zip(heads, grad_scores)
            ]
            to_value = [contract_rows(low, member) for low, member in zip(weights, grad_heads)]
            for pair, c in enumerate(lanes):
                right[6, r, c] = (merged(to_query, pair) * HD**-0.5).astype(bf)
                right[7, r, c] = (to_key[2 * pair] + to_key[2 * pair + 1]).astype(bf)
                right[8, r, c] = (to_value[2 * pair] + to_value[2 * pair + 1]).astype(bf)

        grad = times_transpose(right[6], attend[0])
        for j in range(1, 3):
            grad += times_transpose(right[6 + j], attend[j])
        work[...] = grad

        @pl.when(jnp.logical_not(encoding))
        def _():
            out_copy.wait()

        norm_back(first, normed_one, factor_one, gain_one, saved)

        @pl.when(jnp.logical_not(encoding))
        def _():
            delta[...] = dot(saved[...], bottle[...]).astype(bf)
            across.start()
            bottle_sum[...] = contract_rows(saved[...], codes[...])

        @pl.when(encoding)
        def _():
            out_copy.start()

    def first_pieces():
        @pl.loop(0, slabs)
        def _(k):
            piece(k)
            at(k - 1, slabs, main.after_core)

    @pl.loop(0, 2)
    def _(phase):
        pl.when(phase == main.section)(first_pieces)
        pl.when(phase != main.section)(chain)

    spare = lax.broadcasted_iota(jnp.int32, (width, 128), 1)
    column_one = jnp.sum(gain_one[...].T, axis=1, keepdims=True)
    column_two = jnp.sum(gain_two[...].T, axis=1, keepdims=True)
    gathered = jnp.where(
        spare == code_width, column_one, jnp.where(spare == code_width + 1, column_two, bottle_sum[...])
    ).astype(bf)
    for i in range(4 * depth):
        spot = place(i // 4, (i // 2) % 2, i % 2, depth)
        extra[0, spot * ROWS : (spot + 1) * ROWS, :] = gathered[i * ROWS : (i + 1) * ROWS]
    small.start(0)

    @pl.loop(slabs, count + depth + slabs)
    def _(t):
        at(t, count, piece)
        at(t - 1, count, main.after_core)
        at(t - slabs - 1, 1, small.after_core)
        main.along(t - slabs, count)
        small.along(t - slabs - 2, 1)

    @pl.when(encoding)
    def _():
        out_copy.wait()

    @pl.when(jnp.logical_not(encoding))
    def _():
        across.wait_send()

    small.drain(0)

    @pl.loop(0, count)
    def _(k):
        main.drain(k)


def train(depth, images, arrays):
    patches, signs, _, _, _, attend, project, expand, shrink, _, _, bottle = arrays
    rows, width = patches.shape
    slabs = shrink.shape[0] // width
    count = 2 * slabs + 4
    pairs, length = width // 128, rows // images
    hbm, vmem = pl.BlockSpec(memory_space=pl.ANY), pl.BlockSpec(memory_space=pltpu.VMEM)
    low, full = lambda *shape: pltpu.VMEM(shape, jnp.bfloat16), lambda *shape: pltpu.VMEM(shape, jnp.float32)
    return pl.pallas_call(
        functools.partial(train_kernel, depth, images),
        out_shape=(
            jax.ShapeDtypeStruct((rows, width), jnp.bfloat16),
            jax.ShapeDtypeStruct((count * ROWS, width), jnp.float32),
            jax.ShapeDtypeStruct((ROWS, 128), jnp.float32),
        ),
        in_specs=[hbm, vmem, vmem, vmem, hbm, hbm, hbm, hbm, hbm, vmem, vmem, vmem],
        out_specs=[hbm, vmem, vmem],
        scratch_shapes=[
            low(count, width, width),
            low(3, width, width),
            low(width, width),
            low(slabs + 3, width, rows),
            low(slabs + 5, rows, width),
            low(images * pairs, 2 * length, length),
            low(rows, width),
            low(rows, width),
            full(rows, width),
            full(rows, width),
            full(rows, width),
            full(rows, 1),
            full(rows, 1),
            full(images, length, length),
            low(rows, 128),
            low(width, 128),
            low(rows, 128),
            low(rows, 128),
            full(width, 128),
            full(8, width),
            full(8, width),
            low(1, width, 128),
            pltpu.SemaphoreType.DMA((7 + 2 * slabs,)),
            pltpu.SemaphoreType.DMA((2,)),
        ]
        + Reduction.scratch(depth, count, width)
        + Reduction.scratch(depth, 1, 128),
        compiler_params=pltpu.CompilerParams(collective_id=0, has_side_effects=True, vmem_limit_bytes=63 << 20),
        name="train",
    )(*arrays)


def deliver_kernel(slabs, code, raw, total, rest, results, attend, project, expand, shrink, first, second, bottle):
    width = total.shape[1]
    results[...] = raw[...]
    for j in range(slabs):
        shrink[j * ROWS : (j + 1) * ROWS, :] = total[j * ROWS : (j + 1) * ROWS, :]
        expand[:, j * width : (j + 1) * width] = total[(slabs + j) * ROWS : (slabs + j + 1) * ROWS, :]
    project[...] = total[2 * slabs * ROWS : (2 * slabs + 1) * ROWS, :]
    for j in range(3):
        start = (2 * slabs + 1 + j) * ROWS
        attend[:, j * width : (j + 1) * width] = total[start : start + ROWS, :]
    turned = rest[...].T
    first[...] = turned[code : code + 1]
    second[...] = turned[code + 1 : code + 2]
    for i in range(code):
        bottle[i] = turned[i : i + 1]


def deliver(raw, total, rest, slabs, code):
    width = total.shape[1]
    vmem = pl.BlockSpec(memory_space=pltpu.VMEM)
    full = lambda *shape: jax.ShapeDtypeStruct(shape, jnp.float32)
    return pl.pallas_call(
        functools.partial(deliver_kernel, slabs, code),
        out_shape=(
            jax.ShapeDtypeStruct(raw.shape, raw.dtype),
            full(ROWS, 3 * width),
            full(ROWS, width),
            full(ROWS, slabs * width),
            full(slabs * ROWS, width),
            full(1, ROWS),
            full(1, ROWS),
            full(code, 1, ROWS),
        ),
        in_specs=[vmem] * 3,
        out_specs=[vmem] * 8,
        name="deliver",
    )(raw, total, rest)


def two_images(*arrays):
    images = arrays[2].shape[0]
    code = arrays[1].shape[1]
    slabs = arrays[8].shape[1] // arrays[0].shape[1]
    weights = tuple(member[0] for member in arrays[5:9])
    arrays = (arrays[0], arrays[1].T) + arrays[2:5] + weights + arrays[9:11] + (arrays[11][0].T,)
    raw, total, rest = train(lax.axis_size("batch") // 4, images, arrays)
    results, attend, project, expand, shrink, first, second, bottle = deliver(raw, total, rest, slabs, code)
    return (
        results[None], attend[None], project[None], expand[None], shrink[None], first, second, bottle.transpose(1, 2, 0)
    )


def pick_index(stacked, chosen):
    return lax.dynamic_index_in_dim(stacked, chosen, 0, keepdims=False)


def body(
    patches,
    code_signs,
    tile_ids,
    patch_valid,
    cotangent,
    attend_weight,
    project_weight,
    expand_weight,
    shrink_weight,
    norm_first,
    norm_second,
    bottleneck,
):
    micro_count = tile_ids.shape[0]
    length = tile_ids.shape[1]
    code_width = code_signs.shape[1]
    encoding = lax.axis_index("section") == 0
    encoding_int = encoding.astype(jnp.int32)
    weights = (
        attend_weight[0],
        project_weight[0],
        expand_weight[0],
        shrink_weight[0],
        norm_first[0],
        norm_second[0],
    )
    bottle = bottleneck[0]
    code_values = ((2 * code_signs - 1).astype(jnp.float32) / math.sqrt(code_width)).astype(
        jnp.bfloat16
    )
    block_inputs = []
    outputs_low = []
    unit_codes = []
    unit_factors = []
    decoded_list = []
    kept_list = []
    for turn_index in range(micro_count):
        image_rows = patches[turn_index * length : (turn_index + 1) * length].astype(jnp.float32)
        decoder_in = times_transpose(
            code_values[turn_index * length : (turn_index + 1) * length], bottle
        )
        block_in = jnp.where(encoding, image_rows, decoder_in)
        allowed_keys = allowed(tile_ids[turn_index], patch_valid[turn_index])
        output, kept_parts = block_forward(block_in, weights, allowed_keys)
        output_low = output.astype(jnp.bfloat16)
        latent = jnp.dot(output_low, bottle, preferred_element_type=jnp.float32)
        factor = lax.rsqrt(jnp.sum(latent * latent, axis=-1, keepdims=True) + 1e-06)
        block_inputs.append(block_in)
        outputs_low.append(output_low)
        unit_codes.append(latent * factor)
        unit_factors.append(factor)
        decoded_list.append(output_low)
        kept_list.append(kept_parts)
    block_inputs = jnp.stack(block_inputs)
    outputs_low = jnp.stack(outputs_low)
    unit_codes = jnp.stack(unit_codes)
    unit_factors = jnp.stack(unit_factors)
    kept_stack = jax.tree.map(lambda *members: jnp.stack(members), *kept_list)
    totals = None
    sent_grad = jnp.zeros((length, code_width), jnp.bfloat16)
    input_grads = []
    for turn_index in range(micro_count + 1):
        if turn_index > 0:
            received = passed_along(sent_grad, "section", -1)
        else:
            received = jnp.zeros_like(sent_grad)
        chosen = jnp.clip(turn_index - encoding_int, 0, micro_count - 1)
        turn_flag = jnp.where(encoding, turn_index >= 1, turn_index < micro_count).astype(
            jnp.float32
        )
        kept_parts = jax.tree.map(lambda stacked: pick_index(stacked, chosen), kept_stack)
        unit_code = pick_index(unit_codes, chosen)
        factor = pick_index(unit_factors, chosen)
        output_low = pick_index(outputs_low, chosen)
        grad_unit = received.astype(jnp.float32)
        grad_latent = (
            factor
            * (grad_unit - unit_code * jnp.sum(unit_code * grad_unit, axis=-1, keepdims=True))
        ).astype(jnp.bfloat16)
        grad_encoded = times_transpose(grad_latent, bottle)
        bottle_encoder = contract_rows(output_low, grad_latent)
        given_grad = lax.dynamic_slice_in_dim(cotangent, chosen * length, length, 0).astype(
            jnp.float32
        )
        grad_out = jnp.where(encoding, grad_encoded, given_grad)
        grad_in, grads = block_backward(kept_parts, grad_out, weights)
        grad_in_low = grad_in.astype(jnp.bfloat16)
        code_rows = lax.dynamic_slice_in_dim(code_values, chosen * length, length, 0)
        bottle_decoder = contract_rows(grad_in_low, code_rows)
        sent_grad = jnp.dot(grad_in_low, bottle, preferred_element_type=jnp.float32).astype(
            jnp.bfloat16
        )
        grads = grads + (jnp.where(encoding, bottle_encoder, bottle_decoder),)
        grads = tuple((turn_flag * member for member in grads))
        if turn_index > 0:
            input_grads.append(grad_in_low)
        totals = (
            grads
            if totals is None
            else tuple((former + latter for former, latter in zip(totals, grads)))
        )
    totals = lax.psum_scatter(totals, "batch", scatter_dimension=0, tiled=True)
    pieces = [
        jnp.where(encoding, input_grads[turn_index], decoded_list[turn_index])
        for turn_index in range(micro_count)
    ]
    results = jnp.concatenate(pieces, axis=0)[None]
    return (
        results,
        totals[0][None],
        totals[1][None],
        totals[2][None],
        totals[3][None],
        totals[4][None],
        totals[5][None],
        totals[6][None],
    )


def solution(mesh):
    batch = mesh.shape["batch"]
    return jax.shard_map(
        two_images if batch == 16 else body,
        mesh=mesh,
        in_specs=(
            P("batch", None),
            P("batch", None),
            P("batch", None),
            P("batch", None),
            P("batch", None),
            P("section", None, None),
            P("section", None, None),
            P("section", None, None),
            P("section", None, None),
            P("section", None),
            P("section", None),
            P("section", None, None),
        ),
        out_specs=(
            P("section", "batch", None),
            P("section", "batch", None),
            P("section", "batch", None),
            P("section", "batch", None),
            P("section", "batch", None),
            P("section", "batch"),
            P("section", "batch"),
            P("section", "batch", None),
        ),
        check_vma=False,
    )
```

```python
import functools
import math

import jax
import jax.numpy as jnp
from jax import lax
from jax.experimental import pallas as pl
from jax.experimental.pallas import tpu as pltpu
from jax.sharding import PartitionSpec as P

H = 12
HD = 64
MESH = pl.DeviceIdType.MESH
ROWS = 48
SLOTS = 6
EARLY = 2


def passed_along(block, axis, distance):
    devices = range(lax.axis_size(axis))
    route = [(i - distance, i) for i in devices if i - distance in devices]
    return lax.ppermute(block, axis, route)


def contract_rows(former, latter):
    return lax.dot_general(
        former, latter, (((0,), (0,)), ((), ())), preferred_element_type=jnp.float32
    )


def times_transpose(former, latter):
    return lax.dot_general(
        former, latter, (((1,), (1,)), ((), ())), preferred_element_type=jnp.float32
    )


def normalize(values):
    average = jnp.mean(values, axis=-1, keepdims=True)
    center = values - average
    spread = jnp.mean(center * center, axis=-1, keepdims=True)
    factor = lax.rsqrt(spread + 1e-06)
    return (center * factor, factor)


def norm_back(grad_normed, normed, factor):
    return factor * (
        grad_normed
        - jnp.mean(grad_normed, axis=-1, keepdims=True)
        - normed * jnp.mean(grad_normed * normed, axis=-1, keepdims=True)
    )


def allowed(tile_row, keep_row):
    places = jnp.arange(tile_row.shape[0])
    same_tile = tile_row[:, None] == tile_row[None, :]
    live_keys = keep_row[None, :] == 1
    return same_tile & live_keys | (places[:, None] == places[None, :])


def block_forward(residual, weights, allowed_keys):
    attend, project, expand, shrink, first, second = weights
    length, model_width = residual.shape
    normed_one, factor_one = normalize(residual)
    input_one = (normed_one * first).astype(jnp.bfloat16)
    joint_proj = jnp.dot(input_one, attend, preferred_element_type=jnp.float32).astype(jnp.bfloat16)
    split_parts = joint_proj.reshape(length, 3, H, HD)
    queries = split_parts[:, 0]
    key_rows = split_parts[:, 1]
    value_rows = split_parts[:, 2]
    scores = jnp.einsum(
        "qhd,khd->hqk", queries, key_rows, preferred_element_type=jnp.float32
    ) * HD ** (-0.5)
    scores = jnp.where(allowed_keys[None], scores, -1000000000.0)
    maximum = jnp.max(scores, axis=-1, keepdims=True)
    raised = jnp.exp(scores - maximum)
    softmax_out = raised / jnp.sum(raised, axis=-1, keepdims=True)
    softmax_low = softmax_out.astype(jnp.bfloat16)
    mixed_heads = jnp.einsum(
        "hqk,khd->qhd", softmax_low, value_rows, preferred_element_type=jnp.float32
    )
    mixed_heads = mixed_heads.reshape(length, model_width).astype(jnp.bfloat16)
    middle = residual + jnp.dot(mixed_heads, project, preferred_element_type=jnp.float32)
    normed_two, factor_two = normalize(middle)
    input_two = (normed_two * second).astype(jnp.bfloat16)
    hidden = jnp.dot(input_two, expand, preferred_element_type=jnp.float32)
    active = jax.nn.gelu(hidden, approximate=False).astype(jnp.bfloat16)
    output = middle + jnp.dot(active, shrink, preferred_element_type=jnp.float32)
    kept_parts = (
        normed_one,
        factor_one,
        input_one,
        queries,
        key_rows,
        value_rows,
        softmax_out,
        softmax_low,
        mixed_heads,
        normed_two,
        factor_two,
        input_two,
        hidden,
        active,
    )
    return (output, kept_parts)


def block_backward(kept_parts, grad_out, weights):
    attend, project, expand, shrink, first, second = weights
    (
        normed_one,
        factor_one,
        input_one,
        queries,
        key_rows,
        value_rows,
        softmax_out,
        softmax_low,
        mixed_heads,
        normed_two,
        factor_two,
        input_two,
        hidden,
        active,
    ) = kept_parts
    length, model_width = grad_out.shape
    grad_rounded = grad_out.astype(jnp.bfloat16)
    grad_shrink = contract_rows(active, grad_rounded)
    grad_active = times_transpose(grad_rounded, shrink)
    _, gelu_back = jax.vjp(lambda values: jax.nn.gelu(values, approximate=False), hidden)
    grad_hidden = gelu_back(grad_active)[0].astype(jnp.bfloat16)
    grad_expand = contract_rows(input_two, grad_hidden)
    grad_input_two = times_transpose(grad_hidden, expand)
    grad_second = jnp.sum(grad_input_two * normed_two, axis=0)
    grad_middle = grad_out + norm_back(grad_input_two * second, normed_two, factor_two)
    middle_low = grad_middle.astype(jnp.bfloat16)
    grad_project = contract_rows(mixed_heads, middle_low)
    grad_mixed = times_transpose(middle_low, project).astype(jnp.bfloat16).reshape(length, H, HD)
    grad_soft = jnp.einsum(
        "qhd,khd->hqk", grad_mixed, value_rows, preferred_element_type=jnp.float32
    )
    grad_values = jnp.einsum(
        "hqk,qhd->khd", softmax_low, grad_mixed, preferred_element_type=jnp.float32
    )
    inner_sum = jnp.sum(softmax_out * grad_soft, axis=-1, keepdims=True)
    grad_scores = (softmax_out * (grad_soft - inner_sum)).astype(jnp.bfloat16)
    score_scale = HD ** (-0.5)
    grad_queries = (
        jnp.einsum("hqk,khd->qhd", grad_scores, key_rows, preferred_element_type=jnp.float32)
        * score_scale
    )
    grad_keys = (
        jnp.einsum("hqk,qhd->khd", grad_scores, queries, preferred_element_type=jnp.float32)
        * score_scale
    )
    grad_joint = (
        jnp.stack([grad_queries, grad_keys, grad_values], axis=1)
        .reshape(length, 3 * model_width)
        .astype(jnp.bfloat16)
    )
    grad_attend = contract_rows(input_one, grad_joint)
    grad_input_one = times_transpose(grad_joint, attend)
    grad_first = jnp.sum(grad_input_one * normed_one, axis=0)
    grad_residual = grad_middle + norm_back(grad_input_one * first, normed_one, factor_one)
    return (
        grad_residual,
        (grad_attend, grad_project, grad_expand, grad_shrink, grad_first, grad_second),
    )


def rows_of(index):
    return pl.ds(pl.multiple_of(index * ROWS, ROWS), ROWS)


def place(z, y, core, depth):
    return (core * 2 + y) * depth + z


class Reduction:
    def __init__(self, depth, early, parts, total, scratch):
        self.depth, self.early = depth, early
        self.count, self.passes = parts.shape[0], parts.shape[0] + early
        self.parts, self.total = parts, total
        self.from_core, self.from_y, self.from_low, self.from_high = scratch[:4]
        self.core_s, self.core_r, self.y_s, self.y_r = scratch[4:8]
        self.up_s, self.up_r, self.down_s, self.down_r, self.free = scratch[8:13]
        self.section = lax.axis_index("section")
        self.me = lax.axis_index("batch")
        self.z, self.y, self.core = self.me // 4, (self.me // 2) % 2, self.me % 2

    def scratch(depth, early, count, wide):
        low, dma = lambda *shape: pltpu.VMEM(shape, jnp.bfloat16), pltpu.SemaphoreType.DMA
        return [
            low(min(count, SLOTS), 2 * depth * ROWS, wide),
            low((count - early) * depth * ROWS + early * ROWS, wide),
            low(count + early, (depth - 1) * ROWS, wide),
            low(count + early, (depth - 1) * ROWS, wide),
        ] + [dma((count,))] * 4 + [dma((count + early, depth))] * 4 + [pltpu.SemaphoreType.REGULAR]

    def device(self, z, y, core):
        return (self.section, z * 4 + y * 2 + core)

    def peers(self):
        return (
            self.device(self.z, self.y, 1 - self.core),
            self.device(self.z, 1 - self.y, self.core),
            self.device(jnp.minimum(self.z + 1, self.depth - 1), self.y, self.core),
            self.device(jnp.maximum(self.z - 1, 0), self.y, self.core),
            (1 - self.section, self.me),
        )

    def greet(self):
        barrier = pltpu.get_barrier_semaphore()

        def signal(device):
            pl.semaphore_signal(barrier, inc=1, device_id=device, device_id_type=MESH)

        core, other, _, _, across = self.peers()
        for peer in (core, other, across):
            signal(peer)
        for z in range(self.depth):
            pl.when(self.z != z)(lambda z=z: signal(self.device(z, self.y, self.core)))

    def meet(self):
        pl.semaphore_wait(pltpu.get_barrier_semaphore(), self.depth + 2)

    def block(self, k, core, y, z):
        return self.parts.at[k, rows_of(place(z, y, core, self.depth))]

    def core_copy(self, k):
        half = 2 * self.depth * ROWS
        return pltpu.make_async_remote_copy(
            self.parts.at[k, pl.ds(pl.multiple_of((1 - self.core) * half, half), half)],
            self.from_core.at[k % SLOTS], self.core_s.at[k], self.core_r.at[k],
            device_id=self.peers()[0], device_id_type=MESH,
        )

    def slot(self, k):
        return jnp.maximum(k - self.early, 0)

    def is_early(self, k):
        return (k >= 1) & (k <= self.early)

    def y_copy(self, k):
        quarter = self.depth * ROWS
        start, slot = (self.core * 2 + 1 - self.y) * quarter, self.slot(k) * quarter
        return pltpu.make_async_remote_copy(
            self.parts.at[k, pl.ds(pl.multiple_of(start, quarter), quarter)],
            self.from_y.at[pl.ds(pl.multiple_of(slot, quarter), quarter)], self.y_s.at[k], self.y_r.at[k],
            device_id=self.peers()[1], device_id_type=MESH,
        )

    def last_rows(self, k):
        return rows_of((self.count - self.early) * self.depth + k - 1)

    def last_copy(self, k):
        return pltpu.make_async_remote_copy(
            self.block(k, self.core, 1 - self.y, self.z), self.from_y.at[self.last_rows(k)],
            self.y_s.at[k], self.y_r.at[k],
            device_id=self.peers()[1], device_id_type=MESH,
        )

    def of_pass(self, p):
        if not self.early:
            return p, self.y
        soon = p < 2 * self.early
        piece = jnp.where(soon, 1 + p // 2, jnp.where(p == 2 * self.early, 0, p - self.early))
        return piece, jnp.where(soon & (p % 2 == 0), 1 - self.y, self.y)

    def pass_block(self, p, to):
        k, y = self.of_pass(p)
        return self.block(k, self.core, y, to)

    def up_copy(self, p, to):
        return pltpu.make_async_remote_copy(
            self.pass_block(p, to), self.from_low.at[p, rows_of(to - 1)],
            self.up_s.at[p, to], self.up_r.at[p, to],
            device_id=self.peers()[2], device_id_type=MESH,
        )

    def down_copy(self, p, to):
        return pltpu.make_async_remote_copy(
            self.pass_block(p, to), self.from_high.at[p, rows_of(to)],
            self.down_s.at[p, to], self.down_r.at[p, to],
            device_id=self.peers()[3], device_id_type=MESH,
        )

    def add(self, here, other):
        here[...] = (here[...].astype(jnp.float32) + other.astype(jnp.float32)).astype(jnp.bfloat16)

    def start(self, k):
        @pl.when(k >= SLOTS)
        def _():
            pl.semaphore_wait(self.free, 1)

        self.core_copy(k).start()

    def after_core(self, k):
        self.core_copy(k).wait_recv()
        for far in (1, 0):
            half = (self.y + far) % 2

            @pl.loop(0, self.depth)
            def _(to):
                self.add(self.block(k, self.core, half, to), self.from_core[k % SLOTS, rows_of(half * self.depth + to)])

            if far:

                @pl.when(jnp.logical_not(self.is_early(k)))
                def _():
                    self.y_copy(k).start()

        @pl.when(k + SLOTS < self.count)
        def _():
            pl.semaphore_signal(self.free, inc=1, device_id=self.peers()[0], device_id_type=MESH)

    def after_y(self, p):
        k, _ = self.of_pass(p)
        self.y_copy(k).wait_recv()

        @pl.loop(0, self.depth)
        def _(to):
            self.add(self.block(k, self.core, self.y, to), self.from_y[rows_of(self.slot(k) * self.depth + to)])

    def go_up(self, p):
        for to in range(self.depth - 1, 0, -1):

            @pl.when(self.z < to)
            def _():
                copy = self.up_copy(p, to)

                @pl.when(self.z > 0)
                def _():
                    copy.wait_recv()
                    self.add(self.pass_block(p, to), self.from_low[p, rows_of(to - 1)])

                copy.start()

    def go_down(self, p):
        for to in range(self.depth - 1):

            @pl.when(self.z > to)
            def _():
                copy = self.down_copy(p, to)

                @pl.when(self.z < self.depth - 1)
                def _():
                    copy.wait_recv()
                    self.add(self.pass_block(p, to), self.from_high[p, rows_of(to)])

                copy.start()

    def finish(self, p):
        k, _ = self.of_pass(p)
        own, total = self.pass_block(p, self.z), self.total.at[rows_of(k)]
        total[...] = own[...].astype(jnp.float32)

        @pl.when(self.z > 0)
        def _():
            self.up_copy(p, self.z).wait_recv()
            total[...] += self.from_low[p, rows_of(jnp.maximum(self.z - 1, 0))].astype(jnp.float32)

        @pl.when(self.z < self.depth - 1)
        def _():
            self.down_copy(p, self.z).wait_recv()
            total[...] += self.from_high[p, rows_of(jnp.minimum(self.z, self.depth - 2))].astype(jnp.float32)

        if self.early:

            @pl.when((p < 2 * self.early) & (p % 2 == 0))
            def _():
                own[...] = total[...].astype(jnp.bfloat16)
                self.last_copy(k).start()

    def after_last(self, k):
        self.last_copy(k).wait_recv()
        self.total[rows_of(k), :] += self.from_y[self.last_rows(k)].astype(jnp.float32)

    def drain(self, k):
        self.core_copy(k).wait_send()
        if self.early:
            pl.when(self.is_early(k))(lambda: self.last_copy(k).wait_send())
        pl.when(jnp.logical_not(self.is_early(k)))(lambda: self.y_copy(k).wait_send())

    def drain_pass(self, p):
        for to in range(self.depth - 1):

            @pl.when(self.z < to + 1)
            def _():
                self.up_copy(p, to + 1).wait_send()

            @pl.when(self.z > to)
            def _():
                self.down_copy(p, to).wait_send()

    def direct_copy(self, p, to):
        return pltpu.make_async_remote_copy(
            self.pass_block(p, to), self.from_low.at[p, rows_of(self.z - (self.z > to).astype(jnp.int32))],
            self.up_s.at[p, to], self.up_r.at[p, self.z],
            device_id=self.device(to, self.y, self.core), device_id_type=MESH,
        )

    def go_direct(self, p):
        for distance in range(self.depth - 1, 0, -1):
            pl.when(self.z + distance < self.depth)(lambda: self.direct_copy(p, self.z + distance).start())
            pl.when(self.z >= distance)(lambda: self.direct_copy(p, self.z - distance).start())

    def finish_direct(self, p):
        k, _ = self.of_pass(p)
        total = self.total.at[rows_of(k)]
        total[...] = self.pass_block(p, self.z)[...].astype(jnp.float32)

        @pl.loop(0, self.depth - 1)
        def _(i):
            source = i + (i >= self.z).astype(jnp.int32)
            arrived = self.from_low.at[p, rows_of(i)]
            pltpu.make_async_remote_copy(
                arrived, arrived, self.up_s.at[p, source], self.up_r.at[p, source],
                device_id=self.device(source, self.y, self.core), device_id_type=MESH,
            ).wait_recv()
            total[...] += arrived[...].astype(jnp.float32)

    def drain_direct(self, p):
        for to in range(self.depth):
            pl.when(self.z != to)(lambda: self.direct_copy(p, to).wait_send())

    def along(self, t, ahead):
        last, soon, chained = self.depth - 1, 2 * self.early, self.passes - 1
        for far, action in ((self.z, self.go_up), (last - self.z, self.go_down)) if chained else ():
            pl.when(far > 0)(lambda far=far, action=action: at(t - far, 0, chained, action))

        ends = ((self.z == 0, self.go_up), (self.z == last, self.go_down))
        for end, action in ends:
            if self.early:
                pl.when(end)(lambda action=action: at(t + ahead, 0, soon, action))
        at(t, soon, self.passes, self.after_y)
        for end, action in ends:
            if chained:
                pl.when(end)(lambda action=action: at(t, soon, chained, action))
        at(t, chained, self.passes, self.go_direct)


def at(k, low, high, action):
    @pl.when((k >= low) & (k < high))
    def _():
        action(k)


def over(count, size):
    def run(action):
        @pl.loop(0, count // size)
        def _(i):
            action(pl.ds(pl.multiple_of(i * size, size), size))

    return run


def train_kernel(
    depth, images,
    patches, signs, tiles, valid, cotangent, attend_in, project_in, expand_in, shrink_in, first, second, bottle_in,
    results, total, rest,
    parts, attend, project, left, right, soft, temp, saved, normed_one, normed_two, residual, factor_one,
    factor_two, average_two, bias, codes, bottle, delta, code_grad, bottle_sum, gain_one, gain_two, extra,
    loads, code_sems, *scratch,
):
    rows, width = patches.shape
    length = rows // images
    work = total.at[:rows]
    count, slabs = parts.shape[0], shrink_in.shape[0] // width
    pairs = width // 128
    main = Reduction(depth, EARLY, parts, total, scratch[:13])
    small = Reduction(depth, 0, extra, rest, scratch[13:26])
    encoding = main.section == 0
    lane = lax.broadcasted_iota(jnp.int32, (length, 128), 1)
    low_half = lane < HD
    bf, f32 = jnp.bfloat16, jnp.float32

    def dot(a, b):
        return jnp.dot(a, b, preferred_element_type=f32)

    def load(source, target, i):
        return pltpu.make_async_copy(source, target, loads.at[i])

    main.greet()
    fetch = [load(patches, right.at[5], 0)]
    fetch += [load(attend_in.at[:, pl.ds(j * width, width)], attend.at[j], 1 + j) for j in range(3)]
    for copy in fetch:
        copy.start()
    fetch += [load(project_in, project, 4)]
    fetch += [load(expand_in.at[:, pl.ds(j * width, width)], parts.at[2 * slabs + j], 5 + j) for j in range(slabs)]
    fetch += [load(shrink_in.at[pl.ds(j * width, width)], parts.at[slabs + j], 5 + slabs + j) for j in range(slabs)]
    fetch += [load(cotangent, right.at[0], 5 + 2 * slabs)]

    for i in range(images):
        row = jnp.broadcast_to(tiles[i : i + 1, :].astype(f32), (length, length))
        live = jnp.broadcast_to(valid[i : i + 1, :], (length, length)) == 1
        spot = lax.broadcasted_iota(jnp.int32, (length, length), 0) == lax.broadcasted_iota(
            jnp.int32, (length, length), 1
        )
        bias[i] = jnp.where(((row == row.T) & live) | spot, 0.0, -1000000000.0)
    code_width = signs.shape[0]
    work[:256, :] = jnp.zeros((256, width), f32)
    work[:code_width, :rows] = (2 * signs[...] - 1).astype(f32) / math.sqrt(code_width)
    work[128 : 128 + code_width, :] = bottle_in[...].astype(f32)
    codes[...] = work[:128, :rows].T.astype(bf)
    bottle[...] = work[128:256, :].T.astype(bf)
    gain_one[...] = jnp.zeros_like(gain_one)
    gain_two[...] = jnp.zeros_like(gain_two)
    fetch[0].wait()

    @pl.when(encoding)
    def _():
        residual[...] = right[5].astype(f32)

    @pl.when(jnp.logical_not(encoding))
    def _():
        residual[...] = times_transpose(codes[...], bottle[...])

    def norm(gain, normed, factor, average=None):
        values = residual[...]
        middle = jnp.mean(values, axis=-1, keepdims=True)
        if average is not None:
            average[...] = middle
        center = values - middle
        scale = lax.rsqrt(jnp.mean(center * center, axis=-1, keepdims=True) + 1e-06)
        unscaled = center * scale
        normed[...] = unscaled
        factor[...] = scale
        temp[...] = (unscaled * gain[...]).astype(bf)

    def keep_transpose(source, target):
        half = 8 * ROWS
        for i in range(width // half):
            turned = source[:, i * half : (i + 1) * half].T
            for j in range(8):
                z, y, core = i * 2 + j // 4, (j // 2) % 2, j % 2
                target[place(z, y, core, depth) * ROWS : (place(z, y, core, depth) + 1) * ROWS, :] = turned[
                    j * ROWS : (j + 1) * ROWS
                ]

    norm(first, normed_one, factor_one)
    for j in range(3):
        fetch[1 + j].wait()
        if j == 2:
            for copy in fetch[4:]:
                copy.start()
        right[6 + j] = dot(temp[...], attend[j]).astype(bf)

    keep_transpose(temp, left.at[slabs + 2])

    group = 3
    heads = [(pair, head) for pair in range(group) for head in range(2)]

    def group_of(turn):
        image = turn * group // pairs
        start = turn * group - image * pairs
        lanes = [pl.ds(pl.multiple_of((start + pair) * 128, 128), 128) for pair in range(group)]
        return pl.ds(pl.multiple_of(image * length, length), length), lanes, image

    def masked(values, low, scale=1.0):
        return jnp.where(low_half if low else jnp.logical_not(low_half), values * scale, 0.0).astype(bf)

    def merged(members, pair):
        return jnp.where(low_half, members[2 * pair], members[2 * pair + 1])

    @pl.loop(0, images * pairs // group)
    def _(turn):
        r, lanes, image = group_of(turn)
        query, key, value = ([right[6 + j, r, c] for c in lanes] for j in range(3))
        scores = [
            times_transpose(masked(query[pair], head == 0, HD**-0.5), key[pair]) + bias[image] for pair, head in heads
        ]
        raised = [jnp.exp(member - jnp.max(member, axis=-1, keepdims=True)) for member in scores]
        weights = [(member * (1.0 / jnp.sum(member, axis=-1, keepdims=True))).astype(bf) for member in raised]
        for (pair, head), member in zip(heads, weights):
            soft[turn * group + pair, head * length : (head + 1) * length, :] = member
        mixed = [dot(member, value[pair]) for (pair, head), member in zip(heads, weights)]
        for pair, c in enumerate(lanes):
            temp[r, c] = merged(mixed, pair).astype(bf)

    fetch[4].wait()

    residual[...] += dot(temp[...], project[...])

    keep_transpose(temp, left.at[slabs + 1])
    norm(second, normed_two, factor_two, average_two)
    keep_transpose(temp, left.at[slabs])

    for j in range(slabs):
        fetch[5 + j].wait()

        hidden = dot(temp[...], parts[2 * slabs + j])
        share = 0.5 + 0.5 * lax.erf(hidden * math.sqrt(0.5))
        slope = share + hidden * jnp.exp(-0.5 * hidden * hidden) * (1.0 / math.sqrt(2.0 * math.pi))
        parts[j, :rows, :] = (hidden * share).astype(bf)
        right[1 + j] = slope.astype(bf)

    for copy in fetch[5 + slabs :]:
        copy.wait()
    out_copy = pltpu.make_async_copy(saved, results, loads.at[6 + 2 * slabs])
    across = pltpu.make_async_remote_copy(
        delta, code_grad, code_sems.at[0], code_sems.at[1], device_id=main.peers()[4], device_id_type=MESH
    )
    main.meet()

    @pl.when(jnp.logical_not(encoding))
    def _():
        residual[...] = right[0].astype(f32)

    def block_output():
        output = normed_two[...] * (1.0 / factor_two[...]) + average_two[...]
        for j in range(slabs):
            output += dot(parts[j, :rows, :], parts[slabs + j])
        saved[...] = output.astype(bf)
        pl.when(jnp.logical_not(encoding))(out_copy.start)
        for i in range(2 * slabs):
            z, y = i // 2, i % 2
            turned = parts[i // 2, :rows, (i % 2) * 8 * ROWS : (i % 2 + 1) * 8 * ROWS].T
            for core in range(2):
                for j in range(slabs):
                    spot, start = place(z, y, core, depth) * ROWS, (core * 4 + j) * ROWS
                    left[j, spot : spot + ROWS, :] = turned[start : start + ROWS]

    def from_codes():
        latent = dot(saved[...], bottle[...])
        scale = lax.rsqrt(jnp.sum(latent * latent, axis=-1, keepdims=True) + 1e-06)
        unit_code = latent * scale
        work[:128, :rows] = jnp.zeros((128, rows), f32)
        across.wait_recv()
        work[: delta.shape[0], :rows] = code_grad[...].astype(f32)
        grad_unit = work[:128, :rows].T
        grad_latent = (
            scale * (grad_unit - unit_code * jnp.sum(unit_code * grad_unit, axis=-1, keepdims=True))
        ).astype(bf)
        grad_out = times_transpose(grad_latent, bottle[...])
        right[0] = grad_out.astype(bf)
        residual[...] = grad_out
        bottle_sum[...] = contract_rows(saved[...], grad_latent)

    def piece(k):
        a = jnp.minimum(k, slabs) + (k >= 2 * slabs).astype(jnp.int32) + (k > 2 * slabs).astype(jnp.int32)
        b = jnp.maximum(k - slabs + 1, 0)

        parts[k] = dot(left[a], right[b]).astype(bf)
        main.start(k)

    def norm_back(gain, normed, factor, gain_sum, low):
        @over(rows, length)
        def _(r):
            given, unscaled = work[r, :], normed[r, :]
            gain_sum[...] += jnp.sum((given * unscaled).reshape(-1, 8, width), axis=0)
            grad = given * gain[...]
            inner = jnp.mean(grad * unscaled, axis=-1, keepdims=True)
            grad = residual[r, :] + factor[r, :] * (grad - jnp.mean(grad, axis=-1, keepdims=True) - unscaled * inner)
            residual[r, :] = grad
            low[r, :] = grad.astype(bf)

    def through_shrink():
        for j in range(slabs):
            grad = times_transpose(right[0], parts[slabs + j])
            right[1 + j] = (grad * right[1 + j].astype(f32)).astype(bf)

    def through_expand():
        grad = times_transpose(right[1], parts[2 * slabs])
        for j in range(1, slabs):
            grad += times_transpose(right[1 + j], parts[2 * slabs + j])
        work[...] = grad

    def through_project():
        norm_back(second, normed_two, factor_two, gain_two, right.at[5])

        temp[...] = times_transpose(right[5], project[...]).astype(bf)

    def through_heads(low, high):
        @pl.loop(low, high)
        def _(turn):
            r, lanes, image = group_of(turn)
            query, key, value = ([right[6 + j, r, c] for c in lanes] for j in range(3))
            weights = [soft[turn * group + pair, head * length : (head + 1) * length, :] for pair, head in heads]
            grad_heads = [masked(temp[r, lanes[pair]], head == 0) for pair, head in heads]
            grad_soft = [times_transpose(member, value[pair]) for (pair, head), member in zip(heads, grad_heads)]
            grad_scores = []
            for low, member in zip(weights, grad_soft):
                exact = low.astype(f32)
                inner = jnp.sum(exact * member, axis=-1, keepdims=True)
                grad_scores.append((exact * (member - inner)).astype(bf))
            to_query = [dot(member, key[pair]) for (pair, head), member in zip(heads, grad_scores)]
            to_key = [
                contract_rows(member, masked(query[pair], head == 0, HD**-0.5))
                for (pair, head), member in zip(heads, grad_scores)
            ]
            to_value = [contract_rows(low, member) for low, member in zip(weights, grad_heads)]
            for pair, c in enumerate(lanes):
                right[6, r, c] = (merged(to_query, pair) * HD**-0.5).astype(bf)
                right[7, r, c] = (to_key[2 * pair] + to_key[2 * pair + 1]).astype(bf)
                right[8, r, c] = (to_value[2 * pair] + to_value[2 * pair + 1]).astype(bf)

    def through_attend():
        grad = times_transpose(right[6], attend[0])
        for j in range(1, 3):
            grad += times_transpose(right[6 + j], attend[j])
        work[...] = grad
        norm_back(first, normed_one, factor_one, gain_one, saved)

        @pl.when(jnp.logical_not(encoding))
        def _():
            turned = lax.dot_general(bottle[...], saved[...], (((0,), (1,)), ((), ())), preferred_element_type=f32)
            delta[...] = turned[: delta.shape[0]].astype(bf)
            across.start()
            bottle_sum[...] = contract_rows(saved[...], codes[...])

        @pl.when(encoding)
        def _():
            out_copy.start()

        spare = lax.broadcasted_iota(jnp.int32, (width, 128), 1)
        column_one = jnp.sum(gain_one[...].T, axis=1, keepdims=True)
        column_two = jnp.sum(gain_two[...].T, axis=1, keepdims=True)
        gathered = jnp.where(
            spare == code_width, column_one, jnp.where(spare == code_width + 1, column_two, bottle_sum[...])
        ).astype(bf)
        for i in range(4 * depth):
            spot = place(i // 4, (i // 2) % 2, i % 2, depth)
            extra[0, spot * ROWS : (spot + 1) * ROWS, :] = gathered[i * ROWS : (i + 1) * ROWS]
        small.start(0)

    turns = images * pairs // group
    links, within, last = 6, slabs, depth - 1

    @pl.loop(0, links + main.passes + slabs + 6)
    def _(step):
        k = step - links * main.section
        link = step - within * (1 - main.section)
        pl.when(k == 0)(block_output)
        pl.when((k == 0) & encoding)(from_codes)
        at(k - (k > slabs).astype(jnp.int32), 0, jnp.where(k == slabs, 0, count), piece)
        at(k - 2, 0, count, main.after_core)
        at(k - slabs - 6, 0, 1, small.after_core)
        main.along(k - 5, 2)
        small.along(k - slabs - 12, 0)
        at(k - 10, 0, main.passes - 1, main.finish)
        at(k - 10, main.passes - 1, main.passes, main.finish_direct)
        at(k - slabs - 16, 0, 1, small.finish_direct)
        at(k - 15, 1, 1 + EARLY, main.after_last)
        pl.when(link == 0)(through_shrink)
        pl.when(link == 1)(through_expand)
        pl.when(link == 2)(through_project)
        pl.when((link == 3) | (link == 4))(lambda: through_heads((link - 3) * turns // 2, (link - 2) * turns // 2))
        pl.when(link == 5)(through_attend)

    out_copy.wait()

    @pl.when(jnp.logical_not(encoding))
    def _():
        across.wait_send()

    small.drain(0)
    small.drain_direct(0)
    main.drain_direct(main.passes - 1)

    @pl.loop(0, count)
    def _(k):
        main.drain(k)

    @pl.loop(0, main.passes - 1)
    def _(p):
        main.drain_pass(p)


def train(depth, images, arrays):
    patches, signs, _, _, _, attend, project, expand, shrink, _, _, bottle = arrays
    rows, width = patches.shape
    slabs = shrink.shape[0] // width
    count = 2 * slabs + 4
    pairs, length = width // 128, rows // images
    code_rows = -(-signs.shape[0] // 16) * 16
    hbm, vmem = pl.BlockSpec(memory_space=pl.ANY), pl.BlockSpec(memory_space=pltpu.VMEM)
    low, full = lambda *shape: pltpu.VMEM(shape, jnp.bfloat16), lambda *shape: pltpu.VMEM(shape, jnp.float32)
    return pl.pallas_call(
        functools.partial(train_kernel, depth, images),
        out_shape=(
            jax.ShapeDtypeStruct((rows, width), jnp.bfloat16),
            jax.ShapeDtypeStruct((count * ROWS, width), jnp.float32),
            jax.ShapeDtypeStruct((ROWS, 128), jnp.float32),
        ),
        in_specs=[hbm, vmem, vmem, vmem, hbm, hbm, hbm, hbm, hbm, vmem, vmem, vmem],
        out_specs=[hbm, vmem, vmem],
        scratch_shapes=[
            low(count, width, width),
            low(3, width, width),
            low(width, width),
            low(slabs + 3, width, rows),
            low(slabs + 5, rows, width),
            low(images * pairs, 2 * length, length),
            low(rows, width),
            low(rows, width),
            full(rows, width),
            full(rows, width),
            full(rows, width),
            full(rows, 1),
            full(rows, 1),
            full(rows, 1),
            full(images, length, length),
            low(rows, 128),
            low(width, 128),
            low(code_rows, rows),
            low(code_rows, rows),
            full(width, 128),
            full(8, width),
            full(8, width),
            low(1, width, 128),
            pltpu.SemaphoreType.DMA((7 + 2 * slabs,)),
            pltpu.SemaphoreType.DMA((2,)),
        ]
        + Reduction.scratch(depth, EARLY, count, width)
        + Reduction.scratch(depth, 0, 1, 128),
        compiler_params=pltpu.CompilerParams(collective_id=0, has_side_effects=True, vmem_limit_bytes=63 << 20),
        name="train",
    )(*arrays)


def deliver_kernel(slabs, code, raw, total, rest, results, attend, project, expand, shrink, first, second, bottle):
    width = total.shape[1]
    results[...] = raw[...]
    for j in range(slabs):
        shrink[j * ROWS : (j + 1) * ROWS, :] = total[j * ROWS : (j + 1) * ROWS, :]
        expand[:, j * width : (j + 1) * width] = total[(slabs + j) * ROWS : (slabs + j + 1) * ROWS, :]
    project[...] = total[2 * slabs * ROWS : (2 * slabs + 1) * ROWS, :]
    for j in range(3):
        start = (2 * slabs + 1 + j) * ROWS
        attend[:, j * width : (j + 1) * width] = total[start : start + ROWS, :]
    turned = rest[...].T
    first[...] = turned[code : code + 1]
    second[...] = turned[code + 1 : code + 2]
    for i in range(code):
        bottle[i] = turned[i : i + 1]


def deliver(raw, total, rest, slabs, code):
    width = total.shape[1]
    vmem = pl.BlockSpec(memory_space=pltpu.VMEM)
    full = lambda *shape: jax.ShapeDtypeStruct(shape, jnp.float32)
    return pl.pallas_call(
        functools.partial(deliver_kernel, slabs, code),
        out_shape=(
            jax.ShapeDtypeStruct(raw.shape, raw.dtype),
            full(ROWS, 3 * width),
            full(ROWS, width),
            full(ROWS, slabs * width),
            full(slabs * ROWS, width),
            full(1, ROWS),
            full(1, ROWS),
            full(code, 1, ROWS),
        ),
        in_specs=[vmem] * 3,
        out_specs=[vmem] * 8,
        name="deliver",
    )(raw, total, rest)


def two_images(*arrays):
    images = arrays[2].shape[0]
    code = arrays[1].shape[1]
    slabs = arrays[8].shape[1] // arrays[0].shape[1]
    weights = tuple(member[0] for member in arrays[5:9])
    arrays = (arrays[0], arrays[1].T) + arrays[2:5] + weights + arrays[9:11] + (arrays[11][0].T,)
    raw, total, rest = train(lax.axis_size("batch") // 4, images, arrays)
    results, attend, project, expand, shrink, first, second, bottle = deliver(raw, total, rest, slabs, code)
    return (
        results[None], attend[None], project[None], expand[None], shrink[None], first, second, bottle.transpose(1, 2, 0)
    )


def pick_index(stacked, chosen):
    return lax.dynamic_index_in_dim(stacked, chosen, 0, keepdims=False)


def body(
    patches,
    code_signs,
    tile_ids,
    patch_valid,
    cotangent,
    attend_weight,
    project_weight,
    expand_weight,
    shrink_weight,
    norm_first,
    norm_second,
    bottleneck,
):
    micro_count = tile_ids.shape[0]
    length = tile_ids.shape[1]
    code_width = code_signs.shape[1]
    encoding = lax.axis_index("section") == 0
    encoding_int = encoding.astype(jnp.int32)
    weights = (
        attend_weight[0],
        project_weight[0],
        expand_weight[0],
        shrink_weight[0],
        norm_first[0],
        norm_second[0],
    )
    bottle = bottleneck[0]
    code_values = ((2 * code_signs - 1).astype(jnp.float32) / math.sqrt(code_width)).astype(
        jnp.bfloat16
    )
    block_inputs = []
    outputs_low = []
    unit_codes = []
    unit_factors = []
    decoded_list = []
    kept_list = []
    for turn_index in range(micro_count):
        image_rows = patches[turn_index * length : (turn_index + 1) * length].astype(jnp.float32)
        decoder_in = times_transpose(
            code_values[turn_index * length : (turn_index + 1) * length], bottle
        )
        block_in = jnp.where(encoding, image_rows, decoder_in)
        allowed_keys = allowed(tile_ids[turn_index], patch_valid[turn_index])
        output, kept_parts = block_forward(block_in, weights, allowed_keys)
        output_low = output.astype(jnp.bfloat16)
        latent = jnp.dot(output_low, bottle, preferred_element_type=jnp.float32)
        factor = lax.rsqrt(jnp.sum(latent * latent, axis=-1, keepdims=True) + 1e-06)
        block_inputs.append(block_in)
        outputs_low.append(output_low)
        unit_codes.append(latent * factor)
        unit_factors.append(factor)
        decoded_list.append(output_low)
        kept_list.append(kept_parts)
    block_inputs = jnp.stack(block_inputs)
    outputs_low = jnp.stack(outputs_low)
    unit_codes = jnp.stack(unit_codes)
    unit_factors = jnp.stack(unit_factors)
    kept_stack = jax.tree.map(lambda *members: jnp.stack(members), *kept_list)
    totals = None
    sent_grad = jnp.zeros((length, code_width), jnp.bfloat16)
    input_grads = []
    for turn_index in range(micro_count + 1):
        if turn_index > 0:
            received = passed_along(sent_grad, "section", -1)
        else:
            received = jnp.zeros_like(sent_grad)
        chosen = jnp.clip(turn_index - encoding_int, 0, micro_count - 1)
        turn_flag = jnp.where(encoding, turn_index >= 1, turn_index < micro_count).astype(
            jnp.float32
        )
        kept_parts = jax.tree.map(lambda stacked: pick_index(stacked, chosen), kept_stack)
        unit_code = pick_index(unit_codes, chosen)
        factor = pick_index(unit_factors, chosen)
        output_low = pick_index(outputs_low, chosen)
        grad_unit = received.astype(jnp.float32)
        grad_latent = (
            factor
            * (grad_unit - unit_code * jnp.sum(unit_code * grad_unit, axis=-1, keepdims=True))
        ).astype(jnp.bfloat16)
        grad_encoded = times_transpose(grad_latent, bottle)
        bottle_encoder = contract_rows(output_low, grad_latent)
        given_grad = lax.dynamic_slice_in_dim(cotangent, chosen * length, length, 0).astype(
            jnp.float32
        )
        grad_out = jnp.where(encoding, grad_encoded, given_grad)
        grad_in, grads = block_backward(kept_parts, grad_out, weights)
        grad_in_low = grad_in.astype(jnp.bfloat16)
        code_rows = lax.dynamic_slice_in_dim(code_values, chosen * length, length, 0)
        bottle_decoder = contract_rows(grad_in_low, code_rows)
        sent_grad = jnp.dot(grad_in_low, bottle, preferred_element_type=jnp.float32).astype(
            jnp.bfloat16
        )
        grads = grads + (jnp.where(encoding, bottle_encoder, bottle_decoder),)
        grads = tuple((turn_flag * member for member in grads))
        if turn_index > 0:
            input_grads.append(grad_in_low)
        totals = (
            grads
            if totals is None
            else tuple((former + latter for former, latter in zip(totals, grads)))
        )
    totals = lax.psum_scatter(totals, "batch", scatter_dimension=0, tiled=True)
    pieces = [
        jnp.where(encoding, input_grads[turn_index], decoded_list[turn_index])
        for turn_index in range(micro_count)
    ]
    results = jnp.concatenate(pieces, axis=0)[None]
    return (
        results,
        totals[0][None],
        totals[1][None],
        totals[2][None],
        totals[3][None],
        totals[4][None],
        totals[5][None],
        totals[6][None],
    )


def solution(mesh):
    batch = mesh.shape["batch"]
    return jax.shard_map(
        two_images if batch == 16 else body,
        mesh=mesh,
        in_specs=(
            P("batch", None),
            P("batch", None),
            P("batch", None),
            P("batch", None),
            P("batch", None),
            P("section", None, None),
            P("section", None, None),
            P("section", None, None),
            P("section", None, None),
            P("section", None),
            P("section", None),
            P("section", None, None),
        ),
        out_specs=(
            P("section", "batch", None),
            P("section", "batch", None),
            P("section", "batch", None),
            P("section", "batch", None),
            P("section", "batch", None),
            P("section", "batch"),
            P("section", "batch"),
            P("section", "batch", None),
        ),
        check_vma=False,
    )
```

```python
import functools
import math

import jax
import jax.numpy as jnp
from jax import lax
from jax.experimental import pallas as pl
from jax.experimental.pallas import tpu as pltpu
from jax.sharding import PartitionSpec as P

H = 12
HD = 64
MESH = pl.DeviceIdType.MESH
ROWS = 48
SLOTS = 4
EARLY = 1
MOST = 9
PACK = 32
STRIDE = 24
CUTS = 3
STRAIGHT = 1
LATE = 1
SMALL = -2
GAP = 3


def passed_along(block, axis, distance):
    devices = range(lax.axis_size(axis))
    route = [(i - distance, i) for i in devices if i - distance in devices]
    return lax.ppermute(block, axis, route)


def contract_rows(former, latter):
    return lax.dot_general(
        former, latter, (((0,), (0,)), ((), ())), preferred_element_type=jnp.float32
    )


def times_transpose(former, latter):
    return lax.dot_general(
        former, latter, (((1,), (1,)), ((), ())), preferred_element_type=jnp.float32
    )


def normalize(values):
    average = jnp.mean(values, axis=-1, keepdims=True)
    center = values - average
    spread = jnp.mean(center * center, axis=-1, keepdims=True)
    factor = lax.rsqrt(spread + 1e-06)
    return (center * factor, factor)


def norm_back(grad_normed, normed, factor):
    return factor * (
        grad_normed
        - jnp.mean(grad_normed, axis=-1, keepdims=True)
        - normed * jnp.mean(grad_normed * normed, axis=-1, keepdims=True)
    )


def allowed(tile_row, keep_row):
    places = jnp.arange(tile_row.shape[0])
    same_tile = tile_row[:, None] == tile_row[None, :]
    live_keys = keep_row[None, :] == 1
    return same_tile & live_keys | (places[:, None] == places[None, :])


def block_forward(residual, weights, allowed_keys):
    attend, project, expand, shrink, first, second = weights
    length, model_width = residual.shape
    normed_one, factor_one = normalize(residual)
    input_one = (normed_one * first).astype(jnp.bfloat16)
    joint_proj = jnp.dot(input_one, attend, preferred_element_type=jnp.float32).astype(jnp.bfloat16)
    split_parts = joint_proj.reshape(length, 3, H, HD)
    queries = split_parts[:, 0]
    key_rows = split_parts[:, 1]
    value_rows = split_parts[:, 2]
    scores = jnp.einsum(
        "qhd,khd->hqk", queries, key_rows, preferred_element_type=jnp.float32
    ) * HD ** (-0.5)
    scores = jnp.where(allowed_keys[None], scores, -1000000000.0)
    maximum = jnp.max(scores, axis=-1, keepdims=True)
    raised = jnp.exp(scores - maximum)
    softmax_out = raised / jnp.sum(raised, axis=-1, keepdims=True)
    softmax_low = softmax_out.astype(jnp.bfloat16)
    mixed_heads = jnp.einsum(
        "hqk,khd->qhd", softmax_low, value_rows, preferred_element_type=jnp.float32
    )
    mixed_heads = mixed_heads.reshape(length, model_width).astype(jnp.bfloat16)
    middle = residual + jnp.dot(mixed_heads, project, preferred_element_type=jnp.float32)
    normed_two, factor_two = normalize(middle)
    input_two = (normed_two * second).astype(jnp.bfloat16)
    hidden = jnp.dot(input_two, expand, preferred_element_type=jnp.float32)
    active = jax.nn.gelu(hidden, approximate=False).astype(jnp.bfloat16)
    output = middle + jnp.dot(active, shrink, preferred_element_type=jnp.float32)
    kept_parts = (
        normed_one,
        factor_one,
        input_one,
        queries,
        key_rows,
        value_rows,
        softmax_out,
        softmax_low,
        mixed_heads,
        normed_two,
        factor_two,
        input_two,
        hidden,
        active,
    )
    return (output, kept_parts)


def block_backward(kept_parts, grad_out, weights):
    attend, project, expand, shrink, first, second = weights
    (
        normed_one,
        factor_one,
        input_one,
        queries,
        key_rows,
        value_rows,
        softmax_out,
        softmax_low,
        mixed_heads,
        normed_two,
        factor_two,
        input_two,
        hidden,
        active,
    ) = kept_parts
    length, model_width = grad_out.shape
    grad_rounded = grad_out.astype(jnp.bfloat16)
    grad_shrink = contract_rows(active, grad_rounded)
    grad_active = times_transpose(grad_rounded, shrink)
    _, gelu_back = jax.vjp(lambda values: jax.nn.gelu(values, approximate=False), hidden)
    grad_hidden = gelu_back(grad_active)[0].astype(jnp.bfloat16)
    grad_expand = contract_rows(input_two, grad_hidden)
    grad_input_two = times_transpose(grad_hidden, expand)
    grad_second = jnp.sum(grad_input_two * normed_two, axis=0)
    grad_middle = grad_out + norm_back(grad_input_two * second, normed_two, factor_two)
    middle_low = grad_middle.astype(jnp.bfloat16)
    grad_project = contract_rows(mixed_heads, middle_low)
    grad_mixed = times_transpose(middle_low, project).astype(jnp.bfloat16).reshape(length, H, HD)
    grad_soft = jnp.einsum(
        "qhd,khd->hqk", grad_mixed, value_rows, preferred_element_type=jnp.float32
    )
    grad_values = jnp.einsum(
        "hqk,qhd->khd", softmax_low, grad_mixed, preferred_element_type=jnp.float32
    )
    inner_sum = jnp.sum(softmax_out * grad_soft, axis=-1, keepdims=True)
    grad_scores = (softmax_out * (grad_soft - inner_sum)).astype(jnp.bfloat16)
    score_scale = HD ** (-0.5)
    grad_queries = (
        jnp.einsum("hqk,khd->qhd", grad_scores, key_rows, preferred_element_type=jnp.float32)
        * score_scale
    )
    grad_keys = (
        jnp.einsum("hqk,qhd->khd", grad_scores, queries, preferred_element_type=jnp.float32)
        * score_scale
    )
    grad_joint = (
        jnp.stack([grad_queries, grad_keys, grad_values], axis=1)
        .reshape(length, 3 * model_width)
        .astype(jnp.bfloat16)
    )
    grad_attend = contract_rows(input_one, grad_joint)
    grad_input_one = times_transpose(grad_joint, attend)
    grad_first = jnp.sum(grad_input_one * normed_one, axis=0)
    grad_residual = grad_middle + norm_back(grad_input_one * first, normed_one, factor_one)
    return (
        grad_residual,
        (grad_attend, grad_project, grad_expand, grad_shrink, grad_first, grad_second),
    )


def rows_of(index):
    return pl.ds(pl.multiple_of(index * ROWS, ROWS), ROWS)


def place(z, y, core, depth):
    return (core * 2 + y) * depth + z


class Reduction:
    def __init__(self, depth, early, straight, cuts, count, spot, parts, total, scratch):
        self.depth, self.early, self.cuts = depth, early, cuts
        self.count, self.passes, self.spot = count, count + early, spot
        self.chained, self.hops = self.passes - straight, early > 0
        self.parts, self.total = parts, total
        self.from_core, self.from_y, self.from_low, self.from_high = scratch[:4]
        self.core_s, self.core_r, self.y_s, self.y_r = scratch[4:8]
        self.up_s, self.up_r, self.down_s, self.down_r, self.free = scratch[8:13]
        self.cut_y_s, self.cut_y_r, self.cut_s, self.cut_r = scratch[13:17]
        self.section = lax.axis_index("section")
        self.me = lax.axis_index("batch")
        self.z, self.y, self.core = self.me // 4, (self.me // 2) % 2, self.me % 2

    def scratch(depth, early, cuts, count, wide):
        low, dma = lambda *shape: pltpu.VMEM(shape, jnp.bfloat16), pltpu.SemaphoreType.DMA
        return [
            low(min(count, SLOTS), 2 * depth * ROWS, wide),
            low((count - early) * depth * ROWS + early * ROWS, wide),
            low(count + early, (depth - 1) * ROWS, wide),
            low(count + early, (depth - 1) * ROWS, wide),
        ] + [dma((count,))] * 4 + [dma((count + early, depth))] * 4 + [
            pltpu.SemaphoreType.REGULAR, dma((cuts,)), dma((cuts,)), dma((cuts, depth)), dma((cuts, depth))
        ]

    def device(self, z, y, core):
        return (self.section, z * 4 + y * 2 + core)

    def peers(self):
        return (
            self.device(self.z, self.y, 1 - self.core),
            self.device(self.z, 1 - self.y, self.core),
            self.device(jnp.minimum(self.z + 1, self.depth - 1), self.y, self.core),
            self.device(jnp.maximum(self.z - 1, 0), self.y, self.core),
            (1 - self.section, self.me),
        )

    def greet(self):
        barrier = pltpu.get_barrier_semaphore()

        def signal(device):
            pl.semaphore_signal(barrier, inc=1, device_id=device, device_id_type=MESH)

        core, other, _, _, across = self.peers()
        for peer in (core, other, across):
            signal(peer)
        for z in range(self.depth):
            pl.when(self.z != z)(lambda z=z: signal(self.device(z, self.y, self.core)))

    def meet(self):
        pl.semaphore_wait(pltpu.get_barrier_semaphore(), self.depth + 2)

    def block(self, k, core, y, z):
        return self.parts.at[self.spot(k), rows_of(place(z, y, core, self.depth))]

    def core_copy(self, k):
        half = 2 * self.depth * ROWS
        return pltpu.make_async_remote_copy(
            self.parts.at[self.spot(k), pl.ds(pl.multiple_of((1 - self.core) * half, half), half)],
            self.from_core.at[k % SLOTS], self.core_s.at[k], self.core_r.at[k],
            device_id=self.peers()[0], device_id_type=MESH,
        )

    def slot(self, k):
        return jnp.maximum(k - self.early, 0)

    def is_early(self, k):
        return (k >= 1) & (k <= self.early)

    def y_copy(self, k):
        quarter = self.depth * ROWS
        start, slot = (self.core * 2 + 1 - self.y) * quarter, self.slot(k) * quarter
        return pltpu.make_async_remote_copy(
            self.parts.at[self.spot(k), pl.ds(pl.multiple_of(start, quarter), quarter)],
            self.from_y.at[pl.ds(pl.multiple_of(slot, quarter), quarter)], self.y_s.at[k], self.y_r.at[k],
            device_id=self.peers()[1], device_id_type=MESH,
        )

    def last_rows(self, k):
        return rows_of((MOST - self.early) * self.depth + k - 1)

    def last_copy(self, k):
        return pltpu.make_async_remote_copy(
            self.block(k, self.core, 1 - self.y, self.z), self.from_y.at[self.last_rows(k)],
            self.y_s.at[k], self.y_r.at[k],
            device_id=self.peers()[1], device_id_type=MESH,
        )

    def of_pass(self, p):
        if not self.early:
            return p, self.y
        soon = p < 2 * self.early
        piece = jnp.where(soon, 1 + p // 2, jnp.where(p == 2 * self.early, 0, p - self.early))
        return piece, jnp.where(soon & (p % 2 == 0), 1 - self.y, self.y)

    def pass_block(self, p, to):
        k, y = self.of_pass(p)
        return self.block(k, self.core, y, to)

    def up_copy(self, p, to):
        return pltpu.make_async_remote_copy(
            self.pass_block(p, to), self.from_low.at[p, rows_of(to - 1)],
            self.up_s.at[p, to], self.up_r.at[p, to],
            device_id=self.peers()[2], device_id_type=MESH,
        )

    def down_copy(self, p, to):
        return pltpu.make_async_remote_copy(
            self.pass_block(p, to), self.from_high.at[p, rows_of(to)],
            self.down_s.at[p, to], self.down_r.at[p, to],
            device_id=self.peers()[3], device_id_type=MESH,
        )

    def add(self, here, other):
        here[...] = (here[...].astype(jnp.float32) + other.astype(jnp.float32)).astype(jnp.bfloat16)

    def start(self, k):
        @pl.when(k >= SLOTS)
        def _():
            pl.semaphore_wait(self.free, 1)

        self.core_copy(k).start()

    def after_core(self, k):
        self.core_copy(k).wait_recv()
        for far in (1, 0):
            half = (self.y + far) % 2

            @pl.loop(0, self.depth)
            def _(to):
                self.add(self.block(k, self.core, half, to), self.from_core[k % SLOTS, rows_of(half * self.depth + to)])

            if far:

                @pl.when(jnp.logical_not(self.is_early(k)) & (k < self.count - 1))
                def _():
                    self.y_copy(k).start()

                @pl.when(k == self.count - 1)
                def _():
                    for cut in range(self.cuts):
                        self.y_cut(cut).start()

        @pl.when(k + SLOTS < self.count)
        def _():
            pl.semaphore_signal(self.free, inc=1, device_id=self.peers()[0], device_id_type=MESH)

    def after_y(self, p):
        k, _ = self.of_pass(p)
        self.y_copy(k).wait_recv()

        @pl.loop(0, self.depth)
        def _(to):
            self.add(self.block(k, self.core, self.y, to), self.from_y[rows_of(self.slot(k) * self.depth + to)])

    def go_up(self, p):
        for to in range(self.depth - 1, 0, -1):

            @pl.when(self.z < to)
            def _():
                copy = self.up_copy(p, to)

                @pl.when(self.z > 0)
                def _():
                    copy.wait_recv()
                    self.add(self.pass_block(p, to), self.from_low[p, rows_of(to - 1)])

                copy.start()

    def go_down(self, p):
        for to in range(self.depth - 1):

            @pl.when(self.z > to)
            def _():
                copy = self.down_copy(p, to)

                @pl.when(self.z < self.depth - 1)
                def _():
                    copy.wait_recv()
                    self.add(self.pass_block(p, to), self.from_high[p, rows_of(to)])

                copy.start()

    def finish(self, p):
        k, _ = self.of_pass(p)
        own, total = self.pass_block(p, self.z), self.total.at[rows_of(k)]
        total[...] = own[...].astype(jnp.float32)

        @pl.when(self.z > 0)
        def _():
            self.up_copy(p, self.z).wait_recv()
            total[...] += self.from_low[p, rows_of(jnp.maximum(self.z - 1, 0))].astype(jnp.float32)

        @pl.when(self.z < self.depth - 1)
        def _():
            self.down_copy(p, self.z).wait_recv()
            total[...] += self.from_high[p, rows_of(jnp.minimum(self.z, self.depth - 2))].astype(jnp.float32)

        if self.early:

            @pl.when((p < 2 * self.early) & (p % 2 == 0))
            def _():
                own[...] = total[...].astype(jnp.bfloat16)

    def start_last(self, k):
        self.last_copy(k).start()

    def after_last(self, k):
        self.last_copy(k).wait_recv()
        self.total[rows_of(k), :] += self.from_y[self.last_rows(k)].astype(jnp.float32)

    def drain(self, k):
        self.core_copy(k).wait_send()
        if self.early:
            pl.when(self.is_early(k))(lambda: self.last_copy(k).wait_send())
        pl.when(jnp.logical_not(self.is_early(k)) & (k < self.count - 1))(lambda: self.y_copy(k).wait_send())

    def drain_pass(self, p):
        for to in range(self.depth - 1):

            @pl.when(self.z < to + 1)
            def _():
                self.up_copy(p, to + 1).wait_send()

            @pl.when(self.z > to)
            def _():
                self.down_copy(p, to).wait_send()

    def straight_copy(self, p, to):
        return pltpu.make_async_remote_copy(
            self.pass_block(p, to), self.from_low.at[p, rows_of(self.z - (self.z > to).astype(jnp.int32))],
            self.up_s.at[p, to], self.up_r.at[p, self.z],
            device_id=self.device(to, self.y, self.core), device_id_type=MESH,
        )

    def go_straight(self, p):
        for distance in range(self.depth - 1, 0, -1):
            pl.when(self.z + distance < self.depth)(lambda: self.straight_copy(p, self.z + distance).start())
            pl.when(self.z >= distance)(lambda: self.straight_copy(p, self.z - distance).start())

    def finish_straight(self, p):
        k, _ = self.of_pass(p)
        total = self.total.at[rows_of(k)]
        total[...] = self.pass_block(p, self.z)[...].astype(jnp.float32)

        @pl.loop(0, self.depth - 1)
        def _(i):
            source = i + (i >= self.z).astype(jnp.int32)
            arrived = self.from_low.at[p, rows_of(i)]
            pltpu.make_async_remote_copy(
                arrived, arrived, self.up_s.at[p, source], self.up_r.at[p, source],
                device_id=self.device(source, self.y, self.core), device_id_type=MESH,
            ).wait_recv()
            total[...] += arrived[...].astype(jnp.float32)

    def drain_straight(self, p):
        for to in range(self.depth):
            pl.when(self.z != to)(lambda: self.straight_copy(p, to).wait_send())

    def columns(self, cut):
        wide = self.parts.shape[2] // self.cuts
        return pl.ds(pl.multiple_of(cut * wide, wide), wide)

    def y_cut(self, cut):
        quarter, columns = self.depth * ROWS, self.columns(cut)
        start, slot = (self.core * 2 + 1 - self.y) * quarter, (self.count - 1 - self.early) * quarter
        return pltpu.make_async_remote_copy(
            self.parts.at[self.spot(self.count - 1), pl.ds(pl.multiple_of(start, quarter), quarter), columns],
            self.from_y.at[pl.ds(pl.multiple_of(slot, quarter), quarter), columns], self.cut_y_s.at[cut], self.cut_y_r.at[cut],
            device_id=self.peers()[1], device_id_type=MESH,
        )

    def cut_block(self, to, cut):
        rows = rows_of(place(to, self.y, self.core, self.depth))
        return self.parts.at[self.spot(self.count - 1), rows, self.columns(cut)]

    def direct_copy(self, to, cut):
        rows = rows_of(self.z - (self.z > to).astype(jnp.int32))
        return pltpu.make_async_remote_copy(
            self.cut_block(to, cut), self.from_low.at[self.passes - 1, rows, self.columns(cut)],
            self.cut_s.at[cut, to], self.cut_r.at[cut, self.z],
            device_id=self.device(to, self.y, self.core), device_id_type=MESH,
        )

    def go_direct(self):
        @pl.loop(0, self.cuts)
        def _(cut):
            self.y_cut(cut).wait_recv()
            columns, first = self.columns(cut), (self.count - 1 - self.early) * self.depth

            @pl.loop(0, self.depth)
            def _(to):
                self.add(self.cut_block(to, cut), self.from_y[rows_of(first + to), columns])

            for distance in range(self.depth - 1, 0, -1):
                pl.when(self.z + distance < self.depth)(lambda: self.direct_copy(self.z + distance, cut).start())
                pl.when(self.z >= distance)(lambda: self.direct_copy(self.z - distance, cut).start())

    def finish_direct(self):
        @pl.loop(0, self.cuts)
        def _(cut):
            total = self.total.at[rows_of(self.count - 1), self.columns(cut)]
            total[...] = self.cut_block(self.z, cut)[...].astype(jnp.float32)

            @pl.loop(0, self.depth - 1)
            def _(i):
                source = i + (i >= self.z).astype(jnp.int32)
                arrived = self.from_low.at[self.passes - 1, rows_of(i), self.columns(cut)]
                pltpu.make_async_remote_copy(
                    arrived, arrived, self.cut_s.at[cut, source], self.cut_r.at[cut, source],
                    device_id=self.device(source, self.y, self.core), device_id_type=MESH,
                ).wait_recv()
                total[...] += arrived[...].astype(jnp.float32)

    def drain_direct(self):
        @pl.loop(0, self.cuts)
        def _(cut):
            self.y_cut(cut).wait_send()
            for to in range(self.depth):
                pl.when(self.z != to)(lambda: self.direct_copy(to, cut).wait_send())

    def along(self, t, ahead):
        last, soon, chained = self.depth - 1, 2 * self.early, self.chained
        for far, action in ((self.z, self.go_up), (last - self.z, self.go_down)) if self.hops else ():
            pl.when(far > 0)(lambda far=far, action=action: at(t - far, 0, chained, action))

        ends = ((self.z == 0, self.go_up), (self.z == last, self.go_down))
        for end, action in ends:
            if self.early:
                pl.when(end)(lambda action=action: at(t + ahead, 0, soon, action))
        if self.hops:
            at(t, soon, self.passes - 1, self.after_y)
        for end, action in ends:
            if self.hops:
                pl.when(end)(lambda action=action: at(t, soon, chained, action))
        if self.hops:
            at(t, chained, self.passes - 1, self.go_straight)
        pl.when(t == self.passes - 1)(self.go_direct)


def at(k, low, high, action):
    @pl.when((k >= low) & (k < high))
    def _():
        action(k)


def over(count, size):
    def run(action):
        @pl.loop(0, count // size)
        def _(i):
            action(pl.ds(pl.multiple_of(i * size, size), size))

    return run


def train_kernel(
    depth, images,
    patches, signs_in, tiles_in, valid_in, cotangent, attend_in, project_in, expand_in, shrink_in, first_in, second_in,
    bottle_from, results, total_out, rest_out,
    signs, tiles, valid, first, second, bottle_in, rest, total, parts, attend, project, left, right, soft, temp, saved, normed_one, normed_two, residual, factor_one,
    factor_two, average_two, bias, codes, bottle, delta, code_grad, bottle_sum, mix, packed, code_sum,
    code_core, code_y, code_z, code_other, gain_one, gain_two, extra,
    loads, code_sems, stores, sum_sems, *scratch,
):
    rows, width = patches.shape
    length = rows // images
    work = total.at[:rows]
    count, slabs = parts.shape[0], shrink_in.shape[0] // width
    pairs = width // 128
    encoding = lax.axis_index("section") == 0

    def content(k):
        other = jnp.where(k < 2 * slabs, (k + slabs) % (2 * slabs), k)
        return jnp.where(encoding, (k + slabs) % count, other)

    def location(k):
        return (k + jnp.where(encoding, slabs, 2 * slabs)) % count

    held = jnp.where(encoding, slabs + 4, 2 * slabs + 1)
    main = Reduction(depth, EARLY, STRAIGHT, CUTS, held, location, parts, total, scratch[:17])
    small = Reduction(depth, 0, 1, 1, 1, lambda k: k, extra, rest, scratch[17:34])
    lane = lax.broadcasted_iota(jnp.int32, (length, 128), 1)
    low_half = lane < HD
    bf, f32 = jnp.bfloat16, jnp.float32

    def dot(a, b):
        return jnp.dot(a, b, preferred_element_type=f32)

    def load(source, target, i):
        return pltpu.make_async_copy(source, target, loads.at[i])

    little = [
        load(source, target, 7 + 2 * slabs + i)
        for i, (source, target) in enumerate(
            (
                (signs_in, signs), (bottle_from, bottle_in), (tiles_in, tiles), (valid_in, valid), (first_in, first),
                (second_in, second),
            )
        )
    ]
    for copy in little[:2]:
        copy.start()
    fetch = [load(patches, right.at[5], 0)]
    fetch += [load(attend_in.at[:, pl.ds(j * width, width)], attend.at[j], 1 + j) for j in range(3)]
    for copy in fetch + little[2:]:
        copy.start()
    main.greet()
    fetch += [load(project_in, project, 4)]
    fetch += [load(expand_in.at[:, pl.ds(j * width, width)], parts.at[2 * slabs + j], 5 + j) for j in range(slabs)]
    fetch += [load(shrink_in.at[pl.ds(j * width, width)], parts.at[slabs + j], 5 + slabs + j) for j in range(slabs)]
    fetch += [load(cotangent, right.at[0], 5 + 2 * slabs)]

    for copy in little[:2]:
        copy.wait()
    code_width = signs.shape[0]
    work[:256, :] = jnp.zeros((256, width), f32)
    work[:code_width, :rows] = (2 * signs[...] - 1).astype(f32) / math.sqrt(code_width)
    work[128 : 128 + code_width, :] = bottle_in[...].astype(f32)
    codes[...] = work[:128, :rows].T.astype(bf)
    bottle[...] = work[128:256, :].T.astype(bf)
    for copy in little[2:]:
        copy.wait()
    for i in range(images):
        row = jnp.broadcast_to(tiles[i : i + 1, :].astype(f32), (length, length))
        live = jnp.broadcast_to(valid[i : i + 1, :], (length, length)) == 1
        spot = lax.broadcasted_iota(jnp.int32, (length, length), 0) == lax.broadcasted_iota(
            jnp.int32, (length, length), 1
        )
        bias[i] = jnp.where(((row == row.T) & live) | spot, 0.0, -1000000000.0)
    turned = work[128:256, :]
    mix[...] = ((turned - jnp.mean(turned, axis=1, keepdims=True)) * first[...]).T.astype(bf)
    packed[...] = jnp.zeros_like(packed)
    gain_one[...] = jnp.zeros_like(gain_one)
    gain_two[...] = jnp.zeros_like(gain_two)
    fetch[0].wait()

    @pl.when(encoding)
    def _():
        residual[...] = right[5].astype(f32)

    @pl.when(jnp.logical_not(encoding))
    def _():
        residual[...] = times_transpose(codes[...], bottle[...])

    def norm(gain, normed, factor, average=None):
        values = residual[...]
        middle = jnp.mean(values, axis=-1, keepdims=True)
        if average is not None:
            average[...] = middle
        center = values - middle
        scale = lax.rsqrt(jnp.mean(center * center, axis=-1, keepdims=True) + 1e-06)
        unscaled = center * scale
        normed[...] = unscaled
        factor[...] = scale
        temp[...] = (unscaled * gain[...]).astype(bf)

    def keep_transpose(source, target):
        half = 8 * ROWS
        for i in range(width // half):
            turned = source[:, i * half : (i + 1) * half].T
            for j in range(8):
                z, y, core = i * 2 + j // 4, (j // 2) % 2, j % 2
                target[place(z, y, core, depth) * ROWS : (place(z, y, core, depth) + 1) * ROWS, :] = turned[
                    j * ROWS : (j + 1) * ROWS
                ]

    norm(first, normed_one, factor_one)
    for j in range(3):
        fetch[1 + j].wait()
        if j == 2:
            for copy in fetch[4:]:
                copy.start()
        right[6 + j] = dot(temp[...], attend[j]).astype(bf)


    group = 3
    heads = [(pair, head) for pair in range(group) for head in range(2)]

    def group_of(turn):
        image = turn * group // pairs
        start = turn * group - image * pairs
        lanes = [pl.ds(pl.multiple_of((start + pair) * 128, 128), 128) for pair in range(group)]
        return pl.ds(pl.multiple_of(image * length, length), length), lanes, image

    def masked(values, low, scale=1.0):
        return jnp.where(low_half if low else jnp.logical_not(low_half), values * scale, 0.0).astype(bf)

    def merged(members, pair):
        return jnp.where(low_half, members[2 * pair], members[2 * pair + 1])

    @pl.loop(0, images * pairs // group)
    def _(turn):
        r, lanes, image = group_of(turn)
        query, key, value = ([right[6 + j, r, c] for c in lanes] for j in range(3))
        scores = [
            times_transpose(masked(query[pair], head == 0, HD**-0.5), key[pair]) + bias[image] for pair, head in heads
        ]
        raised = [jnp.exp(member - jnp.max(member, axis=-1, keepdims=True)) for member in scores]
        weights = [(member * (1.0 / jnp.sum(member, axis=-1, keepdims=True))).astype(bf) for member in raised]
        for (pair, head), member in zip(heads, weights):
            soft[turn * group + pair, head * length : (head + 1) * length, :] = member
        mixed = [dot(member, value[pair]) for (pair, head), member in zip(heads, weights)]
        for pair, c in enumerate(lanes):
            temp[r, c] = merged(mixed, pair).astype(bf)

    fetch[4].wait()

    residual[...] += dot(temp[...], project[...])

    keep_transpose(temp, left.at[slabs + 1])
    norm(second, normed_two, factor_two, average_two)

    for j in range(slabs):
        fetch[5 + j].wait()

        hidden = dot(temp[...], parts[2 * slabs + j])
        share = 0.5 + 0.5 * lax.erf(hidden * math.sqrt(0.5))
        slope = share + hidden * jnp.exp(-0.5 * hidden * hidden) * (1.0 / math.sqrt(2.0 * math.pi))
        parts[j, :rows, :] = (hidden * share).astype(bf)
        right[1 + j] = slope.astype(bf)

    for copy in fetch[5 + slabs :]:
        copy.wait()
    out_copy = pltpu.make_async_copy(saved, results, loads.at[6 + 2 * slabs])
    across = pltpu.make_async_remote_copy(
        delta, code_grad, code_sems.at[0], code_sems.at[1], device_id=main.peers()[4], device_id_type=MESH
    )
    main.meet()

    @pl.when(jnp.logical_not(encoding))
    def _():
        residual[...] = right[0].astype(f32)

    def keep_norm(gain, normed, target):
        temp[...] = (normed[...] * gain[...]).astype(bf)
        keep_transpose(temp, target)

    def block_output():
        output = normed_two[...] * (1.0 / factor_two[...]) + average_two[...]
        for j in range(slabs):
            output += dot(parts[j, :rows, :], parts[slabs + j])
        saved[...] = output.astype(bf)
        pl.when(jnp.logical_not(encoding))(out_copy.start)
        for i in range(2 * slabs):
            z, y = i // 2, i % 2
            turned = parts[i // 2, :rows, (i % 2) * 8 * ROWS : (i % 2 + 1) * 8 * ROWS].T
            for core in range(2):
                for j in range(slabs):
                    spot, start = place(z, y, core, depth) * ROWS, (core * 4 + j) * ROWS
                    left[j, spot : spot + ROWS, :] = turned[start : start + ROWS]

    def from_codes():
        latent = dot(saved[...], bottle[...])
        scale = lax.rsqrt(jnp.sum(latent * latent, axis=-1, keepdims=True) + 1e-06)
        unit_code = latent * scale
        work[:128, :rows] = jnp.zeros((128, rows), f32)
        across.wait_recv()
        work[: delta.shape[0], :rows] = code_grad[...].astype(f32)
        grad_unit = work[:128, :rows].T
        grad_latent = (
            scale * (grad_unit - unit_code * jnp.sum(unit_code * grad_unit, axis=-1, keepdims=True))
        ).astype(bf)
        grad_out = times_transpose(grad_latent, bottle[...])
        right[0] = grad_out.astype(bf)
        residual[...] = grad_out
        codes[...] = grad_latent

    def piece(k):
        c = content(k)
        a = jnp.minimum(c, slabs) + (c >= 2 * slabs).astype(jnp.int32) + (c > 2 * slabs).astype(jnp.int32)
        b = jnp.maximum(c - slabs + 1, 0)
        parts[location(k)] = dot(left[a], right[b]).astype(bf)
        main.start(k)

    def norm_back(gain, normed, factor, gain_sum, low):
        @over(rows, length)
        def _(r):
            given, unscaled = work[r, :], normed[r, :]
            gain_sum[...] += jnp.sum((given * unscaled).reshape(-1, 8, width), axis=0)
            grad = given * gain[...]
            inner = jnp.mean(grad * unscaled, axis=-1, keepdims=True)
            grad = residual[r, :] + factor[r, :] * (grad - jnp.mean(grad, axis=-1, keepdims=True) - unscaled * inner)
            residual[r, :] = grad
            low[r, :] = grad.astype(bf)

    def through_shrink():
        for j in range(slabs):
            grad = times_transpose(right[0], parts[slabs + j])
            right[1 + j] = (grad * right[1 + j].astype(f32)).astype(bf)

    def through_expand():
        grad = times_transpose(right[1], parts[2 * slabs])
        for j in range(1, slabs):
            grad += times_transpose(right[1 + j], parts[2 * slabs + j])
        work[...] = grad

    def through_project():
        norm_back(second, normed_two, factor_two, gain_two, right.at[5])

        temp[...] = times_transpose(right[5], project[...]).astype(bf)

    def through_heads(low, high):
        @pl.loop(low, high)
        def _(turn):
            r, lanes, image = group_of(turn)
            query, key, value = ([right[6 + j, r, c] for c in lanes] for j in range(3))
            weights = [soft[turn * group + pair, head * length : (head + 1) * length, :] for pair, head in heads]
            grad_heads = [masked(temp[r, lanes[pair]], head == 0) for pair, head in heads]
            grad_soft = [times_transpose(member, value[pair]) for (pair, head), member in zip(heads, grad_heads)]
            grad_scores = []
            for low, member in zip(weights, grad_soft):
                exact = low.astype(f32)
                inner = jnp.sum(exact * member, axis=-1, keepdims=True)
                grad_scores.append((exact * (member - inner)).astype(bf))
            to_query = [dot(member, key[pair]) for (pair, head), member in zip(heads, grad_scores)]
            to_key = [
                contract_rows(member, masked(query[pair], head == 0, HD**-0.5))
                for (pair, head), member in zip(heads, grad_scores)
            ]
            to_value = [contract_rows(low, member) for low, member in zip(weights, grad_heads)]
            for pair, c in enumerate(lanes):
                right[6, r, c] = (merged(to_query, pair) * HD**-0.5).astype(bf)
                right[7, r, c] = (to_key[2 * pair] + to_key[2 * pair + 1]).astype(bf)
                right[8, r, c] = (to_value[2 * pair] + to_value[2 * pair + 1]).astype(bf)

    half = 3 * width // 2
    own_half = pl.ds(pl.multiple_of(main.core * half, half), half)

    def sum_copy(stage, source, target, send, receive, device):
        return pltpu.make_async_remote_copy(
            source, target, sum_sems.at[2 * stage, send], sum_sems.at[2 * stage + 1, receive],
            device_id=device, device_id_type=MESH,
        )

    def sum_core():
        return sum_copy(0, code_sum, code_core, 0, 0, main.peers()[0])

    def sum_y():
        return sum_copy(0, code_sum.at[:, own_half], code_y, 1, 1, main.peers()[1])

    def sum_back():
        return sum_copy(0, code_sum.at[:, own_half], code_other, 2, 2, main.peers()[0])

    def sum_z(to):
        return sum_copy(
            1, code_sum.at[:, own_half], code_z.at[main.z - (main.z > to).astype(jnp.int32)], to, main.z,
            main.device(to, main.y, main.core),
        )

    def sum_codes():
        scaled = (codes[...].astype(f32) * factor_one[...]).astype(bf)
        for j in range(3):
            code_sum[:, j * width : (j + 1) * width] = contract_rows(scaled, right[6 + j])[: code_sum.shape[0]].astype(bf)
        sum_core().start()

    def sum_after_core():
        sum_core().wait_send()
        sum_core().wait_recv()
        code_sum[...] = (code_sum[...].astype(f32) + code_core[...].astype(f32)).astype(bf)
        sum_y().start()

    def sum_after_y():
        sum_y().wait_send()
        sum_y().wait_recv()
        code_sum[:, own_half] = (code_sum[:, own_half].astype(f32) + code_y[...].astype(f32)).astype(bf)
        for to in range(depth):
            pl.when(main.z != to)(lambda: sum_z(to).start())

    def sum_after_z():
        together = code_sum[:, own_half].astype(f32)
        for z in range(depth):
            pl.when(main.z != z)(lambda: sum_z(z).wait_send())
            source = code_z.at[jnp.minimum(z, depth - 2)]

            @pl.when(main.z != z)
            def _():
                sum_copy(1, source, source, z, z, main.device(z, main.y, main.core)).wait_recv()

        for i in range(depth - 1):
            together += code_z[i].astype(f32)
        code_sum[:, own_half] = together.astype(bf)
        sum_back().start()

    def finish_attend():
        sum_back().wait_send()
        sum_back().wait_recv()
        code_sum[:, pl.ds(pl.multiple_of((1 - main.core) * half, half), half)] = code_other[...]
        own = mix[pl.ds(pl.multiple_of(main.me * ROWS, ROWS), ROWS), :][:, : code_sum.shape[0]]
        for j in range(3):
            k = 2 * slabs + 1 + j
            total[k * ROWS : (k + 1) * ROWS, :] = dot(own, code_sum[:, j * width : (j + 1) * width])
            store(k).start()

    def through_attend():
        grad = times_transpose(right[6], attend[0])
        for j in range(1, 3):
            grad += times_transpose(right[6 + j], attend[j])
        work[...] = grad

        @pl.when(encoding)
        def _():
            bottle_sum[...] = contract_rows(saved[...], codes[...])
            latent = codes[...].astype(f32)
            together = dot(left[0], pltpu.roll(latent, PACK, 1).astype(bf))
            for j in range(1, slabs):
                together += dot(left[j], pltpu.roll(latent, PACK + STRIDE * j, 1).astype(bf))
            packed[...] = together

        norm_back(first, normed_one, factor_one, gain_one, saved)

        @pl.when(jnp.logical_not(encoding))
        def _():
            turned = lax.dot_general(bottle[...], saved[...], (((0,), (1,)), ((), ())), preferred_element_type=f32)
            delta[...] = turned[: delta.shape[0]].astype(bf)
            across.start()
            bottle_sum[...] = contract_rows(saved[...], codes[...])
            sum_codes()

        @pl.when(encoding)
        def _():
            out_copy.start()

        spare = lax.broadcasted_iota(jnp.int32, (width, 128), 1)
        column_one = jnp.sum(gain_one[...].T, axis=1, keepdims=True)
        column_two = jnp.sum(gain_two[...].T, axis=1, keepdims=True)
        gathered = jnp.where(
            spare == code_width, column_one, jnp.where(spare == code_width + 1, column_two, bottle_sum[...])
        )
        for i in range(4 * depth):
            start = place(i // 4, (i // 2) % 2, i % 2, depth) * ROWS
            extra[0, start : start + ROWS, :] = (
                gathered[i * ROWS : (i + 1) * ROWS] + packed[start : start + ROWS, :]
            ).astype(bf)
        small.start(0)

    def store(k):
        return pltpu.make_async_copy(total.at[rows_of(k)], total_out.at[rows_of(content(k))], stores.at[k])

    def finish(p):
        main.finish(p)
        piece, _ = main.of_pass(p)
        pl.when(p >= 2 * EARLY)(store(piece).start)

    def finish_straight(p):
        main.finish_straight(p)
        store(main.of_pass(p)[0]).start()

    def finish_early(k):
        main.after_last(k)
        store(k).start()

    rest_copy = pltpu.make_async_copy(rest, rest_out, loads.at[13 + 2 * slabs])

    def finish_small():
        small.finish_direct()
        rest_copy.start()

        @pl.when(encoding)
        def _():
            for j in range(slabs):
                exact = pltpu.roll(rest[...], 128 - PACK - STRIDE * j, 1)
                high = exact.astype(bf)
                low = (exact - high.astype(f32)).astype(bf)
                k = slabs + 4 + j
                total[k * ROWS : (k + 1) * ROWS, :] = times_transpose(high, bottle[...]) + times_transpose(low, bottle[...])
                store(k).start()

    def send_late():
        for k in range(1 + EARLY - LATE, 1 + EARLY):
            main.start_last(k)

    def finish_last():
        main.finish_direct()
        store(held - 1).start()

    turns, links = images * pairs // group, 6

    @pl.loop(0, links + MOST + EARLY + 10)
    def _(step):
        k = step - links * main.section
        link = jnp.where(encoding, jnp.where(step == 0, 0, jnp.where(step >= 3, step - 2, -1)), step)
        pl.when((k == 0) & encoding)(lambda: keep_norm(first, normed_one, left.at[slabs + 2]))
        pl.when(k == 0)(lambda: keep_norm(second, normed_two, left.at[slabs]))
        pl.when(k == slabs * main.section)(block_output)
        pl.when((k == 0) & encoding)(from_codes)
        pl.when(link == 0)(through_shrink)
        now = jnp.where(k < slabs, k, jnp.where(k == slabs + 1, slabs, jnp.where(k >= slabs + 3, k - 2, -1)))
        at(now, 0, held, piece)
        met = jnp.where(k <= slabs + 2, k - 2, jnp.where(k >= slabs + 4, k - 3, -1))
        at(met, 0, held, main.after_core)
        main.along(k - 5, 2)
        at(k - 10, 0, main.chained, finish)
        at(k - 10, main.chained, main.passes - 1, finish_straight)
        pl.when(k == main.passes + 9)(finish_last)
        at(k - 12, 1, 1 + EARLY - LATE, main.start_last)
        at(k - slabs - SMALL - 6, 0, 1, small.after_core)
        small.along(k - slabs - SMALL - 7 - GAP, 0)
        pl.when(k == main.passes + 4)(send_late)
        pl.when(k == slabs + SMALL + GAP + 8)(finish_small)
        at(k - main.passes - 7, 1, 1 + EARLY, finish_early)
        for moment, action in ((2, sum_after_core), (7, sum_after_y), (9, sum_after_z), (11, finish_attend)):
            pl.when(jnp.logical_not(encoding) & (k == moment))(action)
        pl.when(link == 1)(through_expand)
        pl.when(link == 2)(through_project)
        pl.when((link == 3) | (link == 4))(lambda: through_heads((link - 3) * turns // 2, (link - 2) * turns // 2))
        pl.when(link == 5)(through_attend)

    out_copy.wait()
    rest_copy.wait()

    @pl.when(jnp.logical_not(encoding))
    def _():
        across.wait_send()

    small.drain(0)
    small.drain_direct()
    main.drain_direct()

    @pl.loop(0, held)
    def _(k):
        main.drain(k)

    @pl.loop(0, count)
    def _(k):
        store(k).wait()

    @pl.loop(0, main.chained)
    def _(p):
        main.drain_pass(p)

    @pl.loop(main.chained, main.passes - 1)
    def _(p):
        main.drain_straight(p)


def train(depth, images, arrays):
    patches, signs, _, _, _, attend, project, expand, shrink, _, _, bottle = arrays
    rows, width = patches.shape
    slabs = shrink.shape[0] // width
    count = 2 * slabs + 4
    pairs, length = width // 128, rows // images
    code_rows = -(-signs.shape[0] // 16) * 16
    hbm = pl.BlockSpec(memory_space=pl.ANY)
    low, full = lambda *shape: pltpu.VMEM(shape, jnp.bfloat16), lambda *shape: pltpu.VMEM(shape, jnp.float32)
    return pl.pallas_call(
        functools.partial(train_kernel, depth, images),
        out_shape=(
            jax.ShapeDtypeStruct((rows, width), jnp.bfloat16),
            jax.ShapeDtypeStruct((count * ROWS, width), jnp.float32),
            jax.ShapeDtypeStruct((ROWS, 128), jnp.float32),
        ),
        in_specs=[hbm] * 12,
        out_specs=[hbm] * 3,
        scratch_shapes=[pltpu.VMEM(arrays[i].shape, arrays[i].dtype) for i in (1, 2, 3, 9, 10, 11)]
        + [
            full(ROWS, 128),
            full(count * ROWS, width),
            low(count, width, width),
            low(3, width, width),
            low(width, width),
            low(slabs + 3, width, rows),
            low(slabs + 5, rows, width),
            low(images * pairs, 2 * length, length),
            low(rows, width),
            low(rows, width),
            full(rows, width),
            full(rows, width),
            full(rows, width),
            full(rows, 1),
            full(rows, 1),
            full(rows, 1),
            full(images, length, length),
            low(rows, 128),
            low(width, 128),
            low(code_rows, rows),
            low(code_rows, rows),
            full(width, 128),
            low(width, 128),
            full(width, 128),
            low(code_rows, 3 * width),
            low(code_rows, 3 * width),
            low(code_rows, 3 * width // 2),
            low(depth - 1, code_rows, 3 * width // 2),
            low(code_rows, 3 * width // 2),
            full(8, width),
            full(8, width),
            low(1, width, 128),
            pltpu.SemaphoreType.DMA((14 + 2 * slabs,)),
            pltpu.SemaphoreType.DMA((2,)),
            pltpu.SemaphoreType.DMA((count,)),
            pltpu.SemaphoreType.DMA((6, depth)),
        ]
        + Reduction.scratch(depth, EARLY, CUTS, MOST, width)
        + Reduction.scratch(depth, 0, 1, 1, 128),
        compiler_params=pltpu.CompilerParams(collective_id=0, has_side_effects=True, vmem_limit_bytes=63 << 20),
        name="train",
    )(*arrays)


def deliver_kernel(slabs, code, raw, total, rest, results, attend, project, expand, shrink, first, second, bottle):
    width = total.shape[1]
    results[...] = raw[...]
    for j in range(slabs):
        shrink[j * ROWS : (j + 1) * ROWS, :] = total[j * ROWS : (j + 1) * ROWS, :]
        expand[:, j * width : (j + 1) * width] = total[(slabs + j) * ROWS : (slabs + j + 1) * ROWS, :]
    project[...] = total[2 * slabs * ROWS : (2 * slabs + 1) * ROWS, :]
    for j in range(3):
        start = (2 * slabs + 1 + j) * ROWS
        attend[:, j * width : (j + 1) * width] = total[start : start + ROWS, :]
    turned = rest[...].T
    first[...] = turned[code : code + 1]
    second[...] = turned[code + 1 : code + 2]
    for i in range(code):
        bottle[i] = turned[i : i + 1]


def deliver(raw, total, rest, slabs, code):
    width = total.shape[1]
    vmem = pl.BlockSpec(memory_space=pltpu.VMEM)
    full = lambda *shape: jax.ShapeDtypeStruct(shape, jnp.float32)
    return pl.pallas_call(
        functools.partial(deliver_kernel, slabs, code),
        out_shape=(
            jax.ShapeDtypeStruct(raw.shape, raw.dtype),
            full(ROWS, 3 * width),
            full(ROWS, width),
            full(ROWS, slabs * width),
            full(slabs * ROWS, width),
            full(1, ROWS),
            full(1, ROWS),
            full(code, 1, ROWS),
        ),
        in_specs=[vmem] * 3,
        out_specs=[vmem] * 8,
        name="deliver",
    )(raw, total, rest)


def two_images(*arrays):
    images = arrays[2].shape[0]
    code = arrays[1].shape[1]
    slabs = arrays[8].shape[1] // arrays[0].shape[1]
    weights = tuple(member[0] for member in arrays[5:9])
    arrays = (arrays[0], arrays[1].T) + arrays[2:5] + weights + arrays[9:11] + (arrays[11][0].T,)
    raw, total, rest = train(lax.axis_size("batch") // 4, images, arrays)
    results, attend, project, expand, shrink, first, second, bottle = deliver(raw, total, rest, slabs, code)
    return (
        results[None], attend[None], project[None], expand[None], shrink[None], first, second, bottle.transpose(1, 2, 0)
    )


def pick_index(stacked, chosen):
    return lax.dynamic_index_in_dim(stacked, chosen, 0, keepdims=False)


def body(
    patches,
    code_signs,
    tile_ids,
    patch_valid,
    cotangent,
    attend_weight,
    project_weight,
    expand_weight,
    shrink_weight,
    norm_first,
    norm_second,
    bottleneck,
):
    micro_count = tile_ids.shape[0]
    length = tile_ids.shape[1]
    code_width = code_signs.shape[1]
    encoding = lax.axis_index("section") == 0
    encoding_int = encoding.astype(jnp.int32)
    weights = (
        attend_weight[0],
        project_weight[0],
        expand_weight[0],
        shrink_weight[0],
        norm_first[0],
        norm_second[0],
    )
    bottle = bottleneck[0]
    code_values = ((2 * code_signs - 1).astype(jnp.float32) / math.sqrt(code_width)).astype(
        jnp.bfloat16
    )
    block_inputs = []
    outputs_low = []
    unit_codes = []
    unit_factors = []
    decoded_list = []
    kept_list = []
    for turn_index in range(micro_count):
        image_rows = patches[turn_index * length : (turn_index + 1) * length].astype(jnp.float32)
        decoder_in = times_transpose(
            code_values[turn_index * length : (turn_index + 1) * length], bottle
        )
        block_in = jnp.where(encoding, image_rows, decoder_in)
        allowed_keys = allowed(tile_ids[turn_index], patch_valid[turn_index])
        output, kept_parts = block_forward(block_in, weights, allowed_keys)
        output_low = output.astype(jnp.bfloat16)
        latent = jnp.dot(output_low, bottle, preferred_element_type=jnp.float32)
        factor = lax.rsqrt(jnp.sum(latent * latent, axis=-1, keepdims=True) + 1e-06)
        block_inputs.append(block_in)
        outputs_low.append(output_low)
        unit_codes.append(latent * factor)
        unit_factors.append(factor)
        decoded_list.append(output_low)
        kept_list.append(kept_parts)
    block_inputs = jnp.stack(block_inputs)
    outputs_low = jnp.stack(outputs_low)
    unit_codes = jnp.stack(unit_codes)
    unit_factors = jnp.stack(unit_factors)
    kept_stack = jax.tree.map(lambda *members: jnp.stack(members), *kept_list)
    totals = None
    sent_grad = jnp.zeros((length, code_width), jnp.bfloat16)
    input_grads = []
    for turn_index in range(micro_count + 1):
        if turn_index > 0:
            received = passed_along(sent_grad, "section", -1)
        else:
            received = jnp.zeros_like(sent_grad)
        chosen = jnp.clip(turn_index - encoding_int, 0, micro_count - 1)
        turn_flag = jnp.where(encoding, turn_index >= 1, turn_index < micro_count).astype(
            jnp.float32
        )
        kept_parts = jax.tree.map(lambda stacked: pick_index(stacked, chosen), kept_stack)
        unit_code = pick_index(unit_codes, chosen)
        factor = pick_index(unit_factors, chosen)
        output_low = pick_index(outputs_low, chosen)
        grad_unit = received.astype(jnp.float32)
        grad_latent = (
            factor
            * (grad_unit - unit_code * jnp.sum(unit_code * grad_unit, axis=-1, keepdims=True))
        ).astype(jnp.bfloat16)
        grad_encoded = times_transpose(grad_latent, bottle)
        bottle_encoder = contract_rows(output_low, grad_latent)
        given_grad = lax.dynamic_slice_in_dim(cotangent, chosen * length, length, 0).astype(
            jnp.float32
        )
        grad_out = jnp.where(encoding, grad_encoded, given_grad)
        grad_in, grads = block_backward(kept_parts, grad_out, weights)
        grad_in_low = grad_in.astype(jnp.bfloat16)
        code_rows = lax.dynamic_slice_in_dim(code_values, chosen * length, length, 0)
        bottle_decoder = contract_rows(grad_in_low, code_rows)
        sent_grad = jnp.dot(grad_in_low, bottle, preferred_element_type=jnp.float32).astype(
            jnp.bfloat16
        )
        grads = grads + (jnp.where(encoding, bottle_encoder, bottle_decoder),)
        grads = tuple((turn_flag * member for member in grads))
        if turn_index > 0:
            input_grads.append(grad_in_low)
        totals = (
            grads
            if totals is None
            else tuple((former + latter for former, latter in zip(totals, grads)))
        )
    totals = lax.psum_scatter(totals, "batch", scatter_dimension=0, tiled=True)
    pieces = [
        jnp.where(encoding, input_grads[turn_index], decoded_list[turn_index])
        for turn_index in range(micro_count)
    ]
    results = jnp.concatenate(pieces, axis=0)[None]
    return (
        results,
        totals[0][None],
        totals[1][None],
        totals[2][None],
        totals[3][None],
        totals[4][None],
        totals[5][None],
        totals[6][None],
    )


def solution(mesh):
    batch = mesh.shape["batch"]
    return jax.shard_map(
        two_images if batch == 16 else body,
        mesh=mesh,
        in_specs=(
            P("batch", None),
            P("batch", None),
            P("batch", None),
            P("batch", None),
            P("batch", None),
            P("section", None, None),
            P("section", None, None),
            P("section", None, None),
            P("section", None, None),
            P("section", None),
            P("section", None),
            P("section", None, None),
        ),
        out_specs=(
            P("section", "batch", None),
            P("section", "batch", None),
            P("section", "batch", None),
            P("section", "batch", None),
            P("section", "batch", None),
            P("section", "batch"),
            P("section", "batch"),
            P("section", "batch", None),
        ),
        check_vma=False,
    )
```

```python
import functools
import math

import jax
import jax.numpy as jnp
from jax import lax
from jax.experimental import pallas as pl
from jax.experimental.pallas import tpu as pltpu
from jax.sharding import PartitionSpec as P

H = 12
HD = 64
MESH = pl.DeviceIdType.MESH
ROWS = 48
SLOTS = 4
EARLY = 1
MOST = 9
PACK = 32
STRIDE = 24
CUTS = 3
STRAIGHT = 1
LATE = 1
SMALL = -2
GAP = 3


def passed_along(block, axis, distance):
    devices = range(lax.axis_size(axis))
    route = [(i - distance, i) for i in devices if i - distance in devices]
    return lax.ppermute(block, axis, route)


def contract_rows(former, latter):
    return lax.dot_general(
        former, latter, (((0,), (0,)), ((), ())), preferred_element_type=jnp.float32
    )


def times_transpose(former, latter):
    return lax.dot_general(
        former, latter, (((1,), (1,)), ((), ())), preferred_element_type=jnp.float32
    )


def normalize(values):
    average = jnp.mean(values, axis=-1, keepdims=True)
    center = values - average
    spread = jnp.mean(center * center, axis=-1, keepdims=True)
    factor = lax.rsqrt(spread + 1e-06)
    return (center * factor, factor)


def norm_back(grad_normed, normed, factor):
    return factor * (
        grad_normed
        - jnp.mean(grad_normed, axis=-1, keepdims=True)
        - normed * jnp.mean(grad_normed * normed, axis=-1, keepdims=True)
    )


def allowed(tile_row, keep_row):
    places = jnp.arange(tile_row.shape[0])
    same_tile = tile_row[:, None] == tile_row[None, :]
    live_keys = keep_row[None, :] == 1
    return same_tile & live_keys | (places[:, None] == places[None, :])


def block_forward(residual, weights, allowed_keys):
    attend, project, expand, shrink, first, second = weights
    length, model_width = residual.shape
    normed_one, factor_one = normalize(residual)
    input_one = (normed_one * first).astype(jnp.bfloat16)
    joint_proj = jnp.dot(input_one, attend, preferred_element_type=jnp.float32).astype(jnp.bfloat16)
    split_parts = joint_proj.reshape(length, 3, H, HD)
    queries = split_parts[:, 0]
    key_rows = split_parts[:, 1]
    value_rows = split_parts[:, 2]
    scores = jnp.einsum(
        "qhd,khd->hqk", queries, key_rows, preferred_element_type=jnp.float32
    ) * HD ** (-0.5)
    scores = jnp.where(allowed_keys[None], scores, -1000000000.0)
    maximum = jnp.max(scores, axis=-1, keepdims=True)
    raised = jnp.exp(scores - maximum)
    softmax_out = raised / jnp.sum(raised, axis=-1, keepdims=True)
    softmax_low = softmax_out.astype(jnp.bfloat16)
    mixed_heads = jnp.einsum(
        "hqk,khd->qhd", softmax_low, value_rows, preferred_element_type=jnp.float32
    )
    mixed_heads = mixed_heads.reshape(length, model_width).astype(jnp.bfloat16)
    middle = residual + jnp.dot(mixed_heads, project, preferred_element_type=jnp.float32)
    normed_two, factor_two = normalize(middle)
    input_two = (normed_two * second).astype(jnp.bfloat16)
    hidden = jnp.dot(input_two, expand, preferred_element_type=jnp.float32)
    active = jax.nn.gelu(hidden, approximate=False).astype(jnp.bfloat16)
    output = middle + jnp.dot(active, shrink, preferred_element_type=jnp.float32)
    kept_parts = (
        normed_one,
        factor_one,
        input_one,
        queries,
        key_rows,
        value_rows,
        softmax_out,
        softmax_low,
        mixed_heads,
        normed_two,
        factor_two,
        input_two,
        hidden,
        active,
    )
    return (output, kept_parts)


def block_backward(kept_parts, grad_out, weights):
    attend, project, expand, shrink, first, second = weights
    (
        normed_one,
        factor_one,
        input_one,
        queries,
        key_rows,
        value_rows,
        softmax_out,
        softmax_low,
        mixed_heads,
        normed_two,
        factor_two,
        input_two,
        hidden,
        active,
    ) = kept_parts
    length, model_width = grad_out.shape
    grad_rounded = grad_out.astype(jnp.bfloat16)
    grad_shrink = contract_rows(active, grad_rounded)
    grad_active = times_transpose(grad_rounded, shrink)
    _, gelu_back = jax.vjp(lambda values: jax.nn.gelu(values, approximate=False), hidden)
    grad_hidden = gelu_back(grad_active)[0].astype(jnp.bfloat16)
    grad_expand = contract_rows(input_two, grad_hidden)
    grad_input_two = times_transpose(grad_hidden, expand)
    grad_second = jnp.sum(grad_input_two * normed_two, axis=0)
    grad_middle = grad_out + norm_back(grad_input_two * second, normed_two, factor_two)
    middle_low = grad_middle.astype(jnp.bfloat16)
    grad_project = contract_rows(mixed_heads, middle_low)
    grad_mixed = times_transpose(middle_low, project).astype(jnp.bfloat16).reshape(length, H, HD)
    grad_soft = jnp.einsum(
        "qhd,khd->hqk", grad_mixed, value_rows, preferred_element_type=jnp.float32
    )
    grad_values = jnp.einsum(
        "hqk,qhd->khd", softmax_low, grad_mixed, preferred_element_type=jnp.float32
    )
    inner_sum = jnp.sum(softmax_out * grad_soft, axis=-1, keepdims=True)
    grad_scores = (softmax_out * (grad_soft - inner_sum)).astype(jnp.bfloat16)
    score_scale = HD ** (-0.5)
    grad_queries = (
        jnp.einsum("hqk,khd->qhd", grad_scores, key_rows, preferred_element_type=jnp.float32)
        * score_scale
    )
    grad_keys = (
        jnp.einsum("hqk,qhd->khd", grad_scores, queries, preferred_element_type=jnp.float32)
        * score_scale
    )
    grad_joint = (
        jnp.stack([grad_queries, grad_keys, grad_values], axis=1)
        .reshape(length, 3 * model_width)
        .astype(jnp.bfloat16)
    )
    grad_attend = contract_rows(input_one, grad_joint)
    grad_input_one = times_transpose(grad_joint, attend)
    grad_first = jnp.sum(grad_input_one * normed_one, axis=0)
    grad_residual = grad_middle + norm_back(grad_input_one * first, normed_one, factor_one)
    return (
        grad_residual,
        (grad_attend, grad_project, grad_expand, grad_shrink, grad_first, grad_second),
    )


def rows_of(index):
    return pl.ds(pl.multiple_of(index * ROWS, ROWS), ROWS)


def place(z, y, core, depth):
    return (core * 2 + y) * depth + z


class Reduction:
    def __init__(self, depth, early, straight, cuts, count, spot, parts, total, scratch):
        self.depth, self.early, self.cuts = depth, early, cuts
        self.count, self.passes, self.spot = count, count + early, spot
        self.chained, self.hops = self.passes - straight, early > 0
        self.parts, self.total = parts, total
        self.from_core, self.from_y, self.from_low, self.from_high = scratch[:4]
        self.core_s, self.core_r, self.y_s, self.y_r = scratch[4:8]
        self.up_s, self.up_r, self.down_s, self.down_r, self.free = scratch[8:13]
        self.cut_y_s, self.cut_y_r, self.cut_s, self.cut_r = scratch[13:17]
        self.section = lax.axis_index("section")
        self.me = lax.axis_index("batch")
        self.z, self.y, self.core = self.me // 4, (self.me // 2) % 2, self.me % 2

    def scratch(depth, early, cuts, count, wide):
        low, dma = lambda *shape: pltpu.VMEM(shape, jnp.bfloat16), pltpu.SemaphoreType.DMA
        return [
            low(min(count, SLOTS), 2 * depth * ROWS, wide),
            low((count - early) * depth * ROWS + early * ROWS, wide),
            low(count + early, (depth - 1) * ROWS, wide),
            low(count + early, (depth - 1) * ROWS, wide),
        ] + [dma((count,))] * 4 + [dma((count + early, depth))] * 4 + [
            pltpu.SemaphoreType.REGULAR, dma((cuts,)), dma((cuts,)), dma((cuts, depth)), dma((cuts, depth))
        ]

    def device(self, z, y, core):
        return (self.section, z * 4 + y * 2 + core)

    def peers(self):
        return (
            self.device(self.z, self.y, 1 - self.core),
            self.device(self.z, 1 - self.y, self.core),
            self.device(jnp.minimum(self.z + 1, self.depth - 1), self.y, self.core),
            self.device(jnp.maximum(self.z - 1, 0), self.y, self.core),
            (1 - self.section, self.me),
        )

    def greet(self):
        barrier = pltpu.get_barrier_semaphore()

        def signal(device):
            pl.semaphore_signal(barrier, inc=1, device_id=device, device_id_type=MESH)

        core, other, _, _, across = self.peers()
        for peer in (core, other, across):
            signal(peer)
        for z in range(self.depth):
            pl.when(self.z != z)(lambda z=z: signal(self.device(z, self.y, self.core)))

    def meet(self):
        pl.semaphore_wait(pltpu.get_barrier_semaphore(), self.depth + 2)

    def block(self, k, core, y, z):
        return self.parts.at[self.spot(k), rows_of(place(z, y, core, self.depth))]

    def core_copy(self, k):
        half = 2 * self.depth * ROWS
        return pltpu.make_async_remote_copy(
            self.parts.at[self.spot(k), pl.ds(pl.multiple_of((1 - self.core) * half, half), half)],
            self.from_core.at[k % SLOTS], self.core_s.at[k], self.core_r.at[k],
            device_id=self.peers()[0], device_id_type=MESH,
        )

    def slot(self, k):
        return jnp.maximum(k - self.early, 0)

    def is_early(self, k):
        return (k >= 1) & (k <= self.early)

    def y_copy(self, k):
        quarter = self.depth * ROWS
        start, slot = (self.core * 2 + 1 - self.y) * quarter, self.slot(k) * quarter
        return pltpu.make_async_remote_copy(
            self.parts.at[self.spot(k), pl.ds(pl.multiple_of(start, quarter), quarter)],
            self.from_y.at[pl.ds(pl.multiple_of(slot, quarter), quarter)], self.y_s.at[k], self.y_r.at[k],
            device_id=self.peers()[1], device_id_type=MESH,
        )

    def last_rows(self, k):
        return rows_of((MOST - self.early) * self.depth + k - 1)

    def last_copy(self, k):
        return pltpu.make_async_remote_copy(
            self.block(k, self.core, 1 - self.y, self.z), self.from_y.at[self.last_rows(k)],
            self.y_s.at[k], self.y_r.at[k],
            device_id=self.peers()[1], device_id_type=MESH,
        )

    def of_pass(self, p):
        if not self.early:
            return p, self.y
        soon = p < 2 * self.early
        piece = jnp.where(soon, 1 + p // 2, jnp.where(p == 2 * self.early, 0, p - self.early))
        return piece, jnp.where(soon & (p % 2 == 0), 1 - self.y, self.y)

    def pass_block(self, p, to):
        k, y = self.of_pass(p)
        return self.block(k, self.core, y, to)

    def up_copy(self, p, to):
        return pltpu.make_async_remote_copy(
            self.pass_block(p, to), self.from_low.at[p, rows_of(to - 1)],
            self.up_s.at[p, to], self.up_r.at[p, to],
            device_id=self.peers()[2], device_id_type=MESH,
        )

    def down_copy(self, p, to):
        return pltpu.make_async_remote_copy(
            self.pass_block(p, to), self.from_high.at[p, rows_of(to)],
            self.down_s.at[p, to], self.down_r.at[p, to],
            device_id=self.peers()[3], device_id_type=MESH,
        )

    def add(self, here, other):
        here[...] = (here[...].astype(jnp.float32) + other.astype(jnp.float32)).astype(jnp.bfloat16)

    def start(self, k):
        @pl.when(k >= SLOTS)
        def _():
            pl.semaphore_wait(self.free, 1)

        self.core_copy(k).start()

    def after_core(self, k):
        self.core_copy(k).wait_recv()
        for far in (1, 0):
            half = (self.y + far) % 2

            @pl.loop(0, self.depth)
            def _(to):
                self.add(self.block(k, self.core, half, to), self.from_core[k % SLOTS, rows_of(half * self.depth + to)])

            if far:

                @pl.when(jnp.logical_not(self.is_early(k)) & (k < self.count - 1))
                def _():
                    self.y_copy(k).start()

                @pl.when(k == self.count - 1)
                def _():
                    for cut in range(self.cuts):
                        self.y_cut(cut).start()

        @pl.when(k + SLOTS < self.count)
        def _():
            pl.semaphore_signal(self.free, inc=1, device_id=self.peers()[0], device_id_type=MESH)

    def after_y(self, p):
        k, _ = self.of_pass(p)
        self.y_copy(k).wait_recv()

        @pl.loop(0, self.depth)
        def _(to):
            self.add(self.block(k, self.core, self.y, to), self.from_y[rows_of(self.slot(k) * self.depth + to)])

    def go_up(self, p):
        for to in range(self.depth - 1, 0, -1):

            @pl.when(self.z < to)
            def _():
                copy = self.up_copy(p, to)

                @pl.when(self.z > 0)
                def _():
                    copy.wait_recv()
                    self.add(self.pass_block(p, to), self.from_low[p, rows_of(to - 1)])

                copy.start()

    def go_down(self, p):
        for to in range(self.depth - 1):

            @pl.when(self.z > to)
            def _():
                copy = self.down_copy(p, to)

                @pl.when(self.z < self.depth - 1)
                def _():
                    copy.wait_recv()
                    self.add(self.pass_block(p, to), self.from_high[p, rows_of(to)])

                copy.start()

    def finish(self, p):
        k, _ = self.of_pass(p)
        own, total = self.pass_block(p, self.z), self.total.at[rows_of(k)]
        total[...] = own[...].astype(jnp.float32)

        @pl.when(self.z > 0)
        def _():
            self.up_copy(p, self.z).wait_recv()
            total[...] += self.from_low[p, rows_of(jnp.maximum(self.z - 1, 0))].astype(jnp.float32)

        @pl.when(self.z < self.depth - 1)
        def _():
            self.down_copy(p, self.z).wait_recv()
            total[...] += self.from_high[p, rows_of(jnp.minimum(self.z, self.depth - 2))].astype(jnp.float32)

        if self.early:

            @pl.when((p < 2 * self.early) & (p % 2 == 0))
            def _():
                own[...] = total[...].astype(jnp.bfloat16)

    def start_last(self, k):
        self.last_copy(k).start()

    def after_last(self, k):
        self.last_copy(k).wait_recv()
        self.total[rows_of(k), :] += self.from_y[self.last_rows(k)].astype(jnp.float32)

    def drain(self, k):
        self.core_copy(k).wait_send()
        if self.early:
            pl.when(self.is_early(k))(lambda: self.last_copy(k).wait_send())
        pl.when(jnp.logical_not(self.is_early(k)) & (k < self.count - 1))(lambda: self.y_copy(k).wait_send())

    def drain_pass(self, p):
        for to in range(self.depth - 1):

            @pl.when(self.z < to + 1)
            def _():
                self.up_copy(p, to + 1).wait_send()

            @pl.when(self.z > to)
            def _():
                self.down_copy(p, to).wait_send()

    def straight_copy(self, p, to):
        return pltpu.make_async_remote_copy(
            self.pass_block(p, to), self.from_low.at[p, rows_of(self.z - (self.z > to).astype(jnp.int32))],
            self.up_s.at[p, to], self.up_r.at[p, self.z],
            device_id=self.device(to, self.y, self.core), device_id_type=MESH,
        )

    def go_straight(self, p):
        for distance in range(self.depth - 1, 0, -1):
            pl.when(self.z + distance < self.depth)(lambda: self.straight_copy(p, self.z + distance).start())
            pl.when(self.z >= distance)(lambda: self.straight_copy(p, self.z - distance).start())

    def finish_straight(self, p):
        k, _ = self.of_pass(p)
        total = self.total.at[rows_of(k)]
        total[...] = self.pass_block(p, self.z)[...].astype(jnp.float32)

        @pl.loop(0, self.depth - 1)
        def _(i):
            source = i + (i >= self.z).astype(jnp.int32)
            arrived = self.from_low.at[p, rows_of(i)]
            pltpu.make_async_remote_copy(
                arrived, arrived, self.up_s.at[p, source], self.up_r.at[p, source],
                device_id=self.device(source, self.y, self.core), device_id_type=MESH,
            ).wait_recv()
            total[...] += arrived[...].astype(jnp.float32)

    def drain_straight(self, p):
        for to in range(self.depth):
            pl.when(self.z != to)(lambda: self.straight_copy(p, to).wait_send())

    def columns(self, cut):
        wide = self.parts.shape[2] // self.cuts
        return pl.ds(pl.multiple_of(cut * wide, wide), wide)

    def y_cut(self, cut):
        quarter, columns = self.depth * ROWS, self.columns(cut)
        start, slot = (self.core * 2 + 1 - self.y) * quarter, (self.count - 1 - self.early) * quarter
        return pltpu.make_async_remote_copy(
            self.parts.at[self.spot(self.count - 1), pl.ds(pl.multiple_of(start, quarter), quarter), columns],
            self.from_y.at[pl.ds(pl.multiple_of(slot, quarter), quarter), columns], self.cut_y_s.at[cut], self.cut_y_r.at[cut],
            device_id=self.peers()[1], device_id_type=MESH,
        )

    def cut_block(self, to, cut):
        rows = rows_of(place(to, self.y, self.core, self.depth))
        return self.parts.at[self.spot(self.count - 1), rows, self.columns(cut)]

    def direct_copy(self, to, cut):
        rows = rows_of(self.z - (self.z > to).astype(jnp.int32))
        return pltpu.make_async_remote_copy(
            self.cut_block(to, cut), self.from_low.at[self.passes - 1, rows, self.columns(cut)],
            self.cut_s.at[cut, to], self.cut_r.at[cut, self.z],
            device_id=self.device(to, self.y, self.core), device_id_type=MESH,
        )

    def go_direct(self):
        @pl.loop(0, self.cuts)
        def _(cut):
            self.y_cut(cut).wait_recv()
            columns, first = self.columns(cut), (self.count - 1 - self.early) * self.depth

            @pl.loop(0, self.depth)
            def _(to):
                self.add(self.cut_block(to, cut), self.from_y[rows_of(first + to), columns])

            for distance in range(self.depth - 1, 0, -1):
                pl.when(self.z + distance < self.depth)(lambda: self.direct_copy(self.z + distance, cut).start())
                pl.when(self.z >= distance)(lambda: self.direct_copy(self.z - distance, cut).start())

    def finish_direct(self):
        @pl.loop(0, self.cuts)
        def _(cut):
            total = self.total.at[rows_of(self.count - 1), self.columns(cut)]
            total[...] = self.cut_block(self.z, cut)[...].astype(jnp.float32)

            @pl.loop(0, self.depth - 1)
            def _(i):
                source = i + (i >= self.z).astype(jnp.int32)
                arrived = self.from_low.at[self.passes - 1, rows_of(i), self.columns(cut)]
                pltpu.make_async_remote_copy(
                    arrived, arrived, self.cut_s.at[cut, source], self.cut_r.at[cut, source],
                    device_id=self.device(source, self.y, self.core), device_id_type=MESH,
                ).wait_recv()
                total[...] += arrived[...].astype(jnp.float32)

    def drain_direct(self):
        @pl.loop(0, self.cuts)
        def _(cut):
            self.y_cut(cut).wait_send()
            for to in range(self.depth):
                pl.when(self.z != to)(lambda: self.direct_copy(to, cut).wait_send())

    def along(self, t, ahead):
        last, soon, chained = self.depth - 1, 2 * self.early, self.chained
        for far, action in ((self.z, self.go_up), (last - self.z, self.go_down)) if self.hops else ():
            pl.when(far > 0)(lambda far=far, action=action: at(t - far, 0, chained, action))

        ends = ((self.z == 0, self.go_up), (self.z == last, self.go_down))
        for end, action in ends:
            if self.early:
                pl.when(end)(lambda action=action: at(t + ahead, 0, soon, action))
        if self.hops:
            at(t, soon, self.passes - 1, self.after_y)
        for end, action in ends:
            if self.hops:
                pl.when(end)(lambda action=action: at(t, soon, chained, action))
        if self.hops:
            at(t, chained, self.passes - 1, self.go_straight)
        pl.when(t == self.passes - 1)(self.go_direct)


def at(k, low, high, action):
    @pl.when((k >= low) & (k < high))
    def _():
        action(k)


def over(count, size):
    def run(action):
        @pl.loop(0, count // size)
        def _(i):
            action(pl.ds(pl.multiple_of(i * size, size), size))

    return run


def train_kernel(
    depth, images,
    patches, signs_in, tiles_in, valid_in, cotangent, attend_in, project_in, expand_in, shrink_in, first_in, second_in,
    bottle_from, results, total_out, rest_out,
    signs, tiles, valid, first, second, bottle_in, rest, total, parts, attend, project, left, right, soft, temp, saved, normed_one, normed_two, residual, factor_one,
    factor_two, average_two, bias, codes, bottle, delta, code_grad, bottle_sum, mix, packed, code_sum,
    code_core, code_y, code_z, code_other, gain_one, gain_two, extra,
    loads, code_sems, stores, sum_sems, *scratch,
):
    rows, width = patches.shape
    length = rows // images
    work = total.at[:rows]
    count, slabs = parts.shape[0], shrink_in.shape[0] // width
    pairs = width // 128
    encoding = lax.axis_index("section") == 0

    def content(k):
        other = jnp.where(k < 2 * slabs, (k + slabs) % (2 * slabs), k)
        return jnp.where(encoding, (k + slabs) % count, other)

    def location(k):
        return (k + jnp.where(encoding, slabs, 2 * slabs)) % count

    held = jnp.where(encoding, slabs + 4, 2 * slabs + 1)
    main = Reduction(depth, EARLY, STRAIGHT, CUTS, held, location, parts, total, scratch[:17])
    small = Reduction(depth, 0, 1, 1, 1, lambda k: k, extra, rest, scratch[17:34])
    lane = lax.broadcasted_iota(jnp.int32, (length, 128), 1)
    low_half = lane < HD
    bf, f32 = jnp.bfloat16, jnp.float32

    def dot(a, b):
        return jnp.dot(a, b, preferred_element_type=f32)

    def load(source, target, i):
        return pltpu.make_async_copy(source, target, loads.at[i])

    little = [
        load(source, target, 7 + 2 * slabs + i)
        for i, (source, target) in enumerate(
            (
                (signs_in, signs), (bottle_from, bottle_in), (tiles_in, tiles), (valid_in, valid), (first_in, first),
                (second_in, second),
            )
        )
    ]
    for copy in little[:2]:
        copy.start()
    fetch = [load(patches, right.at[5], 0)]
    fetch += [load(attend_in.at[:, pl.ds(j * width, width)], attend.at[j], 1 + j) for j in range(3)]
    for copy in fetch + little[2:]:
        copy.start()
    main.greet()
    fetch += [load(project_in, project, 4)]
    fetch += [load(expand_in.at[:, pl.ds(j * width, width)], parts.at[2 * slabs + j], 5 + j) for j in range(slabs)]
    fetch += [load(shrink_in.at[pl.ds(j * width, width)], parts.at[slabs + j], 5 + slabs + j) for j in range(slabs)]
    fetch += [load(cotangent, right.at[0], 5 + 2 * slabs)]

    for copy in little[:2]:
        copy.wait()
    code_width = signs.shape[0]
    work[:256, :] = jnp.zeros((256, width), f32)
    work[:code_width, :rows] = (2 * signs[...] - 1).astype(f32) / math.sqrt(code_width)
    work[128 : 128 + code_width, :] = bottle_in[...].astype(f32)
    codes[...] = work[:128, :rows].T.astype(bf)
    bottle[...] = work[128:256, :].T.astype(bf)
    for copy in little[2:]:
        copy.wait()
    for i in range(images):
        row = jnp.broadcast_to(tiles[i : i + 1, :].astype(f32), (length, length))
        live = jnp.broadcast_to(valid[i : i + 1, :], (length, length)) == 1
        spot = lax.broadcasted_iota(jnp.int32, (length, length), 0) == lax.broadcasted_iota(
            jnp.int32, (length, length), 1
        )
        bias[i] = jnp.where(((row == row.T) & live) | spot, 0.0, -1000000000.0)
    turned = work[128:256, :]
    mix[...] = ((turned - jnp.mean(turned, axis=1, keepdims=True)) * first[...]).T.astype(bf)
    packed[...] = jnp.zeros_like(packed)
    gain_one[...] = jnp.zeros_like(gain_one)
    gain_two[...] = jnp.zeros_like(gain_two)
    fetch[0].wait()

    @pl.when(encoding)
    def _():
        residual[...] = right[5].astype(f32)

    @pl.when(jnp.logical_not(encoding))
    def _():
        residual[...] = times_transpose(codes[...], bottle[...])

    def norm(gain, normed, factor, average=None):
        values = residual[...]
        middle = jnp.mean(values, axis=-1, keepdims=True)
        if average is not None:
            average[...] = middle
        center = values - middle
        scale = lax.rsqrt(jnp.mean(center * center, axis=-1, keepdims=True) + 1e-06)
        unscaled = center * scale
        normed[...] = unscaled
        factor[...] = scale
        temp[...] = (unscaled * gain[...]).astype(bf)

    def keep_transpose(source, target):
        half = 8 * ROWS
        for i in range(width // half):
            turned = source[:, i * half : (i + 1) * half].T
            for j in range(8):
                z, y, core = i * 2 + j // 4, (j // 2) % 2, j % 2
                target[place(z, y, core, depth) * ROWS : (place(z, y, core, depth) + 1) * ROWS, :] = turned[
                    j * ROWS : (j + 1) * ROWS
                ]

    norm(first, normed_one, factor_one)
    for j in range(3):
        fetch[1 + j].wait()
        if j == 2:
            for copy in fetch[4:]:
                copy.start()
        right[6 + j] = dot(temp[...], attend[j]).astype(bf)


    group = 6
    heads = [(pair, head) for pair in range(group) for head in range(2)]

    def group_of(turn):
        image = turn * group // pairs
        start = turn * group - image * pairs
        lanes = [pl.ds(pl.multiple_of((start + pair) * 128, 128), 128) for pair in range(group)]
        return pl.ds(pl.multiple_of(image * length, length), length), lanes, image

    def masked(values, low, scale=1.0):
        return jnp.where(low_half if low else jnp.logical_not(low_half), values * scale, 0.0).astype(bf)

    def merged(members, pair):
        return jnp.where(low_half, members[2 * pair], members[2 * pair + 1])

    @pl.loop(0, images * pairs // group)
    def _(turn):
        r, lanes, image = group_of(turn)
        query, key, value = ([right[6 + j, r, c] for c in lanes] for j in range(3))
        scores = [
            times_transpose(masked(query[pair], head == 0, HD**-0.5), key[pair]) + bias[image] for pair, head in heads
        ]
        raised = [jnp.exp(member - jnp.max(member, axis=-1, keepdims=True)) for member in scores]
        weights = [(member * (1.0 / jnp.sum(member, axis=-1, keepdims=True))).astype(bf) for member in raised]
        for (pair, head), member in zip(heads, weights):
            soft[turn * group + pair, head * length : (head + 1) * length, :] = member
        mixed = [dot(member, value[pair]) for (pair, head), member in zip(heads, weights)]
        for pair, c in enumerate(lanes):
            temp[r, c] = merged(mixed, pair).astype(bf)

    fetch[4].wait()

    residual[...] += dot(temp[...], project[...])

    keep_transpose(temp, left.at[slabs + 1])
    norm(second, normed_two, factor_two, average_two)

    for j in range(slabs):
        fetch[5 + j].wait()

        hidden = dot(temp[...], parts[2 * slabs + j])
        share = 0.5 + 0.5 * lax.erf(hidden * math.sqrt(0.5))
        slope = share + hidden * jnp.exp(-0.5 * hidden * hidden) * (1.0 / math.sqrt(2.0 * math.pi))
        parts[j, :rows, :] = (hidden * share).astype(bf)
        right[1 + j] = slope.astype(bf)

    for copy in fetch[5 + slabs :]:
        copy.wait()
    out_copy = pltpu.make_async_copy(saved, results, loads.at[6 + 2 * slabs])
    across = pltpu.make_async_remote_copy(
        delta, code_grad, code_sems.at[0], code_sems.at[1], device_id=main.peers()[4], device_id_type=MESH
    )
    main.meet()

    @pl.when(jnp.logical_not(encoding))
    def _():
        residual[...] = right[0].astype(f32)

    def keep_norm(gain, normed, target):
        temp[...] = (normed[...] * gain[...]).astype(bf)
        keep_transpose(temp, target)

    def block_output():
        output = normed_two[...] * (1.0 / factor_two[...]) + average_two[...]
        for j in range(slabs):
            output += dot(parts[j, :rows, :], parts[slabs + j])
        saved[...] = output.astype(bf)
        pl.when(jnp.logical_not(encoding))(out_copy.start)
        for i in range(2 * slabs):
            z, y = i // 2, i % 2
            turned = parts[i // 2, :rows, (i % 2) * 8 * ROWS : (i % 2 + 1) * 8 * ROWS].T
            for core in range(2):
                for j in range(slabs):
                    spot, start = place(z, y, core, depth) * ROWS, (core * 4 + j) * ROWS
                    left[j, spot : spot + ROWS, :] = turned[start : start + ROWS]

    def from_codes():
        latent = dot(saved[...], bottle[...])
        scale = lax.rsqrt(jnp.sum(latent * latent, axis=-1, keepdims=True) + 1e-06)
        unit_code = latent * scale
        work[:128, :rows] = jnp.zeros((128, rows), f32)
        across.wait_recv()
        work[: delta.shape[0], :rows] = code_grad[...].astype(f32)
        grad_unit = work[:128, :rows].T
        grad_latent = (
            scale * (grad_unit - unit_code * jnp.sum(unit_code * grad_unit, axis=-1, keepdims=True))
        ).astype(bf)
        grad_out = times_transpose(grad_latent, bottle[...])
        right[0] = grad_out.astype(bf)
        residual[...] = grad_out
        codes[...] = grad_latent

    def piece(k):
        c = content(k)
        a = jnp.minimum(c, slabs) + (c >= 2 * slabs).astype(jnp.int32) + (c > 2 * slabs).astype(jnp.int32)
        b = jnp.maximum(c - slabs + 1, 0)
        parts[location(k)] = dot(left[a], right[b]).astype(bf)
        main.start(k)

    def norm_back(gain, normed, factor, gain_sum, low):
        @over(rows, length)
        def _(r):
            given, unscaled = work[r, :], normed[r, :]
            gain_sum[...] += jnp.sum((given * unscaled).reshape(-1, 8, width), axis=0)
            grad = given * gain[...]
            inner = jnp.mean(grad * unscaled, axis=-1, keepdims=True)
            grad = residual[r, :] + factor[r, :] * (grad - jnp.mean(grad, axis=-1, keepdims=True) - unscaled * inner)
            residual[r, :] = grad
            low[r, :] = grad.astype(bf)

    def through_shrink(low, high):
        @pl.loop(low, high)
        def _(j):
            grad = times_transpose(right[0], parts[slabs + j])
            right[1 + j] = (grad * right[1 + j].astype(f32)).astype(bf)

    def through_expand():
        grad = times_transpose(right[1], parts[2 * slabs])
        for j in range(1, slabs):
            grad += times_transpose(right[1 + j], parts[2 * slabs + j])
        work[...] = grad

    def through_project():
        norm_back(second, normed_two, factor_two, gain_two, right.at[5])

        temp[...] = times_transpose(right[5], project[...]).astype(bf)

    def through_heads(low, high):
        @pl.loop(low, high)
        def _(turn):
            r, lanes, image = group_of(turn)
            query, key, value = ([right[6 + j, r, c] for c in lanes] for j in range(3))
            weights = [soft[turn * group + pair, head * length : (head + 1) * length, :] for pair, head in heads]
            grad_heads = [masked(temp[r, lanes[pair]], head == 0) for pair, head in heads]
            grad_soft = [times_transpose(member, value[pair]) for (pair, head), member in zip(heads, grad_heads)]
            grad_scores = []
            for low, member in zip(weights, grad_soft):
                exact = low.astype(f32)
                inner = jnp.sum(exact * member, axis=-1, keepdims=True)
                grad_scores.append((exact * (member - inner)).astype(bf))
            to_query = [dot(member, key[pair]) for (pair, head), member in zip(heads, grad_scores)]
            to_key = [
                contract_rows(member, masked(query[pair], head == 0, HD**-0.5))
                for (pair, head), member in zip(heads, grad_scores)
            ]
            to_value = [contract_rows(low, member) for low, member in zip(weights, grad_heads)]
            for pair, c in enumerate(lanes):
                right[6, r, c] = (merged(to_query, pair) * HD**-0.5).astype(bf)
                right[7, r, c] = (to_key[2 * pair] + to_key[2 * pair + 1]).astype(bf)
                right[8, r, c] = (to_value[2 * pair] + to_value[2 * pair + 1]).astype(bf)

    half = 3 * width // 2
    own_half = pl.ds(pl.multiple_of(main.core * half, half), half)

    def sum_copy(stage, source, target, send, receive, device):
        return pltpu.make_async_remote_copy(
            source, target, sum_sems.at[2 * stage, send], sum_sems.at[2 * stage + 1, receive],
            device_id=device, device_id_type=MESH,
        )

    def sum_core():
        return sum_copy(0, code_sum, code_core, 0, 0, main.peers()[0])

    def sum_y():
        return sum_copy(0, code_sum.at[:, own_half], code_y, 1, 1, main.peers()[1])

    def sum_back():
        return sum_copy(0, code_sum.at[:, own_half], code_other, 2, 2, main.peers()[0])

    def sum_z(to):
        return sum_copy(
            1, code_sum.at[:, own_half], code_z.at[main.z - (main.z > to).astype(jnp.int32)], to, main.z,
            main.device(to, main.y, main.core),
        )

    def sum_codes():
        scaled = (codes[...].astype(f32) * factor_one[...]).astype(bf)
        for j in range(3):
            code_sum[:, j * width : (j + 1) * width] = contract_rows(scaled, right[6 + j])[: code_sum.shape[0]].astype(bf)
        sum_core().start()

    def sum_after_core():
        sum_core().wait_send()
        sum_core().wait_recv()
        code_sum[...] = (code_sum[...].astype(f32) + code_core[...].astype(f32)).astype(bf)
        sum_y().start()

    def sum_after_y():
        sum_y().wait_send()
        sum_y().wait_recv()
        code_sum[:, own_half] = (code_sum[:, own_half].astype(f32) + code_y[...].astype(f32)).astype(bf)
        for to in range(depth):
            pl.when(main.z != to)(lambda: sum_z(to).start())

    def sum_after_z():
        together = code_sum[:, own_half].astype(f32)
        for z in range(depth):
            pl.when(main.z != z)(lambda: sum_z(z).wait_send())
            source = code_z.at[jnp.minimum(z, depth - 2)]

            @pl.when(main.z != z)
            def _():
                sum_copy(1, source, source, z, z, main.device(z, main.y, main.core)).wait_recv()

        for i in range(depth - 1):
            together += code_z[i].astype(f32)
        code_sum[:, own_half] = together.astype(bf)
        sum_back().start()

    def finish_attend():
        sum_back().wait_send()
        sum_back().wait_recv()
        code_sum[:, pl.ds(pl.multiple_of((1 - main.core) * half, half), half)] = code_other[...]
        own = mix[pl.ds(pl.multiple_of(main.me * ROWS, ROWS), ROWS), :][:, : code_sum.shape[0]]
        for j in range(3):
            k = 2 * slabs + 1 + j
            total[k * ROWS : (k + 1) * ROWS, :] = dot(own, code_sum[:, j * width : (j + 1) * width])
            store(k).start()

    def through_attend():
        grad = times_transpose(right[6], attend[0])
        for j in range(1, 3):
            grad += times_transpose(right[6 + j], attend[j])
        work[...] = grad

        @pl.when(encoding)
        def _():
            bottle_sum[...] = contract_rows(saved[...], codes[...])
            latent = codes[...].astype(f32)
            together = dot(left[0], pltpu.roll(latent, PACK, 1).astype(bf))
            for j in range(1, slabs):
                together += dot(left[j], pltpu.roll(latent, PACK + STRIDE * j, 1).astype(bf))
            packed[...] = together

        norm_back(first, normed_one, factor_one, gain_one, saved)

        @pl.when(jnp.logical_not(encoding))
        def _():
            turned = lax.dot_general(bottle[...], saved[...], (((0,), (1,)), ((), ())), preferred_element_type=f32)
            delta[...] = turned[: delta.shape[0]].astype(bf)
            across.start()

        @pl.when(encoding)
        def _():
            out_copy.start()

    def small_sums():
        @pl.when(jnp.logical_not(encoding))
        def _():
            bottle_sum[...] = contract_rows(saved[...], codes[...])
            sum_codes()

        spare = lax.broadcasted_iota(jnp.int32, (width, 128), 1)
        column_one = jnp.sum(gain_one[...].T, axis=1, keepdims=True)
        column_two = jnp.sum(gain_two[...].T, axis=1, keepdims=True)
        gathered = jnp.where(
            spare == code_width, column_one, jnp.where(spare == code_width + 1, column_two, bottle_sum[...])
        )
        for i in range(4 * depth):
            start = place(i // 4, (i // 2) % 2, i % 2, depth) * ROWS
            extra[0, start : start + ROWS, :] = (
                gathered[i * ROWS : (i + 1) * ROWS] + packed[start : start + ROWS, :]
            ).astype(bf)
        small.start(0)

    def store(k):
        return pltpu.make_async_copy(total.at[rows_of(k)], total_out.at[rows_of(content(k))], stores.at[k])

    def finish(p):
        main.finish(p)
        piece, _ = main.of_pass(p)
        pl.when(p >= 2 * EARLY)(store(piece).start)

    def finish_straight(p):
        main.finish_straight(p)
        store(main.of_pass(p)[0]).start()

    def finish_early(k):
        main.after_last(k)
        store(k).start()

    rest_copy = pltpu.make_async_copy(rest, rest_out, loads.at[13 + 2 * slabs])

    def finish_small():
        small.finish_direct()
        rest_copy.start()

        @pl.when(encoding)
        def _():
            for j in range(slabs):
                exact = pltpu.roll(rest[...], 128 - PACK - STRIDE * j, 1)
                high = exact.astype(bf)
                low = (exact - high.astype(f32)).astype(bf)
                k = slabs + 4 + j
                total[k * ROWS : (k + 1) * ROWS, :] = times_transpose(high, bottle[...]) + times_transpose(low, bottle[...])
                store(k).start()

    def send_late():
        for k in range(1 + EARLY - LATE, 1 + EARLY):
            main.start_last(k)

    def finish_last():
        main.finish_direct()
        store(held - 1).start()

    turns, links = images * pairs // group, 6

    @pl.loop(0, links + MOST + EARLY + 10)
    def _(step):
        k = step - links * main.section
        link = jnp.where(encoding, jnp.where(step >= 3, step - 2, -1), step)
        pl.when((k == 0) & encoding)(lambda: keep_norm(first, normed_one, left.at[slabs + 2]))
        pl.when(k == 0)(lambda: keep_norm(second, normed_two, left.at[slabs]))
        pl.when(k == slabs * main.section)(block_output)
        pl.when((k == 0) & encoding)(from_codes)
        pl.when(jnp.where(encoding, step < slabs, step == 0))(
            lambda: through_shrink(jnp.where(encoding, step, 0), jnp.where(encoding, step + 1, slabs))
        )
        now = jnp.where(k < slabs, k, jnp.where(k == slabs + 1, slabs, jnp.where(k >= slabs + 3, k - 2, -1)))
        at(now, 0, held, piece)
        met = jnp.where(k <= slabs + 2, k - 2, jnp.where(k >= slabs + 4, k - 3, -1))
        at(met, 0, held, main.after_core)
        main.along(k - 5, 2)
        at(k - 10, 0, main.chained, finish)
        at(k - 10, main.chained, main.passes - 1, finish_straight)
        pl.when(k == main.passes + 9)(finish_last)
        at(k - 12, 1, 1 + EARLY - LATE, main.start_last)
        at(k - slabs - SMALL - 6, 0, 1, small.after_core)
        small.along(k - slabs - SMALL - 7 - GAP, 0)
        pl.when(k == main.passes + 4)(send_late)
        pl.when(k == slabs + SMALL + GAP + 8)(finish_small)
        at(k - main.passes - 7, 1, 1 + EARLY, finish_early)
        for moment, action in ((5, sum_after_core), (8, sum_after_y), (10, sum_after_z), (12, finish_attend)):
            pl.when(jnp.logical_not(encoding) & (k == moment))(action)
        pl.when(link == 1)(through_expand)
        pl.when(link == 2)(through_project)
        pl.when((link == 3) | (link == 4))(lambda: through_heads((link - 3) * turns // 2, (link - 2) * turns // 2))
        pl.when(link == 5)(through_attend)
        pl.when(k == jnp.where(encoding, 7, 3))(small_sums)

    out_copy.wait()
    rest_copy.wait()

    @pl.when(jnp.logical_not(encoding))
    def _():
        across.wait_send()

    small.drain(0)
    small.drain_direct()
    main.drain_direct()

    @pl.loop(0, held)
    def _(k):
        main.drain(k)

    @pl.loop(0, count)
    def _(k):
        store(k).wait()

    @pl.loop(0, main.chained)
    def _(p):
        main.drain_pass(p)

    @pl.loop(main.chained, main.passes - 1)
    def _(p):
        main.drain_straight(p)


def train(depth, images, arrays):
    patches, signs, _, _, _, attend, project, expand, shrink, _, _, bottle = arrays
    rows, width = patches.shape
    slabs = shrink.shape[0] // width
    count = 2 * slabs + 4
    pairs, length = width // 128, rows // images
    code_rows = -(-signs.shape[0] // 16) * 16
    hbm = pl.BlockSpec(memory_space=pl.ANY)
    low, full = lambda *shape: pltpu.VMEM(shape, jnp.bfloat16), lambda *shape: pltpu.VMEM(shape, jnp.float32)
    return pl.pallas_call(
        functools.partial(train_kernel, depth, images),
        out_shape=(
            jax.ShapeDtypeStruct((rows, width), jnp.bfloat16),
            jax.ShapeDtypeStruct((count * ROWS, width), jnp.float32),
            jax.ShapeDtypeStruct((ROWS, 128), jnp.float32),
        ),
        in_specs=[hbm] * 12,
        out_specs=[hbm] * 3,
        scratch_shapes=[pltpu.VMEM(arrays[i].shape, arrays[i].dtype) for i in (1, 2, 3, 9, 10, 11)]
        + [
            full(ROWS, 128),
            full(count * ROWS, width),
            low(count, width, width),
            low(3, width, width),
            low(width, width),
            low(slabs + 3, width, rows),
            low(slabs + 5, rows, width),
            low(images * pairs, 2 * length, length),
            low(rows, width),
            low(rows, width),
            full(rows, width),
            full(rows, width),
            full(rows, width),
            full(rows, 1),
            full(rows, 1),
            full(rows, 1),
            full(images, length, length),
            low(rows, 128),
            low(width, 128),
            low(code_rows, rows),
            low(code_rows, rows),
            full(width, 128),
            low(width, 128),
            full(width, 128),
            low(code_rows, 3 * width),
            low(code_rows, 3 * width),
            low(code_rows, 3 * width // 2),
            low(depth - 1, code_rows, 3 * width // 2),
            low(code_rows, 3 * width // 2),
            full(8, width),
            full(8, width),
            low(1, width, 128),
            pltpu.SemaphoreType.DMA((14 + 2 * slabs,)),
            pltpu.SemaphoreType.DMA((2,)),
            pltpu.SemaphoreType.DMA((count,)),
            pltpu.SemaphoreType.DMA((6, depth)),
        ]
        + Reduction.scratch(depth, EARLY, CUTS, MOST, width)
        + Reduction.scratch(depth, 0, 1, 1, 128),
        compiler_params=pltpu.CompilerParams(collective_id=0, has_side_effects=True, vmem_limit_bytes=63 << 20),
        name="train",
    )(*arrays)


def deliver_kernel(slabs, code, raw, total, rest, results, attend, project, expand, shrink, first, second, bottle):
    width = total.shape[1]
    results[...] = raw[...]
    for j in range(slabs):
        shrink[j * ROWS : (j + 1) * ROWS, :] = total[j * ROWS : (j + 1) * ROWS, :]
        expand[:, j * width : (j + 1) * width] = total[(slabs + j) * ROWS : (slabs + j + 1) * ROWS, :]
    project[...] = total[2 * slabs * ROWS : (2 * slabs + 1) * ROWS, :]
    for j in range(3):
        start = (2 * slabs + 1 + j) * ROWS
        attend[:, j * width : (j + 1) * width] = total[start : start + ROWS, :]
    turned = rest[...].T
    first[...] = turned[code : code + 1]
    second[...] = turned[code + 1 : code + 2]
    for i in range(code):
        bottle[i] = turned[i : i + 1]


def deliver(raw, total, rest, slabs, code):
    width = total.shape[1]
    vmem = pl.BlockSpec(memory_space=pltpu.VMEM)
    full = lambda *shape: jax.ShapeDtypeStruct(shape, jnp.float32)
    return pl.pallas_call(
        functools.partial(deliver_kernel, slabs, code),
        out_shape=(
            jax.ShapeDtypeStruct(raw.shape, raw.dtype),
            full(ROWS, 3 * width),
            full(ROWS, width),
            full(ROWS, slabs * width),
            full(slabs * ROWS, width),
            full(1, ROWS),
            full(1, ROWS),
            full(code, 1, ROWS),
        ),
        in_specs=[vmem] * 3,
        out_specs=[vmem] * 8,
        name="deliver",
    )(raw, total, rest)


def two_images(*arrays):
    images = arrays[2].shape[0]
    code = arrays[1].shape[1]
    slabs = arrays[8].shape[1] // arrays[0].shape[1]
    weights = tuple(member[0] for member in arrays[5:9])
    arrays = (arrays[0], arrays[1].T) + arrays[2:5] + weights + arrays[9:11] + (arrays[11][0].T,)
    raw, total, rest = train(lax.axis_size("batch") // 4, images, arrays)
    results, attend, project, expand, shrink, first, second, bottle = deliver(raw, total, rest, slabs, code)
    return (
        results[None], attend[None], project[None], expand[None], shrink[None], first, second, bottle.transpose(1, 2, 0)
    )


def pick_index(stacked, chosen):
    return lax.dynamic_index_in_dim(stacked, chosen, 0, keepdims=False)


def body(
    patches,
    code_signs,
    tile_ids,
    patch_valid,
    cotangent,
    attend_weight,
    project_weight,
    expand_weight,
    shrink_weight,
    norm_first,
    norm_second,
    bottleneck,
):
    micro_count = tile_ids.shape[0]
    length = tile_ids.shape[1]
    code_width = code_signs.shape[1]
    encoding = lax.axis_index("section") == 0
    encoding_int = encoding.astype(jnp.int32)
    weights = (
        attend_weight[0],
        project_weight[0],
        expand_weight[0],
        shrink_weight[0],
        norm_first[0],
        norm_second[0],
    )
    bottle = bottleneck[0]
    code_values = ((2 * code_signs - 1).astype(jnp.float32) / math.sqrt(code_width)).astype(
        jnp.bfloat16
    )
    block_inputs = []
    outputs_low = []
    unit_codes = []
    unit_factors = []
    decoded_list = []
    kept_list = []
    for turn_index in range(micro_count):
        image_rows = patches[turn_index * length : (turn_index + 1) * length].astype(jnp.float32)
        decoder_in = times_transpose(
            code_values[turn_index * length : (turn_index + 1) * length], bottle
        )
        block_in = jnp.where(encoding, image_rows, decoder_in)
        allowed_keys = allowed(tile_ids[turn_index], patch_valid[turn_index])
        output, kept_parts = block_forward(block_in, weights, allowed_keys)
        output_low = output.astype(jnp.bfloat16)
        latent = jnp.dot(output_low, bottle, preferred_element_type=jnp.float32)
        factor = lax.rsqrt(jnp.sum(latent * latent, axis=-1, keepdims=True) + 1e-06)
        block_inputs.append(block_in)
        outputs_low.append(output_low)
        unit_codes.append(latent * factor)
        unit_factors.append(factor)
        decoded_list.append(output_low)
        kept_list.append(kept_parts)
    block_inputs = jnp.stack(block_inputs)
    outputs_low = jnp.stack(outputs_low)
    unit_codes = jnp.stack(unit_codes)
    unit_factors = jnp.stack(unit_factors)
    kept_stack = jax.tree.map(lambda *members: jnp.stack(members), *kept_list)
    totals = None
    sent_grad = jnp.zeros((length, code_width), jnp.bfloat16)
    input_grads = []
    for turn_index in range(micro_count + 1):
        if turn_index > 0:
            received = passed_along(sent_grad, "section", -1)
        else:
            received = jnp.zeros_like(sent_grad)
        chosen = jnp.clip(turn_index - encoding_int, 0, micro_count - 1)
        turn_flag = jnp.where(encoding, turn_index >= 1, turn_index < micro_count).astype(
            jnp.float32
        )
        kept_parts = jax.tree.map(lambda stacked: pick_index(stacked, chosen), kept_stack)
        unit_code = pick_index(unit_codes, chosen)
        factor = pick_index(unit_factors, chosen)
        output_low = pick_index(outputs_low, chosen)
        grad_unit = received.astype(jnp.float32)
        grad_latent = (
            factor
            * (grad_unit - unit_code * jnp.sum(unit_code * grad_unit, axis=-1, keepdims=True))
        ).astype(jnp.bfloat16)
        grad_encoded = times_transpose(grad_latent, bottle)
        bottle_encoder = contract_rows(output_low, grad_latent)
        given_grad = lax.dynamic_slice_in_dim(cotangent, chosen * length, length, 0).astype(
            jnp.float32
        )
        grad_out = jnp.where(encoding, grad_encoded, given_grad)
        grad_in, grads = block_backward(kept_parts, grad_out, weights)
        grad_in_low = grad_in.astype(jnp.bfloat16)
        code_rows = lax.dynamic_slice_in_dim(code_values, chosen * length, length, 0)
        bottle_decoder = contract_rows(grad_in_low, code_rows)
        sent_grad = jnp.dot(grad_in_low, bottle, preferred_element_type=jnp.float32).astype(
            jnp.bfloat16
        )
        grads = grads + (jnp.where(encoding, bottle_encoder, bottle_decoder),)
        grads = tuple((turn_flag * member for member in grads))
        if turn_index > 0:
            input_grads.append(grad_in_low)
        totals = (
            grads
            if totals is None
            else tuple((former + latter for former, latter in zip(totals, grads)))
        )
    totals = lax.psum_scatter(totals, "batch", scatter_dimension=0, tiled=True)
    pieces = [
        jnp.where(encoding, input_grads[turn_index], decoded_list[turn_index])
        for turn_index in range(micro_count)
    ]
    results = jnp.concatenate(pieces, axis=0)[None]
    return (
        results,
        totals[0][None],
        totals[1][None],
        totals[2][None],
        totals[3][None],
        totals[4][None],
        totals[5][None],
        totals[6][None],
    )


def solution(mesh):
    batch = mesh.shape["batch"]
    return jax.shard_map(
        two_images if batch == 16 else body,
        mesh=mesh,
        in_specs=(
            P("batch", None),
            P("batch", None),
            P("batch", None),
            P("batch", None),
            P("batch", None),
            P("section", None, None),
            P("section", None, None),
            P("section", None, None),
            P("section", None, None),
            P("section", None),
            P("section", None),
            P("section", None, None),
        ),
        out_specs=(
            P("section", "batch", None),
            P("section", "batch", None),
            P("section", "batch", None),
            P("section", "batch", None),
            P("section", "batch", None),
            P("section", "batch"),
            P("section", "batch"),
            P("section", "batch", None),
        ),
        check_vma=False,
    )
```
